32 devices in a mesh: group: 4 (over z), member: 8 (over y, x, core).
Axes of the slice: x: 2, y: 2, z: 4, core: 2. Of those that a mesh axis runs over, the one named last changes fastest.
Arguments:
- audio_vectors: bfloat16 [4096, 768], P(('group', 'member')), may hold values from -8 to 8
- sentence_vectors: bfloat16 [2048, 768], P(('group', 'member')), may hold values from -8 to 8
- matching_indices: int32 [4096], P(('group', 'member')), may hold values from 0 to 2047, as said below
- sharpness_array: float32 [1], replicated, may hold values from 8 to 16
- offset_term: float32 [1], replicated, may hold values from -4 to -2
Outputs:
- speech_grad: float32 [4096, 768], P(('group', 'member'))
- text_grad: float32 [2048, 768], P(('group', 'member'))
The draws below stay inside these ranges and needn't reach their ends.
Inputs may be any that keep to these rules, and one draw needn't show every extreme that they name: `matching_indices`: each caption matches exactly two speech clips.
All inputs are finite; a program needn't handle non-finite values.
Results may differ from the reference program's by a relative error of at most 0.00072.
Values may be sent and summed in bfloat16 or wider, within the bound.
No kernel may reach another device: no remote copies, remote signals or barrier semaphores. Data moves between devices by JAX's collectives and lax.ppermute only.
A program may use at most 128 MiB of HBM per device.

```python
import math
import jax
import jax.numpy as jnp
from jax import lax

E = 768
BATCH = 4096
CAPTION_TOTAL = 2048


cluster_count = 16


def shared_parts(key):
    centers = jnp.clip(jax.random.normal(jax.random.fold_in(key, 101), (cluster_count, E), jnp.float32), -4.0, 4.0)
    return centers


def tower_rows(key, salt, count):
    centers = shared_parts(key)
    own_key = jax.random.fold_in(key, salt)
    labels = jax.random.randint(jax.random.fold_in(own_key, 1), (count,), 0, cluster_count).astype(jnp.int32)
    picked = centers[labels]
    weight = jnp.exp(jax.random.uniform(jax.random.fold_in(own_key, 2), (count,), jnp.float32, math.log(0.5), math.log(1.8)))
    noise = jnp.clip(jax.random.normal(jax.random.fold_in(own_key, 3), (count, E), jnp.float32), -4.0, 4.0)
    scales = jnp.exp(jax.random.uniform(jax.random.fold_in(own_key, 4), (count,), jnp.float32, 0.0, math.log(10.0)))
    values = weight[:, None] * picked + noise
    return (0.04 * scales[:, None] * values).astype(jnp.bfloat16)


def draw_audio_vectors(key, part):
    return tower_rows(key, 11, BATCH)


def draw_sentence_vectors(key, part):
    return tower_rows(key, 22, CAPTION_TOTAL)


def draw_matching_indices(key, part):
    order = jax.random.permutation(key, BATCH).astype(jnp.int32)
    return (order // 2).astype(jnp.int32)


def setup_inputs(seed: int = 0) -> dict:
    key_of = jax.random.split(jax.random.key(seed), 6)
    return {
        "audio_vectors": draw_audio_vectors(jax.random.fold_in(key_of[5], 71), 0),
        "sentence_vectors": draw_sentence_vectors(jax.random.fold_in(key_of[5], 71), 0),
        "matching_indices": draw_matching_indices(jax.random.fold_in(key_of[5], 71), 0),
        "sharpness_array": jnp.clip(jnp.exp(jax.random.uniform(key_of[3], (1,), jnp.float32, math.log(8.0), math.log(16.0))), 8.0, 16.0),
        "offset_term": jnp.clip(jax.random.uniform(key_of[4], (1,), jnp.float32, -4.0, -2.0), -4.0, -2.0),
    }


def unit_rows(values):
    floats = values.astype(jnp.float32)
    norms = jnp.sqrt(lax.optimization_barrier(jnp.sum(floats * floats, axis=-1, keepdims=True)) + 1e-06)
    return (floats / norms, norms)

def project_gradient(back, direction, norms):
    along = lax.optimization_barrier(jnp.sum(direction * back, axis=-1, keepdims=True))
    return (back - direction * along) / norms

def reference(audio_vectors, sentence_vectors, matching_indices, sharpness_array, offset_term):
    audio_heading, speech_norm = unit_rows(audio_vectors)
    text_dir, text_norm = unit_rows(sentence_vectors)
    speech_unit = audio_heading.astype(jnp.bfloat16)
    text_normalized = text_dir.astype(jnp.bfloat16)
    sharpness_factor = sharpness_array[0]
    shift = offset_term[0]
    block = math.gcd(BATCH, 1024)
    count = BATCH // block
    columns = jnp.arange(CAPTION_TOTAL, dtype=jnp.int32)

    def one_block(text_back, index):
        start = (index * block).astype(jnp.int32)
        rows = lax.dynamic_slice_in_dim(speech_unit, start, block, 0)
        marks = lax.dynamic_slice_in_dim(matching_indices, start, block, 0)
        logits = sharpness_factor * jnp.dot(rows, text_normalized.T, preferred_element_type=jnp.float32) + shift
        match = (marks[:, None] == columns[None, :]).astype(jnp.float32)
        coef = (sharpness_factor * (jax.nn.sigmoid(logits) - match)).astype(jnp.bfloat16)
        speech_part = jnp.dot(coef, text_normalized, preferred_element_type=jnp.float32)
        text_back = text_back + jnp.dot(coef.T, rows, preferred_element_type=jnp.float32)
        return (text_back, speech_part)
    start_back = jnp.zeros((CAPTION_TOTAL, E), jnp.float32)
    text_back, speech_pieces = lax.scan(one_block, start_back, jnp.arange(count, dtype=jnp.int32))
    speech_gradient_back = speech_pieces.reshape(BATCH, E)
    speech_grad = project_gradient(speech_gradient_back, audio_heading, speech_norm)
    text_grad = project_gradient(text_back, text_dir, text_norm)
    return (speech_grad, text_grad)
```

```python
import functools
import jax
import jax.numpy as jnp
from jax import lax
from jax.experimental import pallas as pl
from jax.experimental.pallas import tpu as pltpu
from jax.sharding import PartitionSpec as P

VMEM_LIMIT = 56 * 1024 * 1024
CHUNK = 512


def exchanged(value, axis, mask):
    size = lax.axis_size(axis)
    return lax.ppermute(value, axis, [(i, i ^ mask) for i in range(size)])


def call(body, out_shape, operands, flops=0, names="kernel"):
    moved = sum(v.size * v.dtype.itemsize for v in operands)
    specs = []
    for v in operands:
        smem = v.shape == (1,)
        specs.append(pl.BlockSpec(memory_space=pltpu.SMEM if smem else pltpu.VMEM))
    return pl.pallas_call(
        body,
        out_shape=out_shape,
        in_specs=specs,
        out_specs=jax.tree.map(lambda _: pl.BlockSpec(memory_space=pltpu.VMEM), out_shape),
        compiler_params=pltpu.CompilerParams(vmem_limit_bytes=VMEM_LIMIT),
        cost_estimate=pl.CostEstimate(flops=flops, bytes_accessed=moved, transcendentals=0),
        name=names,
    )(*operands)


def direction(values):
    floats = values.astype(jnp.float32)
    norms = jnp.sqrt(jnp.sum(floats * floats, axis=-1, keepdims=True) + 1e-06)
    return floats / norms, norms


def unit_body(*refs):
    out = refs[-1]
    rows = refs[0].shape[0]
    for k, ref in enumerate(refs[:-1]):
        out[k * rows : (k + 1) * rows, :] = direction(ref[...])[0].astype(jnp.bfloat16)


def unit_rows(blocks):
    rows, width = blocks[0].shape
    shape = jax.ShapeDtypeStruct((len(blocks) * rows, width), jnp.bfloat16)
    return call(unit_body, shape, blocks, names="unit_rows")


def text_coef(text, speech, labels, sharp, shift, own_text):
    groups = lax.axis_size("group")
    members = lax.axis_size("member")
    group = lax.axis_index("group")
    member = lax.axis_index("member")
    logits = sharp * lax.dot_general(
        text, speech, (((1,), (1,)), ((), ())), preferred_element_type=jnp.float32
    ) + shift
    probs = 1.0 / (1.0 + jnp.exp(-logits))
    pieces = []
    for k in range(groups):
        base = ((group ^ k) * members + member) * own_text
        ids = base + lax.broadcasted_iota(jnp.int32, (own_text, labels.shape[1]), 0)
        match = jnp.where(ids == labels, 1.0, 0.0)
        pieces.append(probs[k * own_text : (k + 1) * own_text, :] - match)
    return (sharp * jnp.concatenate(pieces, axis=0)).astype(jnp.bfloat16)


def text_part_body(count, own_text, has_start, *refs):
    sharp, shift = refs[0][0], refs[1][0]
    text, speech = refs[2], refs[3]
    labels = refs[4 : 4 + count]
    at = 4 + count
    start = None
    if has_start:
        start = refs[at]
        at += 1
    outs = refs[at:]
    rows = speech.shape[0] // count
    group = max(1, min(count, CHUNK // rows))
    total = start[...] if has_start else None
    for first in range(0, count, group):
        some = labels[first : first + group]
        mark = jnp.concatenate([ref[...] for ref in some], axis=1)
        block = speech[first * rows : (first + len(some)) * rows, :]
        coef = text_coef(text[...], block, mark, sharp, shift, own_text)
        part = jnp.dot(coef, block, preferred_element_type=jnp.float32)
        total = part if total is None else total + part
    if len(outs) == 1:
        outs[0][...] = total
    else:
        for k, out in enumerate(outs):
            out[...] = total[k * own_text : (k + 1) * own_text, :]


def speech_part_body(own_text, *refs):
    sharp, shift = refs[0][0], refs[1][0]
    label, speech = refs[2], refs[3]
    texts, out = refs[4:-1], refs[-1]
    groups = lax.axis_size("group")
    members = lax.axis_size("member")
    group = lax.axis_index("group")
    member = lax.axis_index("member")
    rows = label.shape[1]
    spread = jnp.broadcast_to(label[...], (rows, rows)).T[:, 0:1]
    block = speech[0:rows, :]
    total = None
    for j, text in enumerate(texts):
        other = member ^ (2 * j)
        logits = sharp * lax.dot_general(
            block, text[...], (((1,), (1,)), ((), ())), preferred_element_type=jnp.float32
        ) + shift
        probs = 1.0 / (1.0 + jnp.exp(-logits))
        lane = lax.broadcasted_iota(jnp.int32, (1, groups * own_text), 1)
        ids = ((group ^ (lane // own_text)) * members + other) * own_text + lane % own_text
        match = jnp.where(spread == ids, 1.0, 0.0)
        coef = (sharp * (probs - match)).astype(jnp.bfloat16)
        part = jnp.dot(coef, text[...], preferred_element_type=jnp.float32)
        total = part if total is None else total + part
    out[...] = total


def finish_body(*refs):
    values, parts, out = refs[0], refs[1:-1], refs[-1]
    heading, norms = direction(values[...])
    back = parts[0][...]
    for part in parts[1:]:
        back = back + part[...]
    along = jnp.sum(heading * back, axis=-1, keepdims=True)
    out[...] = (back - heading * along) / norms


def finish(values, parts):
    shape = jax.ShapeDtypeStruct(values.shape, jnp.float32)
    return call(finish_body, shape, [values, *parts], names="finish")


def shards(audio_vectors, sentence_vectors, matching_indices, sharpness_array, offset_term):
    members = lax.axis_size("member")
    groups = lax.axis_size("group")
    chips = members // 2
    own_speech, width = audio_vectors.shape
    own_text = sentence_vectors.shape[0]
    scalars = [sharpness_array, offset_term]
    label = matching_indices.reshape(1, own_speech)

    text_column = [sentence_vectors]
    for k in range(1, groups):
        text_column.append(exchanged(sentence_vectors, "group", k))
    speech_blocks = [audio_vectors]
    for k in range(1, chips):
        speech_blocks.append(exchanged(audio_vectors, "member", 2 * k))
    labels = [label]
    for k in range(1, members):
        labels.append(exchanged(label, "member", k))

    text = unit_rows(text_column)
    texts = [text]
    for k in range(1, chips):
        texts.append(exchanged(text, "member", 2 * k))
    speech = unit_rows(speech_blocks)
    other = exchanged(speech, "member", 1)

    work = 4 * text.shape[0] * speech.shape[0] * width
    column_shape = jax.ShapeDtypeStruct((groups * own_text, width), jnp.float32)
    half = call(
        functools.partial(text_part_body, chips, own_text, False),
        column_shape,
        scalars + [text, speech] + labels[0::2],
        work,
        "text_part",
    )
    parts = call(
        functools.partial(text_part_body, chips, own_text, True),
        [jax.ShapeDtypeStruct((own_text, width), jnp.float32)] * groups,
        scalars + [text, other] + labels[1::2] + [half],
        work,
        "text_part_sum",
    )
    text_back = [parts[0]]
    for k in range(1, groups):
        text_back.append(exchanged(parts[k], "group", k))

    work = 4 * own_speech * chips * text.shape[0] * width
    row_shape = jax.ShapeDtypeStruct((own_speech, width), jnp.float32)
    speech_part = functools.partial(speech_part_body, own_text)
    away = call(speech_part, row_shape, scalars + [labels[1], other] + texts, work, "speech_part")
    back = exchanged(away, "member", 1)
    home = call(speech_part, row_shape, scalars + [labels[0], speech] + texts, work, "speech_part")

    text_grad = finish(sentence_vectors, text_back)
    speech_grad = finish(audio_vectors, [home, back])
    return (speech_grad, text_grad)


def solution(mesh):
    in_specs = (
        P(("group", "member"), None),
        P(("group", "member"), None),
        P(("group", "member")),
        P(),
        P(),
    )
    out_specs = (P(("group", "member"), None), P(("group", "member"), None))
    return jax.shard_map(shards, mesh=mesh, in_specs=in_specs, out_specs=out_specs, check_vma=False)
```

```python
import functools
import jax
import jax.numpy as jnp
from jax import lax
from jax.experimental import pallas as pl
from jax.experimental.pallas import tpu as pltpu
from jax.sharding import PartitionSpec as P

MARK_ROWS = 16
RADIX = 256
CHUNK = 512


def exchanged(value, axis, mask):
    size = lax.axis_size(axis)
    return lax.ppermute(value, axis, [(i, i ^ mask) for i in range(size)])


def total_bytes(values):
    return sum(v.size * v.dtype.itemsize for v in jax.tree.leaves(values))


def call(body, out_shape, operands, after=(), flops=0, temporary=0, name="kernel"):
    specs = []
    for v in operands:
        scalar = v.shape == (1,)
        specs.append(pl.BlockSpec(memory_space=pltpu.SMEM if scalar else pltpu.VMEM))
    specs += [pl.BlockSpec(memory_space=pl.ANY) for _ in after]
    used = len(operands)

    def whole(*refs):
        body(*refs[:used], *refs[used + len(after) :])

    moved = total_bytes(operands) + total_bytes(out_shape)
    return pl.pallas_call(
        whole,
        out_shape=out_shape,
        in_specs=specs,
        out_specs=jax.tree.map(lambda _: pl.BlockSpec(memory_space=pltpu.VMEM), out_shape),
        compiler_params=pltpu.CompilerParams(vmem_limit_bytes=(4 << 20) + 2 * moved + temporary),
        cost_estimate=pl.CostEstimate(flops=flops, bytes_accessed=moved, transcendentals=0),
        name=name,
    )(*operands, *after)


def direction(values):
    floats = values.astype(jnp.float32)
    norms = jnp.sqrt(jnp.sum(floats * floats, axis=-1, keepdims=True) + 1e-06)
    return floats / norms, norms


def prepare_body(audio, sentence, label, speech, text):
    rows = audio.shape[0]
    speech[0:rows, :] = direction(audio[...])[0].astype(jnp.bfloat16)
    text[...] = direction(sentence[...])[0].astype(jnp.bfloat16)
    number = label[...]
    digits = jnp.concatenate([number % RADIX, number // RADIX], axis=1).astype(jnp.float32)
    wide = jnp.concatenate(
        [digits, jnp.zeros((1, speech.shape[1] - 2 * rows), jnp.float32)], axis=1
    )
    speech[rows : rows + MARK_ROWS, :] = jnp.broadcast_to(
        wide, (MARK_ROWS, speech.shape[1])
    ).astype(jnp.bfloat16)


def join_body(counts, *refs):
    outs = refs[sum(counts) :]
    at = 0
    for count, out in zip(counts, outs):
        rows = refs[at].shape[0]
        for k in range(count):
            out[k * rows : (k + 1) * rows, :] = refs[at + k][...]
        at += count


def marks_of(block, rows):
    digits = block[rows : rows + MARK_ROWS, 0 : 2 * rows][0:1, :].astype(jnp.float32)
    return digits[:, 0:rows] + RADIX * digits[:, rows : 2 * rows]


def coefficients(dots, match, sharp, shift):
    logits = sharp * dots + shift
    probs = 1.0 / (1.0 + jnp.exp(-logits))
    return (sharp * (probs - jnp.where(match, 1.0, 0.0))).astype(jnp.bfloat16)


def dot_rows(left, right):
    return lax.dot_general(left, right, (((1,), (1,)), ((), ())), preferred_element_type=jnp.float32)


def text_part_body(rows, own_text, *refs):
    sharp, shift = refs[0][0], refs[1][0]
    text = jnp.concatenate([refs[2][...], refs[3][...]], axis=0)
    speech = refs[4]
    start = refs[5] if len(refs) > 6 and refs[5].shape == text.shape else None
    outs = refs[5:] if start is None else refs[6:]
    groups = lax.axis_size("group")
    members = lax.axis_size("member")
    group = lax.axis_index("group")
    member = lax.axis_index("member")
    stride = rows + MARK_ROWS
    count = speech.shape[0] // stride
    step = max(1, min(count, CHUNK // rows))
    iota = lax.broadcasted_iota(jnp.int32, (own_text, step * rows), 0)
    ids = [((group ^ k) * members + member) * own_text + iota for k in range(groups)]
    ids = jnp.concatenate(ids, axis=0).astype(jnp.float32)
    total = None if start is None else start[...]
    for first in range(0, count, step):
        blocks = range(first, first + step)
        chunk = jnp.concatenate([speech[k * stride : k * stride + rows, :] for k in blocks], axis=0)
        marks = [marks_of(speech.at[k * stride : (k + 1) * stride, :], rows) for k in blocks]
        match = ids == jnp.concatenate(marks, axis=1)
        coef = coefficients(dot_rows(text, chunk), match, sharp, shift)
        part = jnp.dot(coef, chunk, preferred_element_type=jnp.float32)
        total = part if total is None else total + part
    size = outs[0].shape[0]
    for k, out in enumerate(outs):
        out[...] = total[k * size : (k + 1) * size, :]


def speech_part_body(rows, own_text, places, *refs):
    sharp, shift = refs[0][0], refs[1][0]
    speech, texts, out = refs[2], refs[3:-1], refs[-1]
    groups = lax.axis_size("group")
    members = lax.axis_size("member")
    group = lax.axis_index("group")
    member = lax.axis_index("member")
    marks = jnp.broadcast_to(marks_of(speech, rows), (rows, rows)).T[:, 0:1]
    block = speech[0:rows, :]
    many = groups
    lane = lax.broadcasted_iota(jnp.int32, (1, many * own_text), 1)
    total = None
    at = 0
    for ref in texts:
        for first in range(0, ref.shape[0], many * own_text):
            text = ref[first : first + many * own_text, :]
            ids = lane
            for i, (k, j) in enumerate(places[at : at + many]):
                base = ((group ^ k) * members + (member ^ (2 * j))) * own_text
                ids = jnp.where(lane // own_text == i, lane + (base - i * own_text), ids)
            at += many
            match = marks == ids.astype(jnp.float32)
            coef = coefficients(dot_rows(block, text), match, sharp, shift)
            part = jnp.dot(coef, text, preferred_element_type=jnp.float32)
            total = part if total is None else total + part
    out[...] = total


def finish_body(*refs):
    values, parts, out = refs[0], refs[1:-1], refs[-1]
    heading, norms = direction(values[...])
    back = parts[0][...]
    for part in parts[1:]:
        back = back + part[...]
    along = jnp.sum(heading * back, axis=-1, keepdims=True)
    out[...] = (back - heading * along) / norms


def shards(audio_vectors, sentence_vectors, matching_indices, sharpness_array, offset_term):
    members = lax.axis_size("member")
    groups = lax.axis_size("group")
    chips = members // 2
    rows, width = audio_vectors.shape
    own_text = sentence_vectors.shape[0]
    scalars = [sharpness_array, offset_term]
    label = matching_indices.reshape(1, rows)

    def bf16(*shape):
        return jax.ShapeDtypeStruct(shape, jnp.bfloat16)

    def f32(*shape):
        return jax.ShapeDtypeStruct(shape, jnp.float32)

    speech_own, text_own = call(
        prepare_body,
        [bf16(rows + MARK_ROWS, width), bf16(own_text, width)],
        [audio_vectors, sentence_vectors, label],
        name="unit_rows",
    )
    speech_blocks = [speech_own]
    for k in range(1, chips):
        speech_blocks.append(exchanged(speech_own, "member", 2 * k))
    text_blocks = [text_own]
    for k in range(1, groups):
        text_blocks.append(exchanged(text_own, "group", k))
    half_rows = groups * own_text // 2
    speech, upper, lower = call(
        functools.partial(join_body, (chips, groups // 2, groups // 2)),
        [bf16(chips * (rows + MARK_ROWS), width), bf16(half_rows, width), bf16(half_rows, width)],
        speech_blocks + text_blocks,
        name="join_rows",
    )
    other = exchanged(speech, "member", 1)

    column = groups * own_text
    text_part = functools.partial(text_part_body, rows, own_text)
    work = 4 * column * chips * rows * width
    temporary = 4 * column * (6 * CHUNK + 3 * width)
    half = call(
        text_part,
        [f32(column, width)],
        scalars + [upper, lower, speech],
        (),
        work,
        temporary,
        "text_part",
    )
    parts = call(
        text_part,
        [f32(own_text, width)] * groups,
        scalars + [upper, lower, other, half[0]],
        (),
        work,
        temporary,
        "text_part_sum",
    )
    text_back = [parts[0]]
    for k in range(1, groups):
        text_back.append(exchanged(parts[k], "group", k))

    bits = [1 << i for i in range(chips.bit_length() - 1)]
    orders = [bits, bits[1:] + bits[:1]]
    held = [upper, lower]
    places = [
        [(k, 0) for k in range(groups // 2)],
        [(k, 0) for k in range(groups // 2, groups)],
    ]
    came = []
    for step in range(len(bits)):
        masks = [order[step] for order in orders]
        came = [exchanged(v, "member", 2 * mask) for v, mask in zip(held, masks)]
        theirs = [[(k, j ^ mask) for k, j in own] for own, mask in zip(places, masks)]
        if step + 1 < len(bits):
            held = call(
                functools.partial(join_body, (2, 2)),
                [bf16(2 * v.shape[0], width) for v in held],
                [held[0], came[0], held[1], came[1]],
                (parts[0],) if step + 2 == len(bits) else (),
                name="join_texts",
            )
            places = [own + other for own, other in zip(places, theirs)]
    texts = [*held, *came]
    places = places[0] + places[1] + theirs[0] + theirs[1]

    speech_part = functools.partial(speech_part_body, rows, own_text, places)
    work = 4 * rows * chips * column * width
    stride = rows + MARK_ROWS
    away = call(
        speech_part,
        f32(rows, width),
        scalars + [other[0:stride]] + texts,
        (parts[0],),
        work,
        temporary,
        "speech_part",
    )
    back = exchanged(away, "member", 1)
    home = call(
        speech_part,
        f32(rows, width),
        scalars + [speech_own] + texts,
        (away,),
        work,
        temporary,
        "speech_part",
    )
    text_grad = call(
        finish_body, f32(own_text, width), [sentence_vectors, *text_back], (), 1 << 33, name="finish_text"
    )
    speech_grad = call(
        finish_body, f32(rows, width), [audio_vectors, home, back], name="finish_speech"
    )
    return (speech_grad, text_grad)


def solution(mesh):
    in_specs = (
        P(("group", "member"), None),
        P(("group", "member"), None),
        P(("group", "member")),
        P(),
        P(),
    )
    out_specs = (P(("group", "member"), None), P(("group", "member"), None))
    return jax.shard_map(shards, mesh=mesh, in_specs=in_specs, out_specs=out_specs, check_vma=False)
```

```python
import functools
import jax
import jax.numpy as jnp
from jax import lax
from jax.experimental import pallas as pl
from jax.experimental.pallas import tpu as pltpu
from jax.sharding import PartitionSpec as P

MARK_ROWS = 16
RADIX = 256
CHUNK = 512


def exchanged(value, axis, mask):
    size = lax.axis_size(axis)
    return lax.ppermute(value, axis, [(i, i ^ mask) for i in range(size)])


def total_bytes(values):
    return sum(v.size * v.dtype.itemsize for v in jax.tree.leaves(values))


def call(body, out_shape, operands, after=(), flops=0, temporary=0, name="kernel"):
    specs = []
    for v in operands:
        scalar = v.shape == (1,)
        specs.append(pl.BlockSpec(memory_space=pltpu.SMEM if scalar else pltpu.VMEM))
    specs += [pl.BlockSpec(memory_space=pl.ANY) for _ in after]
    used = len(operands)

    def whole(*refs):
        body(*refs[:used], *refs[used + len(after) :])

    moved = total_bytes(operands) + total_bytes(out_shape)
    return pl.pallas_call(
        whole,
        out_shape=out_shape,
        in_specs=specs,
        out_specs=jax.tree.map(lambda _: pl.BlockSpec(memory_space=pltpu.VMEM), out_shape),
        compiler_params=pltpu.CompilerParams(vmem_limit_bytes=(4 << 20) + 2 * moved + temporary),
        cost_estimate=pl.CostEstimate(flops=flops, bytes_accessed=moved, transcendentals=0),
        name=name,
    )(*operands, *after)


def direction(values):
    floats = values.astype(jnp.float32)
    norms = jnp.sqrt(jnp.sum(floats * floats, axis=-1, keepdims=True) + 1e-06)
    return floats / norms, norms


def prepare_body(audio_hbm, sentence_hbm, label_hbm, speech, text, audio, sentence, label, done):
    pairs = [(audio_hbm, audio), (sentence_hbm, sentence), (label_hbm, label)]
    copies = [
        pltpu.make_async_copy(source, target, done.at[i]) for i, (source, target) in enumerate(pairs)
    ]
    for copy in copies:
        copy.start()
    for copy in copies:
        copy.wait()
    rows = audio.shape[0]
    speech[0:rows, :] = direction(audio[...])[0].astype(jnp.bfloat16)
    text[...] = direction(sentence[...])[0].astype(jnp.bfloat16)
    number = label[...]
    digits = jnp.concatenate([number % RADIX, number // RADIX], axis=1).astype(jnp.float32)
    wide = jnp.concatenate(
        [digits, jnp.zeros((1, speech.shape[1] - 2 * rows), jnp.float32)], axis=1
    )
    speech[rows : rows + MARK_ROWS, :] = jnp.broadcast_to(
        wide, (MARK_ROWS, speech.shape[1])
    ).astype(jnp.bfloat16)


def unit_body(values, out):
    out[...] = direction(values[...])[0].astype(jnp.bfloat16)


def join_body(chips, raw, *refs):
    speech, text = refs[-2:]
    rows = refs[0].shape[0]
    for k in range(chips):
        speech[k * rows : (k + 1) * rows, :] = refs[k][...]
    rows = refs[chips].shape[0]
    for k, is_raw in enumerate(raw):
        block = refs[chips + k]
        target = text.at[k * rows : (k + 1) * rows, :]
        if is_raw:
            unit_body(block, target)
        else:
            target[...] = block[...]


def marks_of(block, rows):
    digits = block[rows : rows + MARK_ROWS, 0 : 2 * rows][0:1, :].astype(jnp.float32)
    return digits[:, 0:rows] + RADIX * digits[:, rows : 2 * rows]


def coefficients(dots, match, sharp, shift):
    logits = sharp * dots + shift
    probs = 1.0 / (1.0 + jnp.exp(-logits))
    return (sharp * (probs - jnp.where(match, 1.0, 0.0))).astype(jnp.bfloat16)


def dot_rows(left, right):
    return lax.dot_general(left, right, (((1,), (1,)), ((), ())), preferred_element_type=jnp.float32)


def text_part_body(rows, own_text, *refs):
    sharp, shift = refs[0][0], refs[1][0]
    text, speech = refs[2][...], refs[3]
    start = refs[4] if len(refs) > 5 and refs[4].shape == text.shape else None
    outs = refs[4:] if start is None else refs[5:]
    groups = lax.axis_size("group")
    members = lax.axis_size("member")
    group = lax.axis_index("group")
    member = lax.axis_index("member")
    stride = rows + MARK_ROWS
    count = speech.shape[0] // stride
    step = max(1, min(count, CHUNK // rows))
    iota = lax.broadcasted_iota(jnp.int32, (own_text, step * rows), 0)
    ids = [((group ^ k) * members + member) * own_text + iota for k in range(groups)]
    ids = jnp.concatenate(ids, axis=0).astype(jnp.float32)
    total = None if start is None else start[...]
    for first in range(0, count, step):
        blocks = range(first, first + step)
        chunk = jnp.concatenate([speech[k * stride : k * stride + rows, :] for k in blocks], axis=0)
        marks = [marks_of(speech.at[k * stride : (k + 1) * stride, :], rows) for k in blocks]
        match = ids == jnp.concatenate(marks, axis=1)
        coef = coefficients(dot_rows(text, chunk), match, sharp, shift)
        part = jnp.dot(coef, chunk, preferred_element_type=jnp.float32)
        total = part if total is None else total + part
    size = outs[0].shape[0]
    for k, out in enumerate(outs):
        out[...] = total[k * size : (k + 1) * size, :]


def speech_part_body(rows, own_text, *refs):
    sharp, shift = refs[0][0], refs[1][0]
    speech, texts, out = refs[2], refs[3:-1], refs[-1]
    groups = lax.axis_size("group")
    members = lax.axis_size("member")
    group = lax.axis_index("group")
    member = lax.axis_index("member")
    marks = jnp.broadcast_to(marks_of(speech, rows), (rows, rows)).T[:, 0:1]
    block = speech[0:rows, :]
    lane = lax.broadcasted_iota(jnp.int32, (1, groups * own_text), 1)
    base = (group ^ (lane // own_text)) * members * own_text + lane % own_text
    total = None
    for j, text in enumerate(texts):
        ids = (base + (member ^ (2 * j)) * own_text).astype(jnp.float32)
        coef = coefficients(dot_rows(block, text[...]), marks == ids, sharp, shift)
        part = jnp.dot(coef, text[...], preferred_element_type=jnp.float32)
        total = part if total is None else total + part
    out[...] = total


def sum_body(*refs):
    total = refs[0][...]
    for ref in refs[1:-1]:
        total = total + ref[...]
    refs[-1][...] = total


def project(values, back, out):
    heading, norms = direction(values)
    along = jnp.sum(heading * back, axis=-1, keepdims=True)
    out[...] = (back - heading * along) / norms


def finish_body(audio, home, back, sentence, text_back, speech_grad, text_grad):
    project(sentence[...], text_back[...], text_grad)
    project(audio[...], home[...] + back[...], speech_grad)


def shards(audio_vectors, sentence_vectors, matching_indices, sharpness_array, offset_term):
    members = lax.axis_size("member")
    groups = lax.axis_size("group")
    chips = members // 2
    rows, width = audio_vectors.shape
    own_text = sentence_vectors.shape[0]
    scalars = [sharpness_array, offset_term]
    label = matching_indices.reshape(1, rows)

    def bf16(*shape):
        return jax.ShapeDtypeStruct(shape, jnp.bfloat16)

    def f32(*shape):
        return jax.ShapeDtypeStruct(shape, jnp.float32)

    speech_own, text_own = pl.pallas_call(
        prepare_body,
        out_shape=[bf16(rows + MARK_ROWS, width), bf16(own_text, width)],
        in_specs=[pl.BlockSpec(memory_space=pltpu.HBM)] * 3,
        out_specs=[pl.BlockSpec(memory_space=pltpu.VMEM)] * 2,
        scratch_shapes=[
            pltpu.VMEM((rows, width), jnp.bfloat16),
            pltpu.VMEM((own_text, width), jnp.bfloat16),
            pltpu.VMEM((1, rows), jnp.int32),
            pltpu.SemaphoreType.DMA((3,)),
        ],
        compiler_params=pltpu.CompilerParams(vmem_limit_bytes=8 << 20),
        name="unit_rows",
    )(*[pltpu.with_memory_space_constraint(v, pltpu.HBM) for v in (audio_vectors, sentence_vectors, label)])
    text_blocks = [text_own] + [None] * (groups - 1)
    raw = [False] * groups
    for k in [1 << i for i in reversed(range(groups.bit_length() - 1))]:
        for j in range(0, groups, 2 * k):
            came = exchanged(text_blocks[j] if j else sentence_vectors, "group", k)
            raw[j + k] = not j
            if not j and k > 1:
                came = call(unit_body, bf16(own_text, width), [came], (), 1 << 33, name="unit_far")
                raw[j + k] = False
            text_blocks[j + k] = came
    speech_blocks = [speech_own]
    for k in range(1, chips):
        speech_blocks.append(exchanged(speech_own, "member", 2 * k))
    column = groups * own_text
    speech, text = call(
        functools.partial(join_body, chips, raw),
        [bf16(chips * (rows + MARK_ROWS), width), bf16(column, width)],
        speech_blocks + text_blocks,
        name="join_rows",
    )
    other = exchanged(speech, "member", 1)
    texts = [text]
    for k in range(1, chips):
        texts.append(exchanged(text, "member", 2 * k))

    text_part = functools.partial(text_part_body, rows, own_text)
    work = 4 * column * chips * rows * width
    temporary = 4 * column * (6 * CHUNK + 3 * width)
    half = call(
        text_part, [f32(column, width)], scalars + [text, speech], (), work, temporary, "text_part"
    )
    parts = call(
        text_part,
        [f32(own_text, width)] * groups,
        scalars + [text, other, half[0]],
        (),
        work,
        temporary,
        "text_part_sum",
    )
    text_back = [parts[0]]
    for k in reversed(range(1, groups)):
        text_back.append(exchanged(parts[k], "group", k))

    speech_part = functools.partial(speech_part_body, rows, own_text)
    work = 4 * rows * chips * column * width
    stride = rows + MARK_ROWS
    away = call(
        speech_part,
        f32(rows, width),
        scalars + [other[0:stride]] + texts,
        (parts[0],),
        work,
        temporary,
        "speech_part",
    )
    back = exchanged(away, "member", 1)
    home = call(
        speech_part,
        f32(rows, width),
        scalars + [speech_own] + texts,
        (away,),
        work,
        temporary,
        "speech_part",
    )
    text_back = call(sum_body, f32(own_text, width), text_back, (), 1 << 33, name="text_sum")
    speech_grad, text_grad = call(
        finish_body,
        [f32(rows, width), f32(own_text, width)],
        [audio_vectors, home, back, sentence_vectors, text_back],
        name="finish",
    )
    return (speech_grad, text_grad)


def solution(mesh):
    in_specs = (
        P(("group", "member"), None),
        P(("group", "member"), None),
        P(("group", "member")),
        P(),
        P(),
    )
    out_specs = (P(("group", "member"), None), P(("group", "member"), None))
    return jax.shard_map(shards, mesh=mesh, in_specs=in_specs, out_specs=out_specs, check_vma=False)
```

```python
import functools
import jax
import jax.numpy as jnp
from jax import lax
from jax.experimental import pallas as pl
from jax.experimental.pallas import tpu as pltpu
from jax.sharding import PartitionSpec as P

MARK_ROWS = 16
RADIX = 256
CHUNK = 512
EARLY = 1 << 33


def exchanged(value, axis, mask):
    size = lax.axis_size(axis)
    return lax.ppermute(value, axis, [(i, i ^ mask) for i in range(size)])


def total_bytes(values):
    return sum(v.size * v.dtype.itemsize for v in jax.tree.leaves(values))


def call(body, out_shape, operands, after=(), flops=0, temporary=0, name="kernel"):
    specs = []
    for v in operands:
        scalar = v.shape == (1,)
        specs.append(pl.BlockSpec(memory_space=pltpu.SMEM if scalar else pltpu.VMEM))
    specs += [pl.BlockSpec(memory_space=pl.ANY) for _ in after]
    used = len(operands)

    def whole(*refs):
        body(*refs[:used], *refs[used + len(after) :])

    moved = total_bytes(operands) + total_bytes(out_shape)
    return pl.pallas_call(
        whole,
        out_shape=out_shape,
        in_specs=specs,
        out_specs=jax.tree.map(lambda _: pl.BlockSpec(memory_space=pltpu.VMEM), out_shape),
        compiler_params=pltpu.CompilerParams(vmem_limit_bytes=(4 << 20) + 2 * moved + temporary),
        cost_estimate=pl.CostEstimate(flops=flops, bytes_accessed=moved, transcendentals=0),
        name=name,
    )(*operands, *after)


def direction(values):
    floats = values.astype(jnp.float32)
    norms = jnp.sqrt(jnp.sum(floats * floats, axis=-1, keepdims=True) + 1e-06)
    return floats / norms, norms


def prepare_body(audio_hbm, sentence_hbm, label_hbm, speech, text, audio, sentence, label, done):
    pairs = [(audio_hbm, audio), (sentence_hbm, sentence), (label_hbm, label)]
    copies = [
        pltpu.make_async_copy(source, target, done.at[i]) for i, (source, target) in enumerate(pairs)
    ]
    for copy in copies:
        copy.start()
    for copy in copies:
        copy.wait()
    rows = audio.shape[0]
    speech[0:rows, :] = direction(audio[...])[0].astype(jnp.bfloat16)
    text[...] = direction(sentence[...])[0].astype(jnp.bfloat16)
    number = label[...]
    digits = jnp.concatenate([number % RADIX, number // RADIX], axis=1).astype(jnp.float32)
    wide = jnp.concatenate(
        [digits, jnp.zeros((1, speech.shape[1] - 2 * rows), jnp.float32)], axis=1
    )
    speech[rows : rows + MARK_ROWS, :] = jnp.broadcast_to(
        wide, (MARK_ROWS, speech.shape[1])
    ).astype(jnp.bfloat16)


def unit_body(values, out):
    out[...] = direction(values[...])[0].astype(jnp.bfloat16)


def join_body(raw, *refs):
    out = refs[-1]
    at = 0
    for ref, is_raw in zip(refs[:-1], raw):
        target = out.at[at : at + ref.shape[0], :]
        at += ref.shape[0]
        if is_raw:
            unit_body(ref, target)
        else:
            target[...] = ref[...]


def halves_body(upper, lower, upper_out, lower_out):
    upper_out[...] = upper[: upper_out.shape[0], :]
    lower_out[...] = lower[upper_out.shape[0] :, :]


def joined(blocks, raw=None, after=(), name="join"):
    shape = (sum(v.shape[0] for v in blocks), blocks[0].shape[1])
    body = functools.partial(join_body, raw or [False] * len(blocks))
    return call(body, jax.ShapeDtypeStruct(shape, jnp.bfloat16), blocks, after, name=name)


def marks_of(block, rows):
    digits = block[rows : rows + MARK_ROWS, 0 : 2 * rows][0:1, :].astype(jnp.float32)
    return digits[:, 0:rows] + RADIX * digits[:, rows : 2 * rows]


def coefficients(dots, match, sharp, shift):
    logits = sharp * dots + shift
    probs = 1.0 / (1.0 + jnp.exp(-logits))
    return (sharp * (probs - jnp.where(match, 1.0, 0.0))).astype(jnp.bfloat16)


def dot_rows(left, right):
    return lax.dot_general(left, right, (((1,), (1,)), ((), ())), preferred_element_type=jnp.float32)


def text_part_body(rows, own_text, has_start, speeches, *refs):
    sharp, shift, text = refs[0][0], refs[1][0], refs[2][...]
    total = refs[3][...] if has_start else None
    at = 4 if has_start else 3
    blocks = refs[at : at + speeches]
    outs = refs[at + speeches :]
    groups = lax.axis_size("group")
    members = lax.axis_size("member")
    group = lax.axis_index("group")
    member = lax.axis_index("member")
    stride = rows + MARK_ROWS
    for speech in blocks:
        count = speech.shape[0] // stride
        for first in range(0, count, CHUNK // rows):
            some = range(first, min(count, first + CHUNK // rows))
            chunk = [speech[k * stride : k * stride + rows, :] for k in some]
            marks = [marks_of(speech.at[k * stride : (k + 1) * stride, :], rows) for k in some]
            chunk = jnp.concatenate(chunk, axis=0)
            marks = jnp.concatenate(marks, axis=1)
            iota = lax.broadcasted_iota(jnp.int32, (own_text, marks.shape[1]), 0)
            ids = [((group ^ k) * members + member) * own_text + iota for k in range(groups)]
            match = jnp.concatenate(ids, axis=0).astype(jnp.float32) == marks
            coef = coefficients(dot_rows(text, chunk), match, sharp, shift)
            part = jnp.dot(coef, chunk, preferred_element_type=jnp.float32)
            total = part if total is None else total + part
    size = outs[0].shape[0]
    for k, out in enumerate(outs):
        out[...] = total[k * size : (k + 1) * size, :]


def speech_part_body(rows, own_text, has_start, masks, *refs):
    sharp, shift, speech = refs[0][0], refs[1][0], refs[2]
    total = refs[3][...] if has_start else None
    texts, out = list(refs[4 if has_start else 3 : -1]), refs[-1]
    groups = lax.axis_size("group")
    members = lax.axis_size("member")
    group = lax.axis_index("group")
    member = lax.axis_index("member")
    marks = jnp.broadcast_to(marks_of(speech, rows), (rows, rows)).T[:, 0:1]
    block = speech[0:rows, :]
    column = groups * own_text
    lane = lax.broadcasted_iota(jnp.int32, (1, column), 1)
    base = (group ^ (lane // own_text)) * members * own_text + lane % own_text
    for mask in masks:
        pieces = [texts.pop(0)[...]]
        while sum(v.shape[0] for v in pieces) < column:
            pieces.append(texts.pop(0)[...])
        text = jnp.concatenate(pieces, axis=0)
        ids = (base + (member ^ (2 * mask)) * own_text).astype(jnp.float32)
        coef = coefficients(dot_rows(block, text), marks == ids, sharp, shift)
        part = jnp.dot(coef, text, preferred_element_type=jnp.float32)
        total = part if total is None else total + part
    out[...] = total


def sum_body(*refs):
    total = refs[0][...]
    for ref in refs[1:-1]:
        total = total + ref[...]
    refs[-1][...] = total


def project(values, back, out):
    heading, norms = direction(values)
    along = jnp.sum(heading * back, axis=-1, keepdims=True)
    out[...] = (back - heading * along) / norms


def finish_body(audio, home, back, sentence, text_back, speech_grad, text_grad):
    project(sentence[...], text_back[...], text_grad)
    project(audio[...], home[...] + back[...], speech_grad)


def shards(audio_vectors, sentence_vectors, matching_indices, sharpness_array, offset_term):
    members = lax.axis_size("member")
    groups = lax.axis_size("group")
    chips = members // 2
    rows, width = audio_vectors.shape
    own_text = sentence_vectors.shape[0]
    scalars = [sharpness_array, offset_term]
    label = matching_indices.reshape(1, rows)

    def bf16(*shape):
        return jax.ShapeDtypeStruct(shape, jnp.bfloat16)

    def f32(*shape):
        return jax.ShapeDtypeStruct(shape, jnp.float32)

    speech_own, text_own = pl.pallas_call(
        prepare_body,
        out_shape=[bf16(rows + MARK_ROWS, width), bf16(own_text, width)],
        in_specs=[pl.BlockSpec(memory_space=pltpu.HBM)] * 3,
        out_specs=[pl.BlockSpec(memory_space=pltpu.VMEM)] * 2,
        scratch_shapes=[
            pltpu.VMEM((rows, width), jnp.bfloat16),
            pltpu.VMEM((own_text, width), jnp.bfloat16),
            pltpu.VMEM((1, rows), jnp.int32),
            pltpu.SemaphoreType.DMA((3,)),
        ],
        compiler_params=pltpu.CompilerParams(vmem_limit_bytes=8 << 20),
        name="unit_rows",
    )(*[pltpu.with_memory_space_constraint(v, pltpu.HBM) for v in (audio_vectors, sentence_vectors, label)])
    text_blocks = [text_own] + [None] * (groups - 1)
    raw = [False] * groups
    for k in [1 << i for i in reversed(range(groups.bit_length() - 1))]:
        for j in range(0, groups, 2 * k):
            came = exchanged(text_blocks[j] if j else sentence_vectors, "group", k)
            raw[j + k] = not j
            if not j and k > 1:
                came = call(unit_body, bf16(own_text, width), [came], (), EARLY, name="unit_far")
                raw[j + k] = False
            text_blocks[j + k] = came
    square = chips == 4
    masks = [1, 2] if square else list(range(1, chips))

    def far_halves(near, middle, after=()):
        sizes = [middle, near[0].shape[0] - middle]
        halves = call(
            halves_body, [bf16(size, width) for size in sizes], near[::-1], after, name="halves"
        )
        return [exchanged(half, "member", 2 * k) for half, k in zip(halves, masks)]

    speech_near = [exchanged(speech_own, "member", 2 * k) for k in masks]
    speech = [joined([speech_own, *speech_near], name="join_speech")]
    other = [exchanged(speech[0], "member", 1)]
    if square:
        speech.append(joined(far_halves(speech_near, rows // 2), name="join_far"))
        other.append(exchanged(speech[1], "member", 1))
    text = joined(text_blocks, raw, (speech[-1],), name="join_text")
    text_near = [exchanged(text, "member", 2 * k) for k in masks]

    column = groups * own_text
    temporary = 4 * column * (6 * CHUNK + 3 * width)

    def text_part(outs, blocks, start):
        count = sum(v.shape[0] for v in blocks) // (rows + MARK_ROWS)
        body = functools.partial(text_part_body, rows, own_text, bool(start), len(blocks))
        operands = [*scalars, text, *start, *blocks]
        work = 4 * column * count * rows * width
        return call(body, outs, operands, (), work, temporary, "text_part")

    half = text_part([f32(column, width)], [*speech, *other[:-1]], [])
    parts = list(text_part([f32(own_text, width)] * groups, other[-1:], half))

    text_back = [parts[0]]
    for bit in [1 << i for i in range(groups.bit_length() - 1)]:
        for k in reversed(range(bit, groups, 2 * bit)):
            came = exchanged(parts[k], "group", bit)
            if k == bit:
                text_back.append(came)
            else:
                parts[k - bit] = call(
                    sum_body, f32(own_text, width), [parts[k - bit], came], name="sum_near"
                )

    def speech_part(block, start, columns, texts, after=()):
        body = functools.partial(speech_part_body, rows, own_text, bool(start), columns)
        operands = [*scalars, block, *start, *texts]
        work = 40 * rows * column * len(columns) * width
        return call(body, f32(rows, width), operands, after, work, temporary, "speech_part")

    near = [[0, *masks], [text, *text_near], (parts[groups // 2],)]
    away = speech_part(other[0][0 : rows + MARK_ROWS], [], *near)
    home = speech_part(speech_own, [], *near)
    if square:
        text_far = far_halves(text_near, column // 2, (parts[groups // 2],))
        away = speech_part(other[0][0 : rows + MARK_ROWS], [away], [3], text_far)
        home = speech_part(speech_own, [home], [3], text_far)
    back = exchanged(away, "member", 1)
    text_back = call(sum_body, f32(own_text, width), text_back, (), EARLY, name="text_sum")
    speech_grad, text_grad = call(
        finish_body,
        [f32(rows, width), f32(own_text, width)],
        [audio_vectors, home, back, sentence_vectors, text_back],
        name="finish",
    )
    return (speech_grad, text_grad)


def solution(mesh):
    in_specs = (
        P(("group", "member"), None),
        P(("group", "member"), None),
        P(("group", "member")),
        P(),
        P(),
    )
    out_specs = (P(("group", "member"), None), P(("group", "member"), None))
    return jax.shard_map(shards, mesh=mesh, in_specs=in_specs, out_specs=out_specs, check_vma=False)
```

```python
import functools
import jax
import jax.numpy as jnp
from jax import lax
from jax.experimental import pallas as pl
from jax.experimental.pallas import tpu as pltpu
from jax.sharding import PartitionSpec as P

MARK_ROWS = 16
RADIX = 256
CHUNK = 512
EARLY = 1 << 33


def exchanged(value, axis, mask):
    size = lax.axis_size(axis)
    return lax.ppermute(value, axis, [(i, i ^ mask) for i in range(size)])


def total_bytes(values):
    return sum(v.size * v.dtype.itemsize for v in jax.tree.leaves(values))


def call(body, out_shape, operands, after=(), flops=0, temporary=0, name="kernel"):
    specs = [pl.BlockSpec(memory_space=pltpu.VMEM) for _ in operands]
    specs += [pl.BlockSpec(memory_space=pl.ANY) for _ in after]
    used = len(operands)

    def whole(*refs):
        body(*refs[:used], *refs[used + len(after) :])

    moved = total_bytes(operands) + total_bytes(out_shape)
    return pl.pallas_call(
        whole,
        out_shape=out_shape,
        in_specs=specs,
        out_specs=jax.tree.map(lambda _: pl.BlockSpec(memory_space=pltpu.VMEM), out_shape),
        compiler_params=pltpu.CompilerParams(vmem_limit_bytes=(4 << 20) + 2 * moved + temporary),
        cost_estimate=pl.CostEstimate(flops=flops, bytes_accessed=moved, transcendentals=0),
        name=name,
    )(*operands, *after)


def direction(values):
    floats = values.astype(jnp.float32)
    norms = jnp.sqrt(jnp.sum(floats * floats, axis=-1, keepdims=True) + 1e-06)
    return floats / norms, norms


def prepare_body(*refs):
    sources, (speech, text) = refs[:3], refs[3:5]
    held, done = refs[5:8], refs[8]
    copies = [pltpu.make_async_copy(sources[i], held[i], done.at[i]) for i in range(3)]
    for copy in copies:
        copy.start()
    for copy in copies:
        copy.wait()
    audio, sentence, label = held
    rows = audio.shape[0]
    speech[0:rows, :] = direction(audio[...])[0].astype(jnp.bfloat16)
    text[...] = direction(sentence[...])[0].astype(jnp.bfloat16)
    number = label[...]
    digits = jnp.concatenate([number % RADIX, number // RADIX], axis=1).astype(jnp.float32)
    wide = jnp.concatenate(
        [digits, jnp.zeros((1, speech.shape[1] - 2 * rows), jnp.float32)], axis=1
    )
    speech[rows : rows + MARK_ROWS, :] = jnp.broadcast_to(
        wide, (MARK_ROWS, speech.shape[1])
    ).astype(jnp.bfloat16)


def unit_body(values, out):
    out[...] = direction(values[...])[0].astype(jnp.bfloat16)


def join_body(chips, raw, *refs):
    speech, text = refs[-2:]
    rows = refs[0].shape[0]
    for k in range(chips):
        speech[k * rows : (k + 1) * rows, :] = refs[k][...]
    rows = refs[chips].shape[0]
    for k, is_raw in enumerate(raw):
        block = refs[chips + k]
        target = text.at[k * rows : (k + 1) * rows, :]
        if is_raw:
            unit_body(block, target)
        else:
            target[...] = block[...]


def halves_body(upper, lower, upper_out, lower_out):
    upper_out[...] = upper[: upper_out.shape[0], :]
    lower_out[...] = lower[upper_out.shape[0] :, :]


def marks_of(block, rows):
    digits = block[rows : rows + MARK_ROWS, 0 : 2 * rows][0:1, :].astype(jnp.float32)
    return digits[:, 0:rows] + RADIX * digits[:, rows : 2 * rows]


def coefficients(dots, match, sharp, shift):
    logits = sharp * dots + shift
    probs = 1.0 / (1.0 + jnp.exp(-logits))
    return (sharp * (probs - jnp.where(match, 1.0, 0.0))).astype(jnp.bfloat16)


def dot_rows(left, right):
    return lax.dot_general(left, right, (((1,), (1,)), ((), ())), preferred_element_type=jnp.float32)


def text_part_body(rows, own_text, has_start, speeches, *refs):
    sharp, shift, text = refs[0][0:1, 0:1], refs[0][1:2, 0:1], refs[1][...]
    total = refs[2][...] if has_start else None
    at = 3 if has_start else 2
    blocks = refs[at : at + speeches]
    outs = refs[at + speeches :]
    groups = lax.axis_size("group")
    members = lax.axis_size("member")
    group = lax.axis_index("group")
    member = lax.axis_index("member")
    stride = rows + MARK_ROWS
    for speech in blocks:
        count = speech.shape[0] // stride
        for first in range(0, count, CHUNK // rows):
            some = range(first, min(count, first + CHUNK // rows))
            chunk = [speech[k * stride : k * stride + rows, :] for k in some]
            marks = [marks_of(speech.at[k * stride : (k + 1) * stride, :], rows) for k in some]
            chunk = jnp.concatenate(chunk, axis=0)
            marks = jnp.concatenate(marks, axis=1)
            iota = lax.broadcasted_iota(jnp.int32, (own_text, marks.shape[1]), 0)
            ids = [((group ^ k) * members + member) * own_text + iota for k in range(groups)]
            match = jnp.concatenate(ids, axis=0).astype(jnp.float32) == marks
            coef = coefficients(dot_rows(text, chunk), match, sharp, shift)
            part = jnp.dot(coef, chunk, preferred_element_type=jnp.float32)
            total = part if total is None else total + part
    size = outs[0].shape[0]
    for k, out in enumerate(outs):
        out[...] = total[k * size : (k + 1) * size, :]


def speech_part_body(rows, own_text, has_start, masks, *refs):
    sharp, shift, speech = refs[0][0:1, 0:1], refs[0][1:2, 0:1], refs[1]
    total = refs[2][...] if has_start else None
    texts, out = list(refs[3 if has_start else 2 : -1]), refs[-1]
    groups = lax.axis_size("group")
    members = lax.axis_size("member")
    group = lax.axis_index("group")
    member = lax.axis_index("member")
    marks = jnp.broadcast_to(marks_of(speech, rows), (rows, rows)).T[:, 0:1]
    block = speech[0:rows, :]
    column = groups * own_text
    lane = lax.broadcasted_iota(jnp.int32, (1, column), 1)
    base = (group ^ (lane // own_text)) * members * own_text + lane % own_text
    for mask in masks:
        pieces = [texts.pop(0)[...]]
        while sum(v.shape[0] for v in pieces) < column:
            pieces.append(texts.pop(0)[...])
        text = jnp.concatenate(pieces, axis=0)
        ids = (base + (member ^ (2 * mask)) * own_text).astype(jnp.float32)
        coef = coefficients(dot_rows(block, text), marks == ids, sharp, shift)
        part = jnp.dot(coef, text, preferred_element_type=jnp.float32)
        total = part if total is None else total + part
    out[...] = total


def sum_near_body(mine, came, kept, total, kept_out):
    total[...] = mine[...] + came[...]
    kept_out[...] = kept[...]


def sum_body(*refs):
    total = refs[0][...]
    for ref in refs[1:-1]:
        total = total + ref[...]
    refs[-1][...] = total


def project(values, back, out):
    heading, norms = direction(values)
    along = jnp.sum(heading * back, axis=-1, keepdims=True)
    out[...] = (back - heading * along) / norms


def finish_body(audio, home, back, sentence, text_back, speech_grad, text_grad):
    project(sentence[...], text_back[...], text_grad)
    project(audio[...], home[...] + back[...], speech_grad)


def shards(audio_vectors, sentence_vectors, matching_indices, sharpness_array, offset_term):
    members = lax.axis_size("member")
    groups = lax.axis_size("group")
    chips = members // 2
    rows, width = audio_vectors.shape
    own_text = sentence_vectors.shape[0]
    label = matching_indices.reshape(1, rows)
    scalars = jnp.concatenate(
        [jnp.broadcast_to(v[:, None], (1, 128)) for v in (sharpness_array, offset_term)], axis=0
    )

    def bf16(*shape):
        return jax.ShapeDtypeStruct(shape, jnp.bfloat16)

    def f32(*shape):
        return jax.ShapeDtypeStruct(shape, jnp.float32)

    arguments = [audio_vectors, sentence_vectors, label]
    speech_own, text_own = pl.pallas_call(
        prepare_body,
        out_shape=[bf16(rows + MARK_ROWS, width), bf16(own_text, width)],
        in_specs=[pl.BlockSpec(memory_space=pltpu.HBM)] * 3,
        out_specs=[pl.BlockSpec(memory_space=pltpu.VMEM)] * 2,
        scratch_shapes=[
            *[pltpu.VMEM(v.shape, v.dtype) for v in arguments],
            pltpu.SemaphoreType.DMA((3,)),
        ],
        compiler_params=pltpu.CompilerParams(vmem_limit_bytes=8 << 20),
        name="unit_rows",
    )(*[pltpu.with_memory_space_constraint(v, pltpu.HBM) for v in arguments])
    text_blocks = [text_own] + [None] * (groups - 1)
    raw = [False] * groups
    for k in [1 << i for i in reversed(range(groups.bit_length() - 1))]:
        for j in range(0, groups, 2 * k):
            came = exchanged(text_blocks[j] if j else sentence_vectors, "group", k)
            raw[j + k] = not j
            if not j and k > 1:
                came = call(unit_body, bf16(own_text, width), [came], (scalars,), EARLY, name="unit_far")
                raw[j + k] = False
            text_blocks[j + k] = came
    square = chips == 4
    masks = [1, 2] if square else list(range(1, chips))

    def far_halves(near, middle, after=()):
        sizes = [middle, near[0].shape[0] - middle]
        halves = call(
            halves_body, [bf16(size, width) for size in sizes], near[::-1], after, name="halves"
        )
        return [exchanged(half, "member", 2 * k) for half, k in zip(halves, masks)]

    speech_blocks = [exchanged(speech_own, "member", 2 * k) for k in reversed(range(1, chips))]
    column = groups * own_text
    speech, text = call(
        functools.partial(join_body, chips, raw),
        [bf16(chips * (rows + MARK_ROWS), width), bf16(column, width)],
        [speech_own, *speech_blocks, *text_blocks],
        name="join_rows",
    )
    other = exchanged(speech, "member", 1)
    text_near = [exchanged(text, "member", 2 * k) for k in masks]

    temporary = 4 * column * (6 * CHUNK + 3 * width)

    def text_part(outs, blocks, start):
        count = sum(v.shape[0] for v in blocks) // (rows + MARK_ROWS)
        body = functools.partial(text_part_body, rows, own_text, bool(start), len(blocks))
        operands = [scalars, text, *start, *blocks]
        work = 4 * column * count * rows * width
        return call(body, outs, operands, (), work, temporary, "text_part")

    half = text_part([f32(column, width)], [speech], [])
    parts = list(text_part([f32(own_text, width)] * groups, [other], half))

    text_back = [parts[0]]
    for bit in [1 << i for i in range(groups.bit_length() - 1)]:
        for k in reversed(range(bit, groups, 2 * bit)):
            came = exchanged(parts[k], "group", bit)
            if k == bit:
                text_back.append(came)
            else:
                parts[k - bit], parts[bit] = call(
                    sum_near_body,
                    [f32(own_text, width)] * 2,
                    [parts[k - bit], came, parts[bit]],
                    name="sum_near",
                )

    def speech_part(block, start, columns, texts, after=()):
        body = functools.partial(speech_part_body, rows, own_text, bool(start), columns)
        operands = [scalars, block, *start, *texts]
        work = 40 * rows * column * len(columns) * width
        return call(body, f32(rows, width), operands, after, work, temporary, "speech_part")

    near = [[0, *masks], [text, *text_near], (parts[groups // 2],)]
    away = speech_part(other[0 : rows + MARK_ROWS], [], *near)
    home = speech_part(speech_own, [], *near)
    if square:
        text_far = far_halves(text_near, column // 2, (parts[groups // 2],))
        away = speech_part(other[0 : rows + MARK_ROWS], [away], [3], text_far)
        home = speech_part(speech_own, [home], [3], text_far)
    back = exchanged(away, "member", 1)
    text_back = call(sum_body, f32(own_text, width), text_back[::-1], (), EARLY, name="text_sum")
    speech_grad, text_grad = call(
        finish_body,
        [f32(rows, width), f32(own_text, width)],
        [audio_vectors, home, back, sentence_vectors, text_back],
        name="finish",
    )
    return (speech_grad, text_grad)


def solution(mesh):
    in_specs = (
        P(("group", "member"), None),
        P(("group", "member"), None),
        P(("group", "member")),
        P(),
        P(),
    )
    out_specs = (P(("group", "member"), None), P(("group", "member"), None))
    return jax.shard_map(shards, mesh=mesh, in_specs=in_specs, out_specs=out_specs, check_vma=False)
```

```python
import functools
import jax
import jax.numpy as jnp
from jax import lax
from jax.experimental import pallas as pl
from jax.experimental.pallas import tpu as pltpu
from jax.sharding import PartitionSpec as P

MARK_ROWS = 16
RADIX = 256
CHUNK = 512
EARLY = 1 << 33


def exchanged(value, axis, mask):
    size = lax.axis_size(axis)
    return lax.ppermute(value, axis, [(i, i ^ mask) for i in range(size)])


def total_bytes(values):
    return sum(v.size * v.dtype.itemsize for v in jax.tree.leaves(values))


def call(body, out_shape, operands, after=(), flops=0, temporary=0, name="kernel"):
    specs = [pl.BlockSpec(memory_space=pltpu.VMEM) for _ in operands]
    specs += [pl.BlockSpec(memory_space=pl.ANY) for _ in after]
    used = len(operands)

    def whole(*refs):
        body(*refs[:used], *refs[used + len(after) :])

    moved = total_bytes(operands) + total_bytes(out_shape)
    return pl.pallas_call(
        whole,
        out_shape=out_shape,
        in_specs=specs,
        out_specs=jax.tree.map(lambda _: pl.BlockSpec(memory_space=pltpu.VMEM), out_shape),
        compiler_params=pltpu.CompilerParams(vmem_limit_bytes=(4 << 20) + 2 * moved + temporary),
        cost_estimate=pl.CostEstimate(flops=flops, bytes_accessed=moved, transcendentals=0),
        name=name,
    )(*operands, *after)


def direction(values):
    floats = values.astype(jnp.float32)
    norms = jnp.sqrt(jnp.sum(floats * floats, axis=-1, keepdims=True) + 1e-06)
    return floats / norms, norms


def prepare_body(*refs):
    sources, (speech, text) = refs[:3], refs[3:5]
    held, done = refs[5:8], refs[8]
    copies = [pltpu.make_async_copy(sources[i], held[i], done.at[i]) for i in range(3)]
    for copy in copies:
        copy.start()
    for copy in copies:
        copy.wait()
    audio, sentence, label = held
    rows = audio.shape[0]
    speech[0:rows, :] = direction(audio[...])[0].astype(jnp.bfloat16)
    text[...] = direction(sentence[...])[0].astype(jnp.bfloat16)
    number = label[...]
    digits = jnp.concatenate([number % RADIX, number // RADIX], axis=1).astype(jnp.float32)
    wide = jnp.concatenate(
        [digits, jnp.zeros((1, speech.shape[1] - 2 * rows), jnp.float32)], axis=1
    )
    speech[rows : rows + MARK_ROWS, :] = jnp.broadcast_to(
        wide, (MARK_ROWS, speech.shape[1])
    ).astype(jnp.bfloat16)


def join_body(*refs):
    out = refs[-1]
    at = 0
    for ref in refs[:-1]:
        out[at : at + ref.shape[0], :] = ref[...]
        at += ref.shape[0]


def join_both_body(count, *refs):
    join_body(*refs[:count], refs[-2])
    join_body(*refs[count:-2], refs[-1])


def halves_body(upper, lower, upper_out, lower_out):
    upper_out[...] = upper[: upper_out.shape[0], :]
    lower_out[...] = lower[upper_out.shape[0] :, :]


def marks_of(block, rows):
    digits = block[rows : rows + MARK_ROWS, 0 : 2 * rows][0:1, :].astype(jnp.float32)
    return digits[:, 0:rows] + RADIX * digits[:, rows : 2 * rows]


def coefficients(dots, match, sharp, shift):
    logits = sharp * dots + shift
    probs = 1.0 / (1.0 + jnp.exp(-logits))
    return (sharp * (probs - jnp.where(match, 1.0, 0.0))).astype(jnp.bfloat16)


def dot_rows(left, right):
    return lax.dot_general(left, right, (((1,), (1,)), ((), ())), preferred_element_type=jnp.float32)


def text_part_body(rows, own_text, ks, has_start, speeches, *refs):
    sharp, shift = refs[0][0:1, 0:1], refs[0][1:2, 0:1]
    some_text = slice(ks[0] * own_text, (ks[-1] + 1) * own_text)
    text = refs[1][some_text, :]
    total = refs[2][some_text, :] if has_start else None
    at = 3 if has_start else 2
    blocks = refs[at : at + speeches]
    outs = refs[at + speeches :]
    groups = lax.axis_size("group")
    members = lax.axis_size("member")
    group = lax.axis_index("group")
    member = lax.axis_index("member")
    stride = rows + MARK_ROWS
    for speech in blocks:
        count = speech.shape[0] // stride
        for first in range(0, count, CHUNK // rows):
            some = range(first, min(count, first + CHUNK // rows))
            chunk = [speech[k * stride : k * stride + rows, :] for k in some]
            marks = [marks_of(speech.at[k * stride : (k + 1) * stride, :], rows) for k in some]
            chunk = jnp.concatenate(chunk, axis=0)
            marks = jnp.concatenate(marks, axis=1)
            iota = lax.broadcasted_iota(jnp.int32, (own_text, marks.shape[1]), 0)
            ids = [((group ^ k) * members + member) * own_text + iota for k in ks]
            match = jnp.concatenate(ids, axis=0).astype(jnp.float32) == marks
            coef = coefficients(dot_rows(text, chunk), match, sharp, shift)
            part = jnp.dot(coef, chunk, preferred_element_type=jnp.float32)
            total = part if total is None else total + part
    size = outs[0].shape[0]
    for k, out in enumerate(outs):
        out[...] = total[k * size : (k + 1) * size, :]


def speech_part_body(rows, own_text, has_start, masks, *refs):
    sharp, shift, speech = refs[0][0:1, 0:1], refs[0][1:2, 0:1], refs[1]
    total = refs[2][...] if has_start else None
    texts, out = list(refs[3 if has_start else 2 : -1]), refs[-1]
    groups = lax.axis_size("group")
    members = lax.axis_size("member")
    group = lax.axis_index("group")
    member = lax.axis_index("member")
    marks = jnp.broadcast_to(marks_of(speech, rows), (rows, rows)).T[:, 0:1]
    block = speech[0:rows, :]
    column = groups * own_text
    lane = lax.broadcasted_iota(jnp.int32, (1, column), 1)
    base = (group ^ (lane // own_text)) * members * own_text + lane % own_text
    for mask in masks:
        pieces = [texts.pop(0)[...]]
        while sum(v.shape[0] for v in pieces) < column:
            pieces.append(texts.pop(0)[...])
        text = jnp.concatenate(pieces, axis=0)
        ids = (base + (member ^ (2 * mask)) * own_text).astype(jnp.float32)
        coef = coefficients(dot_rows(block, text), marks == ids, sharp, shift)
        part = jnp.dot(coef, text, preferred_element_type=jnp.float32)
        total = part if total is None else total + part
    out[...] = total


def sum_near_body(mine, came, kept, total, kept_out):
    total[...] = mine[...] + came[...]
    kept_out[...] = kept[...]


def sum_body(*refs):
    total = refs[0][...]
    for ref in refs[1:-1]:
        total = total + ref[...]
    refs[-1][...] = total


def project(values, back, out):
    heading, norms = direction(values)
    along = jnp.sum(heading * back, axis=-1, keepdims=True)
    out[...] = (back - heading * along) / norms


def finish_body(audio, home, back, sentence, text_back, speech_grad, text_grad):
    project(sentence[...], text_back[...], text_grad)
    project(audio[...], home[...] + back[...], speech_grad)


def shards(audio_vectors, sentence_vectors, matching_indices, sharpness_array, offset_term):
    members = lax.axis_size("member")
    groups = lax.axis_size("group")
    chips = members // 2
    rows, width = audio_vectors.shape
    own_text = sentence_vectors.shape[0]
    label = matching_indices.reshape(1, rows)
    scalars = jnp.concatenate(
        [jnp.broadcast_to(v[:, None], (1, 128)) for v in (sharpness_array, offset_term)], axis=0
    )

    def bf16(*shape):
        return jax.ShapeDtypeStruct(shape, jnp.bfloat16)

    def f32(*shape):
        return jax.ShapeDtypeStruct(shape, jnp.float32)

    arguments = [audio_vectors, sentence_vectors, label]
    speech_own, text_own = pl.pallas_call(
        prepare_body,
        out_shape=[bf16(rows + MARK_ROWS, width), bf16(own_text, width)],
        in_specs=[pl.BlockSpec(memory_space=pltpu.HBM)] * 3,
        out_specs=[pl.BlockSpec(memory_space=pltpu.VMEM)] * 2,
        scratch_shapes=[
            *[pltpu.VMEM(v.shape, v.dtype) for v in arguments],
            pltpu.SemaphoreType.DMA((3,)),
        ],
        compiler_params=pltpu.CompilerParams(vmem_limit_bytes=8 << 20),
        name="unit_rows",
    )(*[pltpu.with_memory_space_constraint(v, pltpu.HBM) for v in arguments])
    def passed_on(block):
        return call(join_body, bf16(own_text, width), [block], (scalars,), 1 << 29, name="pass_on")

    text_blocks = [text_own] + [None] * (groups - 1)
    for k in [1 << i for i in reversed(range(groups.bit_length() - 1))]:
        for j in range(0, groups, 2 * k):
            came = exchanged(text_blocks[j], "group", k)
            text_blocks[j + k] = passed_on(came) if k > 1 else came
    square = chips == 4
    masks = [1, 2] if square else list(range(1, chips))

    def far_halves(near, middle, after=()):
        sizes = [middle, near[0].shape[0] - middle]
        halves = call(
            halves_body, [bf16(size, width) for size in sizes], near[::-1], after, name="halves"
        )
        return [exchanged(half, "member", 2 * k) for half, k in zip(halves, masks)]

    speech_blocks = [exchanged(speech_own, "member", 2 * k) for k in reversed(range(1, chips))]
    column = groups * own_text
    text, speech = call(
        functools.partial(join_both_body, groups),
        [bf16(column, width), bf16(chips * (rows + MARK_ROWS), width)],
        [*text_blocks, speech_own, *speech_blocks[::-1]],
        name="join_rows",
    )
    other = exchanged(speech, "member", 1)
    text_near = [exchanged(text, "member", 2 * k) for k in masks]

    temporary = 4 * column * (6 * CHUNK + 3 * width)

    def text_part(outs, blocks, start, ks=range(groups)):
        count = sum(v.shape[0] for v in blocks) // (rows + MARK_ROWS)
        body = functools.partial(text_part_body, rows, own_text, list(ks), bool(start), len(blocks))
        operands = [scalars, text, *start, *blocks]
        work = 4 * len(ks) * own_text * count * rows * width
        return call(body, outs, operands, (), work, temporary, "text_part")

    half = text_part([f32(column, width)], [speech], [])
    parts = [None] * groups
    first = [groups - 1]
    parts[groups - 1] = text_part([f32(own_text, width)], [other], half, first)[0]
    rest = list(range(groups - 1))
    for k, part in zip(rest, text_part([f32(own_text, width)] * len(rest), [other], half, rest)):
        parts[k] = part

    text_back = [parts[0]]
    for bit in [1 << i for i in range(groups.bit_length() - 1)]:
        for k in reversed(range(bit, groups, 2 * bit)):
            came = exchanged(parts[k], "group", bit)
            if k == bit:
                text_back.append(came)
            else:
                parts[k - bit], parts[bit] = call(
                    sum_near_body,
                    [f32(own_text, width)] * 2,
                    [parts[k - bit], came, parts[bit]],
                    name="sum_near",
                )

    def speech_part(block, start, columns, texts, after=()):
        body = functools.partial(speech_part_body, rows, own_text, bool(start), columns)
        operands = [scalars, block, *start, *texts]
        work = 40 * rows * column * len(columns) * width
        return call(body, f32(rows, width), operands, after, work, temporary, "speech_part")

    near = [[0, *masks], [text, *text_near], (parts[groups // 2],)]
    away = speech_part(other[0 : rows + MARK_ROWS], [], *near)
    home = speech_part(speech_own, [], *near)
    if square:
        text_far = far_halves(text_near, column // 2, (parts[groups // 2],))
        away = speech_part(other[0 : rows + MARK_ROWS], [away], [3], text_far)
        home = speech_part(speech_own, [home], [3], text_far)
    back = exchanged(away, "member", 1)
    text_back = call(sum_body, f32(own_text, width), text_back[::-1], (home,), EARLY, name="text_sum")
    speech_grad, text_grad = call(
        finish_body,
        [f32(rows, width), f32(own_text, width)],
        [audio_vectors, home, back, sentence_vectors, text_back],
        name="finish",
    )
    return (speech_grad, text_grad)


def solution(mesh):
    in_specs = (
        P(("group", "member"), None),
        P(("group", "member"), None),
        P(("group", "member")),
        P(),
        P(),
    )
    out_specs = (P(("group", "member"), None), P(("group", "member"), None))
    return jax.shard_map(shards, mesh=mesh, in_specs=in_specs, out_specs=out_specs, check_vma=False)
```

```python
import functools
import jax
import jax.numpy as jnp
from jax import lax
from jax.experimental import pallas as pl
from jax.experimental.pallas import tpu as pltpu
from jax.sharding import PartitionSpec as P

MARK_ROWS = 16
RADIX = 256
CHUNK = 512
EARLY = 1 << 33


def exchanged(value, axis, mask):
    size = lax.axis_size(axis)
    return lax.ppermute(value, axis, [(i, i ^ mask) for i in range(size)])


def total_bytes(values):
    return sum(v.size * v.dtype.itemsize for v in jax.tree.leaves(values))


def call(body, out_shape, operands, after=(), flops=0, temporary=0, name="kernel"):
    specs = [pl.BlockSpec(memory_space=pltpu.VMEM) for _ in operands]
    specs += [pl.BlockSpec(memory_space=pl.ANY) for _ in after]
    used = len(operands)

    def whole(*refs):
        body(*refs[:used], *refs[used + len(after) :])

    moved = total_bytes(operands) + total_bytes(out_shape)
    return pl.pallas_call(
        whole,
        out_shape=out_shape,
        in_specs=specs,
        out_specs=jax.tree.map(lambda _: pl.BlockSpec(memory_space=pltpu.VMEM), out_shape),
        compiler_params=pltpu.CompilerParams(vmem_limit_bytes=(4 << 20) + 2 * moved + temporary),
        cost_estimate=pl.CostEstimate(flops=flops, bytes_accessed=moved, transcendentals=0),
        name=name,
    )(*operands, *after)


def direction(values):
    floats = values.astype(jnp.float32)
    norms = jnp.sqrt(jnp.sum(floats * floats, axis=-1, keepdims=True) + 1e-06)
    return floats / norms, norms


def prepare_body(*refs):
    sources, (speech, text) = refs[:3], refs[3:5]
    held, done = refs[5:8], refs[8]
    copies = [pltpu.make_async_copy(sources[i], held[i], done.at[i]) for i in range(3)]
    for copy in copies:
        copy.start()
    for copy in copies:
        copy.wait()
    audio, sentence, label = held
    rows = audio.shape[0]
    speech[0:rows, :] = direction(audio[...])[0].astype(jnp.bfloat16)
    text[...] = direction(sentence[...])[0].astype(jnp.bfloat16)
    number = label[...]
    digits = jnp.concatenate([number % RADIX, number // RADIX], axis=1).astype(jnp.float32)
    wide = jnp.concatenate(
        [digits, jnp.zeros((1, speech.shape[1] - 2 * rows), jnp.float32)], axis=1
    )
    speech[rows : rows + MARK_ROWS, :] = jnp.broadcast_to(
        wide, (MARK_ROWS, speech.shape[1])
    ).astype(jnp.bfloat16)


def join_body(*refs):
    out = refs[-1]
    at = 0
    for ref in refs[:-1]:
        out[at : at + ref.shape[0], :] = ref[...]
        at += ref.shape[0]


def join_both_body(count, *refs):
    join_body(*refs[:count], refs[-2])
    join_body(*refs[count:-2], refs[-1])


def halves_body(upper, lower, upper_out, lower_out):
    upper_out[...] = upper[: upper_out.shape[0], :]
    lower_out[...] = lower[upper_out.shape[0] :, :]


def marks_of(block, rows):
    digits = block[rows : rows + MARK_ROWS, 0 : 2 * rows][0:1, :].astype(jnp.float32)
    return digits[:, 0:rows] + RADIX * digits[:, rows : 2 * rows]


def coefficients(dots, match, sharp, shift):
    logits = sharp * dots + shift
    probs = 1.0 / (1.0 + jnp.exp(-logits))
    return (sharp * (probs - jnp.where(match, 1.0, 0.0))).astype(jnp.bfloat16)


def dot_rows(left, right):
    return lax.dot_general(left, right, (((1,), (1,)), ((), ())), preferred_element_type=jnp.float32)


def text_part_body(rows, own_text, ks, has_start, speeches, *refs):
    sharp, shift = refs[0][0:1, 0:1], refs[0][1:2, 0:1]
    some_text = slice(ks[0] * own_text, (ks[-1] + 1) * own_text)
    text = refs[1][some_text, :]
    total = refs[2][some_text, :] if has_start else None
    at = 3 if has_start else 2
    blocks = refs[at : at + speeches]
    outs = refs[at + speeches :]
    groups = lax.axis_size("group")
    members = lax.axis_size("member")
    group = lax.axis_index("group")
    member = lax.axis_index("member")
    stride = rows + MARK_ROWS
    for speech in blocks:
        count = speech.shape[0] // stride
        for first in range(0, count, CHUNK // rows):
            some = range(first, min(count, first + CHUNK // rows))
            chunk = [speech[k * stride : k * stride + rows, :] for k in some]
            marks = [marks_of(speech.at[k * stride : (k + 1) * stride, :], rows) for k in some]
            chunk = jnp.concatenate(chunk, axis=0)
            marks = jnp.concatenate(marks, axis=1)
            iota = lax.broadcasted_iota(jnp.int32, (own_text, marks.shape[1]), 0)
            ids = [((group ^ k) * members + member) * own_text + iota for k in ks]
            match = jnp.concatenate(ids, axis=0).astype(jnp.float32) == marks
            coef = coefficients(dot_rows(text, chunk), match, sharp, shift)
            part = jnp.dot(coef, chunk, preferred_element_type=jnp.float32)
            total = part if total is None else total + part
    size = outs[0].shape[0]
    for k, out in enumerate(outs):
        out[...] = total[k * size : (k + 1) * size, :]


def speech_part_body(rows, own_text, has_start, masks, *refs):
    sharp, shift, speech = refs[0][0:1, 0:1], refs[0][1:2, 0:1], refs[1]
    total = refs[2][...] if has_start else None
    texts, out = list(refs[3 if has_start else 2 : -1]), refs[-1]
    groups = lax.axis_size("group")
    members = lax.axis_size("member")
    group = lax.axis_index("group")
    member = lax.axis_index("member")
    marks = jnp.broadcast_to(marks_of(speech, rows), (rows, rows)).T[:, 0:1]
    block = speech[0:rows, :]
    column = groups * own_text
    lane = lax.broadcasted_iota(jnp.int32, (1, column), 1)
    base = (group ^ (lane // own_text)) * members * own_text + lane % own_text
    for mask in masks:
        pieces = [texts.pop(0)[...]]
        while sum(v.shape[0] for v in pieces) < column:
            pieces.append(texts.pop(0)[...])
        text = jnp.concatenate(pieces, axis=0)
        ids = (base + (member ^ (2 * mask)) * own_text).astype(jnp.float32)
        coef = coefficients(dot_rows(block, text), marks == ids, sharp, shift)
        part = jnp.dot(coef, text, preferred_element_type=jnp.float32)
        total = part if total is None else total + part
    out[...] = total


def sum_near_body(mine, came, kept, total, kept_out):
    total[...] = mine[...] + came[...]
    kept_out[...] = kept[...]


def sum_body(*refs):
    total = refs[0][...]
    for ref in refs[1:-1]:
        total = total + ref[...]
    refs[-1][...] = total


def project(values, back, out):
    heading, norms = direction(values)
    along = jnp.sum(heading * back, axis=-1, keepdims=True)
    out[...] = (back - heading * along) / norms


def finish_body(audio, home, back, sentence, text_back, speech_grad, text_grad):
    project(sentence[...], text_back[...], text_grad)
    project(audio[...], home[...] + back[...], speech_grad)


def shards(audio_vectors, sentence_vectors, matching_indices, sharpness_array, offset_term):
    members = lax.axis_size("member")
    groups = lax.axis_size("group")
    chips = members // 2
    rows, width = audio_vectors.shape
    own_text = sentence_vectors.shape[0]
    label = matching_indices.reshape(1, rows)
    scalars = jnp.concatenate(
        [jnp.broadcast_to(v[:, None], (1, 128)) for v in (sharpness_array, offset_term)], axis=0
    )

    def bf16(*shape):
        return jax.ShapeDtypeStruct(shape, jnp.bfloat16)

    def f32(*shape):
        return jax.ShapeDtypeStruct(shape, jnp.float32)

    arguments = [audio_vectors, sentence_vectors, label]
    speech_own, text_own, audio, sentence = pl.pallas_call(
        prepare_body,
        out_shape=[
            bf16(rows + MARK_ROWS, width),
            bf16(own_text, width),
            bf16(rows, width),
            bf16(own_text, width),
        ],
        in_specs=[pl.BlockSpec(memory_space=pltpu.HBM)] * 3,
        out_specs=[pl.BlockSpec(memory_space=pltpu.VMEM)] * 4,
        scratch_shapes=[pltpu.VMEM((1, rows), jnp.int32), pltpu.SemaphoreType.DMA((3,))],
        compiler_params=pltpu.CompilerParams(vmem_limit_bytes=8 << 20),
        name="unit_rows",
    )(*[pltpu.with_memory_space_constraint(v, pltpu.HBM) for v in arguments])

    def passed_on(block):
        return call(join_body, bf16(own_text, width), [block], (scalars,), 1 << 29, name="pass_on")

    text_blocks = [text_own] + [None] * (groups - 1)
    for k in [1 << i for i in reversed(range(groups.bit_length() - 1))]:
        for j in range(0, groups, 2 * k):
            came = exchanged(text_blocks[j], "group", k)
            text_blocks[j + k] = passed_on(came) if k > 1 else came
    square = chips == 4
    masks = [1, 2] if square else list(range(1, chips))

    def far_halves(near, middle, after=()):
        sizes = [middle, near[0].shape[0] - middle]
        halves = call(
            halves_body, [bf16(size, width) for size in sizes], near[::-1], after, name="halves"
        )
        return [exchanged(half, "member", 2 * k) for half, k in zip(halves, masks)]

    speech_blocks = [exchanged(speech_own, "member", 2 * k) for k in reversed(range(1, chips))]
    column = groups * own_text
    text, speech = call(
        functools.partial(join_both_body, groups),
        [bf16(column, width), bf16(chips * (rows + MARK_ROWS), width)],
        [*text_blocks, speech_own, *speech_blocks[::-1]],
        name="join_rows",
    )
    other = exchanged(speech, "member", 1)
    text_near = [exchanged(text, "member", 2 * k) for k in masks]

    temporary = 4 * column * (6 * CHUNK + 3 * width)

    def text_part(outs, blocks, start, ks=range(groups)):
        count = sum(v.shape[0] for v in blocks) // (rows + MARK_ROWS)
        body = functools.partial(text_part_body, rows, own_text, list(ks), bool(start), len(blocks))
        operands = [scalars, text, *start, *blocks]
        work = 4 * len(ks) * own_text * count * rows * width
        return call(body, outs, operands, (), work, temporary, "text_part")

    half = text_part([f32(column, width)], [speech], [])
    parts = list(text_part([f32(own_text, width)] * groups, [other], half))

    text_back = [parts[0]]
    for bit in [1 << i for i in range(groups.bit_length() - 1)]:
        for k in reversed(range(bit, groups, 2 * bit)):
            came = exchanged(parts[k], "group", bit)
            if k == bit:
                text_back.append(came)
            else:
                parts[k - bit], parts[bit] = call(
                    sum_near_body,
                    [f32(own_text, width)] * 2,
                    [parts[k - bit], came, parts[bit]],
                    name="sum_near",
                )

    def speech_part(block, start, columns, texts, after=()):
        body = functools.partial(speech_part_body, rows, own_text, bool(start), columns)
        operands = [scalars, block, *start, *texts]
        work = 40 * rows * column * len(columns) * width
        return call(body, f32(rows, width), operands, after, work, temporary, "speech_part")

    near = [[0, *masks], [text, *text_near], (parts[groups // 2],)]
    away = speech_part(other[0 : rows + MARK_ROWS], [], *near)
    home = speech_part(speech_own, [], *near)
    if square:
        text_far = far_halves(text_near, column // 2, (parts[groups // 2],))
        away = speech_part(other[0 : rows + MARK_ROWS], [away], [3], text_far)
        home = speech_part(speech_own, [home], [3], text_far)
    back = exchanged(away, "member", 1)
    text_back = call(sum_body, f32(own_text, width), text_back[::-1], (), EARLY, name="text_sum")
    speech_grad, text_grad = call(
        finish_body,
        [f32(rows, width), f32(own_text, width)],
        [audio, home, back, sentence, text_back],
        name="finish",
    )
    return (speech_grad, text_grad)


def solution(mesh):
    in_specs = (
        P(("group", "member"), None),
        P(("group", "member"), None),
        P(("group", "member")),
        P(),
        P(),
    )
    out_specs = (P(("group", "member"), None), P(("group", "member"), None))
    return jax.shard_map(shards, mesh=mesh, in_specs=in_specs, out_specs=out_specs, check_vma=False)
```

```python
import functools
import jax
import jax.numpy as jnp
from jax import lax
from jax.experimental import pallas as pl
from jax.experimental.pallas import tpu as pltpu
from jax.sharding import PartitionSpec as P

MARK_ROWS = 16
RADIX = 256
CHUNK = 512
EARLY = 1 << 33


def exchanged(value, axis, mask):
    size = lax.axis_size(axis)
    return lax.ppermute(value, axis, [(i, i ^ mask) for i in range(size)])


def total_bytes(values):
    return sum(v.size * v.dtype.itemsize for v in jax.tree.leaves(values))


def call(body, out_shape, operands, after=(), flops=0, temporary=0, name="kernel"):
    specs = [pl.BlockSpec(memory_space=pltpu.VMEM) for _ in operands]
    specs += [pl.BlockSpec(memory_space=pl.ANY) for _ in after]
    used = len(operands)

    def whole(*refs):
        body(*refs[:used], *refs[used + len(after) :])

    moved = total_bytes(operands) + total_bytes(out_shape)
    return pl.pallas_call(
        whole,
        out_shape=out_shape,
        in_specs=specs,
        out_specs=jax.tree.map(lambda _: pl.BlockSpec(memory_space=pltpu.VMEM), out_shape),
        compiler_params=pltpu.CompilerParams(vmem_limit_bytes=(4 << 20) + 2 * moved + temporary),
        cost_estimate=pl.CostEstimate(flops=flops, bytes_accessed=moved, transcendentals=0),
        name=name,
    )(*operands, *after)


def direction(values):
    floats = values.astype(jnp.float32)
    norms = jnp.sqrt(jnp.sum(floats * floats, axis=-1, keepdims=True) + 1e-06)
    return floats / norms, norms


def prepare_body(*refs):
    sources, (speech, text) = refs[:3], refs[3:5]
    held, done = refs[5:8], refs[8]
    copies = [pltpu.make_async_copy(sources[i], held[i], done.at[i]) for i in range(3)]
    for copy in copies:
        copy.start()
    for copy in copies:
        copy.wait()
    audio, sentence, label = held
    rows = audio.shape[0]
    speech[0:rows, :] = direction(audio[...])[0].astype(jnp.bfloat16)
    text[...] = direction(sentence[...])[0].astype(jnp.bfloat16)
    number = label[...]
    digits = jnp.concatenate([number % RADIX, number // RADIX], axis=1).astype(jnp.float32)
    wide = jnp.concatenate(
        [digits, jnp.zeros((1, speech.shape[1] - 2 * rows), jnp.float32)], axis=1
    )
    speech[rows : rows + MARK_ROWS, :] = jnp.broadcast_to(
        wide, (MARK_ROWS, speech.shape[1])
    ).astype(jnp.bfloat16)


def join_body(*refs):
    out = refs[-1]
    at = 0
    for ref in refs[:-1]:
        out[at : at + ref.shape[0], :] = ref[...]
        at += ref.shape[0]


def join_both_body(count, *refs):
    join_body(*refs[:count], refs[-2])
    join_body(*refs[count:-2], refs[-1])


def halves_body(upper, lower, upper_out, lower_out):
    upper_out[...] = upper[: upper_out.shape[0], :]
    lower_out[...] = lower[upper_out.shape[0] :, :]


def marks_of(block, rows):
    digits = block[rows : rows + MARK_ROWS, 0 : 2 * rows][0:1, :].astype(jnp.float32)
    return digits[:, 0:rows] + RADIX * digits[:, rows : 2 * rows]


def coefficients(dots, match, sharp, shift):
    logits = sharp * dots + shift
    probs = 1.0 / (1.0 + jnp.exp(-logits))
    return (sharp * (probs - jnp.where(match, 1.0, 0.0))).astype(jnp.bfloat16)


def dot_rows(left, right):
    return lax.dot_general(left, right, (((1,), (1,)), ((), ())), preferred_element_type=jnp.float32)


def text_part_body(rows, own_text, ks, has_start, speeches, *refs):
    sharp, shift = refs[0][0:1, 0:1], refs[0][1:2, 0:1]
    some_text = slice(ks[0] * own_text, (ks[-1] + 1) * own_text)
    text = refs[1][some_text, :]
    total = refs[2][some_text, :] if has_start else None
    at = 3 if has_start else 2
    blocks = refs[at : at + speeches]
    outs = refs[at + speeches :]
    groups = lax.axis_size("group")
    members = lax.axis_size("member")
    group = lax.axis_index("group")
    member = lax.axis_index("member")
    stride = rows + MARK_ROWS
    for speech in blocks:
        count = speech.shape[0] // stride
        for first in range(0, count, CHUNK // rows):
            some = range(first, min(count, first + CHUNK // rows))
            chunk = [speech[k * stride : k * stride + rows, :] for k in some]
            marks = [marks_of(speech.at[k * stride : (k + 1) * stride, :], rows) for k in some]
            chunk = jnp.concatenate(chunk, axis=0)
            marks = jnp.concatenate(marks, axis=1)
            iota = lax.broadcasted_iota(jnp.int32, (own_text, marks.shape[1]), 0)
            ids = [((group ^ k) * members + member) * own_text + iota for k in ks]
            match = jnp.concatenate(ids, axis=0).astype(jnp.float32) == marks
            coef = coefficients(dot_rows(text, chunk), match, sharp, shift)
            part = jnp.dot(coef, chunk, preferred_element_type=jnp.float32)
            total = part if total is None else total + part
    size = outs[0].shape[0]
    for k, out in enumerate(outs):
        out[...] = total[k * size : (k + 1) * size, :]


def speech_part_body(rows, own_text, has_start, masks, *refs):
    sharp, shift, speech = refs[0][0:1, 0:1], refs[0][1:2, 0:1], refs[1]
    total = refs[2][...] if has_start else None
    texts, out = list(refs[3 if has_start else 2 : -1]), refs[-1]
    groups = lax.axis_size("group")
    members = lax.axis_size("member")
    group = lax.axis_index("group")
    member = lax.axis_index("member")
    marks = jnp.broadcast_to(marks_of(speech, rows), (rows, rows)).T[:, 0:1]
    block = speech[0:rows, :]
    column = groups * own_text
    lane = lax.broadcasted_iota(jnp.int32, (1, column), 1)
    base = (group ^ (lane // own_text)) * members * own_text + lane % own_text
    for mask in masks:
        pieces = [texts.pop(0)[...]]
        while sum(v.shape[0] for v in pieces) < column:
            pieces.append(texts.pop(0)[...])
        text = jnp.concatenate(pieces, axis=0)
        ids = (base + (member ^ (2 * mask)) * own_text).astype(jnp.float32)
        coef = coefficients(dot_rows(block, text), marks == ids, sharp, shift)
        part = jnp.dot(coef, text, preferred_element_type=jnp.float32)
        total = part if total is None else total + part
    out[...] = total


def sum_near_body(mine, came, kept, total, kept_out):
    total[...] = mine[...] + came[...]
    kept_out[...] = kept[...]


def sum_body(*refs):
    total = refs[0][...]
    for ref in refs[1:-1]:
        total = total + ref[...]
    refs[-1][...] = total


def project(values, back, out):
    heading, norms = direction(values)
    along = jnp.sum(heading * back, axis=-1, keepdims=True)
    out[...] = (back - heading * along) / norms


def finish_body(audio, home, back, sentence, text_back, speech_grad, text_grad):
    project(sentence[...], text_back[...], text_grad)
    project(audio[...], home[...] + back[...], speech_grad)


def shards(audio_vectors, sentence_vectors, matching_indices, sharpness_array, offset_term):
    members = lax.axis_size("member")
    groups = lax.axis_size("group")
    chips = members // 2
    rows, width = audio_vectors.shape
    own_text = sentence_vectors.shape[0]
    label = matching_indices.reshape(1, rows)
    scalars = jnp.concatenate(
        [jnp.broadcast_to(v[:, None], (1, 128)) for v in (sharpness_array, offset_term)], axis=0
    )

    def bf16(*shape):
        return jax.ShapeDtypeStruct(shape, jnp.bfloat16)

    def f32(*shape):
        return jax.ShapeDtypeStruct(shape, jnp.float32)

    arguments = [audio_vectors, sentence_vectors, label]
    speech_own, text_own, audio, sentence = pl.pallas_call(
        prepare_body,
        out_shape=[
            bf16(rows + MARK_ROWS, width),
            bf16(own_text, width),
            bf16(rows, width),
            bf16(own_text, width),
        ],
        in_specs=[pl.BlockSpec(memory_space=pltpu.HBM)] * 3,
        out_specs=[pl.BlockSpec(memory_space=pltpu.VMEM)] * 4,
        scratch_shapes=[pltpu.VMEM((1, rows), jnp.int32), pltpu.SemaphoreType.DMA((3,))],
        compiler_params=pltpu.CompilerParams(vmem_limit_bytes=8 << 20),
        name="unit_rows",
    )(*[pltpu.with_memory_space_constraint(v, pltpu.HBM) for v in arguments])

    def passed_on(block):
        return call(join_body, bf16(own_text, width), [block], (scalars,), 1 << 20, name="pass_on")

    text_blocks = [text_own] + [None] * (groups - 1)
    for k in [1 << i for i in reversed(range(groups.bit_length() - 1))]:
        for j in range(0, groups, 2 * k):
            came = exchanged(text_blocks[j], "group", k)
            text_blocks[j + k] = passed_on(came) if k > 1 else came
    square = chips == 4
    masks = [1, 2] if square else list(range(1, chips))

    def far_halves(near, middle, after=()):
        sizes = [middle, near[0].shape[0] - middle]
        halves = call(
            halves_body, [bf16(size, width) for size in sizes], near[::-1], after, name="halves"
        )
        return [exchanged(half, "member", 2 * k) for half, k in zip(halves, masks)]

    speech_blocks = [exchanged(speech_own, "member", 2 * k) for k in reversed(range(1, chips))]
    column = groups * own_text
    text, speech = call(
        functools.partial(join_both_body, groups),
        [bf16(column, width), bf16(chips * (rows + MARK_ROWS), width)],
        [*text_blocks, speech_own, *speech_blocks[::-1]],
        name="join_rows",
    )
    other = exchanged(speech, "member", 1)
    text_near = [exchanged(text, "member", 2 * k) for k in masks]

    temporary = 4 * column * (6 * CHUNK + 3 * width)

    def text_part(outs, blocks, start, ks=range(groups)):
        count = sum(v.shape[0] for v in blocks) // (rows + MARK_ROWS)
        body = functools.partial(text_part_body, rows, own_text, list(ks), bool(start), len(blocks))
        operands = [scalars, text, *start, *blocks]
        work = 4 * len(ks) * own_text * count * rows * width
        return call(body, outs, operands, (), work, temporary, "text_part")

    half = text_part([f32(column, width)], [speech], [])
    parts = list(text_part([f32(own_text, width)] * groups, [other], half))

    text_back = [parts[0]]
    for bit in [1 << i for i in range(groups.bit_length() - 1)]:
        for k in reversed(range(bit, groups, 2 * bit)):
            came = exchanged(parts[k], "group", bit)
            if k == bit:
                text_back.append(came)
            else:
                parts[k - bit], parts[bit] = call(
                    sum_near_body,
                    [f32(own_text, width)] * 2,
                    [parts[k - bit], came, parts[bit]],
                    name="sum_near",
                )

    def speech_part(block, start, columns, texts, after=()):
        body = functools.partial(speech_part_body, rows, own_text, bool(start), columns)
        operands = [scalars, block, *start, *texts]
        work = 40 * rows * column * len(columns) * width
        return call(body, f32(rows, width), operands, after, work, temporary, "speech_part")

    near = [[0, *masks], [text, *text_near], (parts[groups // 2],)]
    away = speech_part(other[0 : rows + MARK_ROWS], [], *near)
    home = speech_part(speech_own, [], *near)
    if square:
        text_far = far_halves(text_near, column // 2, (parts[groups // 2],))
        away = speech_part(other[0 : rows + MARK_ROWS], [away], [3], text_far)
        home = speech_part(speech_own, [home], [3], text_far)
    back = exchanged(away, "member", 1)
    text_back = call(sum_body, f32(own_text, width), text_back[::-1], (), EARLY, name="text_sum")
    speech_grad, text_grad = call(
        finish_body,
        [f32(rows, width), f32(own_text, width)],
        [audio, home, back, sentence, text_back],
        name="finish",
    )
    return (speech_grad, text_grad)


def solution(mesh):
    in_specs = (
        P(("group", "member"), None),
        P(("group", "member"), None),
        P(("group", "member")),
        P(),
        P(),
    )
    out_specs = (P(("group", "member"), None), P(("group", "member"), None))
    return jax.shard_map(shards, mesh=mesh, in_specs=in_specs, out_specs=out_specs, check_vma=False)
```

```python
import functools
import jax
import jax.numpy as jnp
from jax import lax
from jax.experimental import pallas as pl
from jax.experimental.pallas import tpu as pltpu
from jax.sharding import PartitionSpec as P

MARK_ROWS = 16
RADIX = 256
CHUNK = 512
EARLY = 1 << 33


def exchanged(value, axis, mask):
    size = lax.axis_size(axis)
    return lax.ppermute(value, axis, [(i, i ^ mask) for i in range(size)])


def total_bytes(values):
    return sum(v.size * v.dtype.itemsize for v in jax.tree.leaves(values))


def call(body, out_shape, operands, after=(), flops=0, temporary=0, name="kernel"):
    specs = [pl.BlockSpec(memory_space=pltpu.VMEM) for _ in operands]
    specs += [pl.BlockSpec(memory_space=pl.ANY) for _ in after]
    used = len(operands)

    def whole(*refs):
        body(*refs[:used], *refs[used + len(after) :])

    moved = total_bytes(operands) + total_bytes(out_shape)
    return pl.pallas_call(
        whole,
        out_shape=out_shape,
        in_specs=specs,
        out_specs=jax.tree.map(lambda _: pl.BlockSpec(memory_space=pltpu.VMEM), out_shape),
        compiler_params=pltpu.CompilerParams(vmem_limit_bytes=(4 << 20) + 2 * moved + temporary),
        cost_estimate=pl.CostEstimate(flops=flops, bytes_accessed=moved, transcendentals=0),
        name=name,
    )(*operands, *after)


def direction(values):
    floats = values.astype(jnp.float32)
    norms = jnp.sqrt(jnp.sum(floats * floats, axis=-1, keepdims=True) + 1e-06)
    return floats / norms, norms


def prepare_body(*refs):
    sources, (speech, text) = refs[:3], refs[3:5]
    held, done = refs[5:8], refs[8]
    copies = [pltpu.make_async_copy(sources[i], held[i], done.at[i]) for i in range(3)]
    for copy in copies:
        copy.start()
    for copy in copies:
        copy.wait()
    audio, sentence, label = held
    rows = audio.shape[0]
    speech[0:rows, :] = direction(audio[...])[0].astype(jnp.bfloat16)
    text[...] = direction(sentence[...])[0].astype(jnp.bfloat16)
    number = label[...]
    digits = jnp.concatenate([number % RADIX, number // RADIX], axis=1).astype(jnp.float32)
    wide = jnp.concatenate(
        [digits, jnp.zeros((1, speech.shape[1] - 2 * rows), jnp.float32)], axis=1
    )
    speech[rows : rows + MARK_ROWS, :] = jnp.broadcast_to(
        wide, (MARK_ROWS, speech.shape[1])
    ).astype(jnp.bfloat16)


def unit_body(values, out):
    out[...] = direction(values[...])[0].astype(jnp.bfloat16)


def unit_sum_body(rows, values, out):
    out[...] = rows[...] + direction(values[...])[0].astype(jnp.bfloat16)


def join_body(*refs):
    out = refs[-1]
    at = 0
    for ref in refs[:-1]:
        out[at : at + ref.shape[0], :] = ref[...]
        at += ref.shape[0]


def join_both_body(count, *refs):
    join_body(*refs[:count], refs[-2])
    join_body(*refs[count:-2], refs[-1])


def halves_body(upper, lower, upper_out, lower_out):
    upper_out[...] = upper[: upper_out.shape[0], :]
    lower_out[...] = lower[upper_out.shape[0] :, :]


def marks_of(block, rows):
    digits = block[rows : rows + MARK_ROWS, 0 : 2 * rows][0:1, :].astype(jnp.float32)
    return digits[:, 0:rows] + RADIX * digits[:, rows : 2 * rows]


def coefficients(dots, match, sharp, shift):
    logits = sharp * dots + shift
    probs = 1.0 / (1.0 + jnp.exp(-logits))
    return (sharp * (probs - jnp.where(match, 1.0, 0.0))).astype(jnp.bfloat16)


def dot_rows(left, right):
    return lax.dot_general(left, right, (((1,), (1,)), ((), ())), preferred_element_type=jnp.float32)


def text_part_body(rows, own_text, ks, has_start, speeches, *refs):
    sharp, shift = refs[0][0:1, 0:1], refs[0][1:2, 0:1]
    some_text = slice(ks[0] * own_text, (ks[-1] + 1) * own_text)
    text = refs[1][some_text, :]
    total = refs[2][some_text, :] if has_start else None
    at = 3 if has_start else 2
    blocks = refs[at : at + speeches]
    outs = refs[at + speeches :]
    groups = lax.axis_size("group")
    members = lax.axis_size("member")
    group = lax.axis_index("group")
    member = lax.axis_index("member")
    stride = rows + MARK_ROWS
    for speech in blocks:
        count = speech.shape[0] // stride
        for first in range(0, count, CHUNK // rows):
            some = range(first, min(count, first + CHUNK // rows))
            chunk = [speech[k * stride : k * stride + rows, :] for k in some]
            marks = [marks_of(speech.at[k * stride : (k + 1) * stride, :], rows) for k in some]
            chunk = jnp.concatenate(chunk, axis=0)
            marks = jnp.concatenate(marks, axis=1)
            iota = lax.broadcasted_iota(jnp.int32, (own_text, marks.shape[1]), 0)
            ids = [((group ^ k) * members + member) * own_text + iota for k in ks]
            match = jnp.concatenate(ids, axis=0).astype(jnp.float32) == marks
            coef = coefficients(dot_rows(text, chunk), match, sharp, shift)
            part = jnp.dot(coef, chunk, preferred_element_type=jnp.float32)
            total = part if total is None else total + part
    size = outs[0].shape[0]
    for k, out in enumerate(outs):
        out[...] = total[k * size : (k + 1) * size, :]


def speech_part_body(rows, own_text, has_start, masks, *refs):
    sharp, shift, speech = refs[0][0:1, 0:1], refs[0][1:2, 0:1], refs[1]
    total = refs[2][...] if has_start else None
    texts, out = list(refs[3 if has_start else 2 : -1]), refs[-1]
    groups = lax.axis_size("group")
    members = lax.axis_size("member")
    group = lax.axis_index("group")
    member = lax.axis_index("member")
    marks = jnp.broadcast_to(marks_of(speech, rows), (rows, rows)).T[:, 0:1]
    block = speech[0:rows, :]
    column = groups * own_text
    lane = lax.broadcasted_iota(jnp.int32, (1, column), 1)
    base = (group ^ (lane // own_text)) * members * own_text + lane % own_text
    for mask in masks:
        pieces = [texts.pop(0)[...]]
        while sum(v.shape[0] for v in pieces) < column:
            pieces.append(texts.pop(0)[...])
        text = jnp.concatenate(pieces, axis=0)
        ids = (base + (member ^ (2 * mask)) * own_text).astype(jnp.float32)
        coef = coefficients(dot_rows(block, text), marks == ids, sharp, shift)
        part = jnp.dot(coef, text, preferred_element_type=jnp.float32)
        total = part if total is None else total + part
    out[...] = total


def sum_near_body(mine, came, kept, total, kept_out):
    total[...] = mine[...] + came[...]
    kept_out[...] = kept[...]


def sum_body(*refs):
    total = refs[0][...]
    for ref in refs[1:-1]:
        total = total + ref[...]
    refs[-1][...] = total


def project(values, back, out):
    heading, norms = direction(values)
    along = jnp.sum(heading * back, axis=-1, keepdims=True)
    out[...] = (back - heading * along) / norms


def finish_body(audio, home, back, sentence, text_back, speech_grad, text_grad):
    project(sentence[...], text_back[...], text_grad)
    project(audio[...], home[...] + back[...], speech_grad)


def shards(audio_vectors, sentence_vectors, matching_indices, sharpness_array, offset_term):
    members = lax.axis_size("member")
    groups = lax.axis_size("group")
    chips = members // 2
    rows, width = audio_vectors.shape
    own_text = sentence_vectors.shape[0]
    label = matching_indices.reshape(1, rows)
    scalars = jnp.concatenate(
        [jnp.broadcast_to(v[:, None], (1, 128)) for v in (sharpness_array, offset_term)], axis=0
    )

    def bf16(*shape):
        return jax.ShapeDtypeStruct(shape, jnp.bfloat16)

    def f32(*shape):
        return jax.ShapeDtypeStruct(shape, jnp.float32)

    arguments = [audio_vectors, sentence_vectors, label]
    speech_own, text_own, audio, sentence = pl.pallas_call(
        prepare_body,
        out_shape=[
            bf16(rows + MARK_ROWS, width),
            bf16(own_text, width),
            bf16(rows, width),
            bf16(own_text, width),
        ],
        in_specs=[pl.BlockSpec(memory_space=pltpu.HBM)] * 3,
        out_specs=[pl.BlockSpec(memory_space=pltpu.VMEM)] * 4,
        scratch_shapes=[pltpu.VMEM((1, rows), jnp.int32), pltpu.SemaphoreType.DMA((3,))],
        compiler_params=pltpu.CompilerParams(vmem_limit_bytes=8 << 20),
        name="unit_rows",
    )(*[pltpu.with_memory_space_constraint(v, pltpu.HBM) for v in arguments])

    text_blocks = [text_own] + [None] * (groups - 1)
    far = groups // 2
    up = lax.ppermute(sentence_vectors, "group", [(i, i - far) for i in range(far, groups)])
    down = lax.ppermute(sentence_vectors, "group", [(i, i + far) for i in range(far)])
    shape = bf16(own_text, width)
    up = call(unit_body, shape, [up], (), EARLY, name="unit_far")
    text_blocks[far] = call(unit_sum_body, shape, [up, down], (scalars,), 1 << 20, name="pass_on")
    for k in [1 << i for i in reversed(range(groups.bit_length() - 2))]:
        for j in range(0, groups, 2 * k):
            text_blocks[j + k] = exchanged(text_blocks[j], "group", k)
    square = chips == 4
    masks = [1, 2] if square else list(range(1, chips))

    def far_halves(near, middle, after=()):
        sizes = [middle, near[0].shape[0] - middle]
        halves = call(
            halves_body, [bf16(size, width) for size in sizes], near[::-1], after, name="halves"
        )
        return [exchanged(half, "member", 2 * k) for half, k in zip(halves, masks)]

    speech_blocks = [exchanged(speech_own, "member", 2 * k) for k in reversed(range(1, chips))]
    column = groups * own_text
    text, speech = call(
        functools.partial(join_both_body, groups),
        [bf16(column, width), bf16(chips * (rows + MARK_ROWS), width)],
        [*text_blocks, speech_own, *speech_blocks[::-1]],
        name="join_rows",
    )
    other = exchanged(speech, "member", 1)
    text_near = [exchanged(text, "member", 2 * k) for k in masks]

    temporary = 4 * column * (6 * CHUNK + 3 * width)

    def text_part(outs, blocks, start, ks=range(groups)):
        count = sum(v.shape[0] for v in blocks) // (rows + MARK_ROWS)
        body = functools.partial(text_part_body, rows, own_text, list(ks), bool(start), len(blocks))
        operands = [scalars, text, *start, *blocks]
        work = 4 * len(ks) * own_text * count * rows * width
        return call(body, outs, operands, (), work, temporary, "text_part")

    half = text_part([f32(column, width)], [speech], [])
    parts = list(text_part([f32(own_text, width)] * groups, [other], half))

    text_back = [parts[0]]
    for bit in [1 << i for i in range(groups.bit_length() - 1)]:
        for k in reversed(range(bit, groups, 2 * bit)):
            came = exchanged(parts[k], "group", bit)
            if k == bit:
                text_back.append(came)
            else:
                parts[k - bit], parts[bit] = call(
                    sum_near_body,
                    [f32(own_text, width)] * 2,
                    [parts[k - bit], came, parts[bit]],
                    name="sum_near",
                )

    def speech_part(block, start, columns, texts, after=()):
        body = functools.partial(speech_part_body, rows, own_text, bool(start), columns)
        operands = [scalars, block, *start, *texts]
        work = 40 * rows * column * len(columns) * width
        return call(body, f32(rows, width), operands, after, work, temporary, "speech_part")

    near = [[0, *masks], [text, *text_near], (parts[groups // 2],)]
    away = speech_part(other[0 : rows + MARK_ROWS], [], *near)
    home = speech_part(speech_own, [], *near)
    if square:
        text_far = far_halves(text_near, column // 2, (parts[groups // 2],))
        away = speech_part(other[0 : rows + MARK_ROWS], [away], [3], text_far)
        home = speech_part(speech_own, [home], [3], text_far)
    back = exchanged(away, "member", 1)
    text_back = call(sum_body, f32(own_text, width), text_back[::-1], (), EARLY, name="text_sum")
    speech_grad, text_grad = call(
        finish_body,
        [f32(rows, width), f32(own_text, width)],
        [audio, home, back, sentence, text_back],
        name="finish",
    )
    return (speech_grad, text_grad)


def solution(mesh):
    in_specs = (
        P(("group", "member"), None),
        P(("group", "member"), None),
        P(("group", "member")),
        P(),
        P(),
    )
    out_specs = (P(("group", "member"), None), P(("group", "member"), None))
    return jax.shard_map(shards, mesh=mesh, in_specs=in_specs, out_specs=out_specs, check_vma=False)
```

```python
import functools
import jax
import jax.numpy as jnp
from jax import lax
from jax.experimental import pallas as pl
from jax.experimental.pallas import tpu as pltpu
from jax.sharding import PartitionSpec as P

MARK_ROWS = 16
RADIX = 256
CHUNK = 512
EARLY = 1 << 33


def exchanged(value, axis, mask):
    size = lax.axis_size(axis)
    return lax.ppermute(value, axis, [(i, i ^ mask) for i in range(size)])


def total_bytes(values):
    return sum(v.size * v.dtype.itemsize for v in jax.tree.leaves(values))


def call(body, out_shape, operands, after=(), flops=0, temporary=0, name="kernel"):
    specs = [pl.BlockSpec(memory_space=pltpu.VMEM) for _ in operands]
    specs += [pl.BlockSpec(memory_space=pl.ANY) for _ in after]
    used = len(operands)

    def whole(*refs):
        body(*refs[:used], *refs[used + len(after) :])

    moved = total_bytes(operands) + total_bytes(out_shape)
    return pl.pallas_call(
        whole,
        out_shape=out_shape,
        in_specs=specs,
        out_specs=jax.tree.map(lambda _: pl.BlockSpec(memory_space=pltpu.VMEM), out_shape),
        compiler_params=pltpu.CompilerParams(vmem_limit_bytes=(4 << 20) + 2 * moved + temporary),
        cost_estimate=pl.CostEstimate(flops=flops, bytes_accessed=moved, transcendentals=0),
        name=name,
    )(*operands, *after)


def direction(values):
    floats = values.astype(jnp.float32)
    norms = jnp.sqrt(jnp.sum(floats * floats, axis=-1, keepdims=True) + 1e-06)
    return floats / norms, norms


def prepare_body(*refs):
    sources, (speech, text) = refs[:3], refs[3:5]
    held, done = refs[5:8], refs[8]
    copies = [pltpu.make_async_copy(sources[i], held[i], done.at[i]) for i in range(3)]
    for copy in copies:
        copy.start()
    for copy in copies:
        copy.wait()
    audio, sentence, label = held
    rows = audio.shape[0]
    speech[0:rows, :] = direction(audio[...])[0].astype(jnp.bfloat16)
    text[...] = direction(sentence[...])[0].astype(jnp.bfloat16)
    number = label[...]
    digits = jnp.concatenate([number % RADIX, number // RADIX], axis=1).astype(jnp.float32)
    wide = jnp.concatenate(
        [digits, jnp.zeros((1, speech.shape[1] - 2 * rows), jnp.float32)], axis=1
    )
    speech[rows : rows + MARK_ROWS, :] = jnp.broadcast_to(
        wide, (MARK_ROWS, speech.shape[1])
    ).astype(jnp.bfloat16)


def join_body(*refs):
    out = refs[-1]
    at = 0
    for ref in refs[:-1]:
        out[at : at + ref.shape[0], :] = ref[...]
        at += ref.shape[0]


def joined(blocks, after=(), name="join"):
    shape = (sum(v.shape[0] for v in blocks), blocks[0].shape[1])
    return call(join_body, jax.ShapeDtypeStruct(shape, blocks[0].dtype), blocks, after, name=name)


def halves_body(upper, lower, kept, upper_out, lower_out, kept_out):
    upper_out[...] = upper[: upper_out.shape[0], :]
    lower_out[...] = lower[upper_out.shape[0] :, :]
    kept_out[...] = kept[...]


def marks_of(block, rows):
    digits = block[rows : rows + MARK_ROWS, 0 : 2 * rows][0:1, :].astype(jnp.float32)
    return digits[:, 0:rows] + RADIX * digits[:, rows : 2 * rows]


def coefficients(dots, match, sharp, shift):
    logits = sharp * dots + shift
    probs = 1.0 / (1.0 + jnp.exp(-logits))
    return (sharp * (probs - jnp.where(match, 1.0, 0.0))).astype(jnp.bfloat16)


def dot_rows(left, right):
    return lax.dot_general(left, right, (((1,), (1,)), ((), ())), preferred_element_type=jnp.float32)


def text_part_body(rows, own_text, ks, has_start, speeches, *refs):
    sharp, shift = refs[0][0:1, 0:1], refs[0][1:2, 0:1]
    some_text = slice(ks[0] * own_text, (ks[-1] + 1) * own_text)
    text = refs[1][some_text, :]
    total = refs[2][some_text, :] if has_start else None
    at = 3 if has_start else 2
    blocks = refs[at : at + speeches]
    outs = refs[at + speeches :]
    groups = lax.axis_size("group")
    members = lax.axis_size("member")
    group = lax.axis_index("group")
    member = lax.axis_index("member")
    stride = rows + MARK_ROWS
    for speech in blocks:
        count = speech.shape[0] // stride
        for first in range(0, count, CHUNK // rows):
            some = range(first, min(count, first + CHUNK // rows))
            chunk = [speech[k * stride : k * stride + rows, :] for k in some]
            marks = [marks_of(speech.at[k * stride : (k + 1) * stride, :], rows) for k in some]
            chunk = jnp.concatenate(chunk, axis=0)
            marks = jnp.concatenate(marks, axis=1)
            iota = lax.broadcasted_iota(jnp.int32, (own_text, marks.shape[1]), 0)
            ids = [((group ^ k) * members + member) * own_text + iota for k in ks]
            match = jnp.concatenate(ids, axis=0).astype(jnp.float32) == marks
            coef = coefficients(dot_rows(text, chunk), match, sharp, shift)
            part = jnp.dot(coef, chunk, preferred_element_type=jnp.float32)
            total = part if total is None else total + part
    row, at = 0, 0
    for out in outs:
        out[...] = total[row : row + out.shape[0], at : at + out.shape[1]]
        at += out.shape[1]
        if at == total.shape[1]:
            row, at = row + out.shape[0], 0


def speech_part_body(rows, own_text, has_start, masks, *refs):
    sharp, shift, speech = refs[0][0:1, 0:1], refs[0][1:2, 0:1], refs[1]
    total = refs[2][...] if has_start else None
    texts, out = list(refs[3 if has_start else 2 : -1]), refs[-1]
    groups = lax.axis_size("group")
    members = lax.axis_size("member")
    group = lax.axis_index("group")
    member = lax.axis_index("member")
    marks = jnp.broadcast_to(marks_of(speech, rows), (rows, rows)).T[:, 0:1]
    block = speech[0:rows, :]
    column = groups * own_text
    lane = lax.broadcasted_iota(jnp.int32, (1, column), 1)
    base = (group ^ (lane // own_text)) * members * own_text + lane % own_text
    for mask in masks:
        pieces = [texts.pop(0)[...]]
        while sum(v.shape[0] for v in pieces) < column:
            pieces.append(texts.pop(0)[...])
        text = jnp.concatenate(pieces, axis=0)
        ids = (base + (member ^ (2 * mask)) * own_text).astype(jnp.float32)
        coef = coefficients(dot_rows(block, text), marks == ids, sharp, shift)
        part = jnp.dot(coef, text, preferred_element_type=jnp.float32)
        total = part if total is None else total + part
    out[...] = total


def add_sides_body(mine, *refs):
    out = refs[-1]
    at = 0
    for side in refs[:-1]:
        columns = slice(at, at + side.shape[1])
        out[:, columns] = mine[:, columns] + side[...]
        at += side.shape[1]


def sum_body(*refs):
    total = refs[0][...]
    for ref in refs[1:-1]:
        total = total + ref[...]
    refs[-1][...] = total


def project(values, back, out):
    heading, norms = direction(values)
    along = jnp.sum(heading * back, axis=-1, keepdims=True)
    out[...] = (back - heading * along) / norms


def finish_body(audio, home, back, sentence, *refs):
    parts, (speech_grad, text_grad) = refs[:-2], refs[-2:]
    text_back = parts[0][...]
    for part in parts[1:]:
        text_back = text_back + part[...]
    project(sentence[...], text_back, text_grad)
    project(audio[...], home[...] + back[...], speech_grad)


def shards(audio_vectors, sentence_vectors, matching_indices, sharpness_array, offset_term):
    members = lax.axis_size("member")
    groups = lax.axis_size("group")
    chips = members // 2
    rows, width = audio_vectors.shape
    own_text = sentence_vectors.shape[0]
    label = matching_indices.reshape(1, rows)
    scalars = jnp.concatenate(
        [jnp.broadcast_to(v[:, None], (1, 128)) for v in (sharpness_array, offset_term)], axis=0
    )

    def bf16(*shape):
        return jax.ShapeDtypeStruct(shape, jnp.bfloat16)

    def f32(*shape):
        return jax.ShapeDtypeStruct(shape, jnp.float32)

    arguments = [audio_vectors, sentence_vectors, label]
    speech_own, text_own, audio, sentence = pl.pallas_call(
        prepare_body,
        out_shape=[
            bf16(rows + MARK_ROWS, width),
            bf16(own_text, width),
            bf16(rows, width),
            bf16(own_text, width),
        ],
        in_specs=[pl.BlockSpec(memory_space=pltpu.HBM)] * 3,
        out_specs=[pl.BlockSpec(memory_space=pltpu.VMEM)] * 4,
        scratch_shapes=[pltpu.VMEM((1, rows), jnp.int32), pltpu.SemaphoreType.DMA((3,))],
        compiler_params=pltpu.CompilerParams(vmem_limit_bytes=8 << 20),
        name="unit_rows",
    )(*[pltpu.with_memory_space_constraint(v, pltpu.HBM) for v in arguments])

    def passed_on(block):
        return call(join_body, bf16(own_text, width), [block], (scalars,), 1 << 31, name="pass_on")

    text_blocks = [text_own] + [None] * (groups - 1)
    for k in [1 << i for i in reversed(range(groups.bit_length() - 1))]:
        for j in range(0, groups, 2 * k):
            came = exchanged(text_blocks[j], "group", k)
            text_blocks[j + k] = passed_on(came) if k > 1 else came
    square = chips == 4
    masks = [1, 2] if square else list(range(1, chips))

    speech_blocks = [exchanged(speech_own, "member", 2 * k) for k in reversed(range(1, chips))]
    column = groups * own_text
    if square:
        speech = [speech_own, *speech_blocks]
    else:
        speech = [joined([speech_own, *speech_blocks], name="join_speech")]
    other = [exchanged(block, "member", 1) for block in speech]
    text = joined(text_blocks, tuple(other[:1]) if square else (), name="join_text")
    text_near = [exchanged(text, "member", 2 * k) for k in masks]

    temporary = 4 * column * (6 * CHUNK + 3 * width)

    def text_part(outs, blocks, start, ks=range(groups)):
        count = sum(v.shape[0] for v in blocks) // (rows + MARK_ROWS)
        body = functools.partial(text_part_body, rows, own_text, list(ks), bool(start), len(blocks))
        operands = [scalars, text, *start, *blocks]
        work = 4 * len(ks) * own_text * count * rows * width
        return call(body, outs, operands, (), work, temporary, "text_part")

    half = text_part([f32(column, width)], speech, [])
    sides = 2
    side = f32(own_text, width // sides)
    outs = [f32(own_text, width)] * (groups // 2) + [side] * (groups // 2 * sides)
    parts = list(text_part(outs, other, half))
    far = [parts[groups // 2 + i * sides :][:sides] for i in range(groups // 2)]

    bit = 1
    while bit < groups // 2:
        for k in reversed(range(bit, groups // 2, 2 * bit)):
            came = [exchanged(v, "group", bit) for v in far[k]]
            far[k - bit] = [
                call(sum_body, side, [mine, v], name="sum_near") for mine, v in zip(far[k - bit], came)
            ]
        bit *= 2
    from_far = [exchanged(v, "group", groups // 2) for v in far[0]]
    def speech_part(block, start, columns, texts, after=()):
        body = functools.partial(speech_part_body, rows, own_text, bool(start), columns)
        operands = [scalars, block, *start, *texts]
        work = 40 * rows * column * len(columns) * width
        return call(body, f32(rows, width), operands, after, work, temporary, "speech_part")

    near = [[0, *masks], [text, *text_near], tuple(far[0])]
    away = speech_part(other[0][0 : rows + MARK_ROWS], [], *near)
    home = speech_part(speech_own, [], *near)
    if square:
        *sent, parts[1] = call(
            halves_body,
            [bf16(column // 2, width)] * 2 + [f32(own_text, width)],
            [*text_near[::-1], parts[1]],
            tuple(far[0]),
            name="halves",
        )
        text_far = [exchanged(half, "member", 2 * k) for half, k in zip(sent, masks)]
        away = speech_part(other[0][0 : rows + MARK_ROWS], [away], [3], text_far)
        home = speech_part(speech_own, [home], [3], text_far)
    back = exchanged(away, "member", 1)
    from_near = [exchanged(parts[k], "group", k) for k in range(1, groups // 2)]
    text_back = call(
        add_sides_body, f32(own_text, width), [parts[0], *from_far], (), EARLY, name="text_sum"
    )
    speech_grad, text_grad = call(
        finish_body,
        [f32(rows, width), f32(own_text, width)],
        [audio, home, back, sentence, text_back, *from_near],
        name="finish",
    )
    return (speech_grad, text_grad)


def solution(mesh):
    in_specs = (
        P(("group", "member"), None),
        P(("group", "member"), None),
        P(("group", "member")),
        P(),
        P(),
    )
    out_specs = (P(("group", "member"), None), P(("group", "member"), None))
    return jax.shard_map(shards, mesh=mesh, in_specs=in_specs, out_specs=out_specs, check_vma=False)
```

```python
import functools
import jax
import jax.numpy as jnp
from jax import lax
from jax.experimental import pallas as pl
from jax.experimental.pallas import tpu as pltpu
from jax.sharding import PartitionSpec as P

MARK_ROWS = 16
RADIX = 256
CHUNK = 512
EARLY = 1 << 33


def exchanged(value, axis, mask):
    size = lax.axis_size(axis)
    return lax.ppermute(value, axis, [(i, i ^ mask) for i in range(size)])


def total_bytes(values):
    return sum(v.size * v.dtype.itemsize for v in jax.tree.leaves(values))


def call(body, out_shape, operands, after=(), flops=0, temporary=0, name="kernel"):
    specs = [pl.BlockSpec(memory_space=pltpu.VMEM) for _ in operands]
    specs += [pl.BlockSpec(memory_space=pl.ANY) for _ in after]
    used = len(operands)

    def whole(*refs):
        body(*refs[:used], *refs[used + len(after) :])

    moved = total_bytes(operands) + total_bytes(out_shape)
    return pl.pallas_call(
        whole,
        out_shape=out_shape,
        in_specs=specs,
        out_specs=jax.tree.map(lambda _: pl.BlockSpec(memory_space=pltpu.VMEM), out_shape),
        compiler_params=pltpu.CompilerParams(vmem_limit_bytes=(4 << 20) + 2 * moved + temporary),
        cost_estimate=pl.CostEstimate(flops=flops, bytes_accessed=moved, transcendentals=0),
        name=name,
    )(*operands, *after)


def direction(values):
    floats = values.astype(jnp.float32)
    norms = jnp.sqrt(jnp.sum(floats * floats, axis=-1, keepdims=True) + 1e-06)
    return floats / norms, norms


def prepare_body(*refs):
    sources, (speech, text) = refs[:3], refs[3:5]
    held, done = refs[5:8], refs[8]
    copies = [pltpu.make_async_copy(sources[i], held[i], done.at[i]) for i in range(3)]
    for copy in copies:
        copy.start()
    for copy in copies:
        copy.wait()
    audio, sentence, label = held
    rows = audio.shape[0]
    speech[0:rows, :] = direction(audio[...])[0].astype(jnp.bfloat16)
    text[...] = direction(sentence[...])[0].astype(jnp.bfloat16)
    number = label[...]
    digits = jnp.concatenate([number % RADIX, number // RADIX], axis=1).astype(jnp.float32)
    wide = jnp.concatenate(
        [digits, jnp.zeros((1, speech.shape[1] - 2 * rows), jnp.float32)], axis=1
    )
    speech[rows : rows + MARK_ROWS, :] = jnp.broadcast_to(
        wide, (MARK_ROWS, speech.shape[1])
    ).astype(jnp.bfloat16)


def join_body(*refs):
    out = refs[-1]
    at = 0
    for ref in refs[:-1]:
        out[at : at + ref.shape[0], :] = ref[...]
        at += ref.shape[0]


def join_both_body(count, *refs):
    join_body(*refs[:count], refs[-2])
    join_body(*refs[count:-2], refs[-1])


def halves_body(upper, lower, upper_out, lower_out):
    upper_out[...] = upper[: upper_out.shape[0], :]
    lower_out[...] = lower[upper_out.shape[0] :, :]


def marks_of(block, rows):
    digits = block[rows : rows + MARK_ROWS, 0 : 2 * rows][0:1, :].astype(jnp.float32)
    return digits[:, 0:rows] + RADIX * digits[:, rows : 2 * rows]


def coefficients(dots, match, sharp, shift):
    logits = sharp * dots + shift
    probs = 1.0 / (1.0 + jnp.exp(-logits))
    return (sharp * (probs - jnp.where(match, 1.0, 0.0))).astype(jnp.bfloat16)


def dot_rows(left, right):
    return lax.dot_general(left, right, (((1,), (1,)), ((), ())), preferred_element_type=jnp.float32)


def text_part_body(rows, own_text, ks, has_start, speeches, *refs):
    sharp, shift = refs[0][0:1, 0:1], refs[0][1:2, 0:1]
    some_text = slice(ks[0] * own_text, (ks[-1] + 1) * own_text)
    text = refs[1][some_text, :]
    total = refs[2][some_text, :] if has_start else None
    at = 3 if has_start else 2
    blocks = refs[at : at + speeches]
    outs = refs[at + speeches :]
    groups = lax.axis_size("group")
    members = lax.axis_size("member")
    group = lax.axis_index("group")
    member = lax.axis_index("member")
    stride = rows + MARK_ROWS
    for speech in blocks:
        count = speech.shape[0] // stride
        for first in range(0, count, CHUNK // rows):
            some = range(first, min(count, first + CHUNK // rows))
            chunk = [speech[k * stride : k * stride + rows, :] for k in some]
            marks = [marks_of(speech.at[k * stride : (k + 1) * stride, :], rows) for k in some]
            chunk = jnp.concatenate(chunk, axis=0)
            marks = jnp.concatenate(marks, axis=1)
            iota = lax.broadcasted_iota(jnp.int32, (own_text, marks.shape[1]), 0)
            ids = [((group ^ k) * members + member) * own_text + iota for k in ks]
            match = jnp.concatenate(ids, axis=0).astype(jnp.float32) == marks
            coef = coefficients(dot_rows(text, chunk), match, sharp, shift)
            part = jnp.dot(coef, chunk, preferred_element_type=jnp.float32)
            total = part if total is None else total + part
    row, at = 0, 0
    for out in outs:
        out[...] = total[row : row + out.shape[0], at : at + out.shape[1]]
        at += out.shape[1]
        if at == total.shape[1]:
            row, at = row + out.shape[0], 0


def speech_part_body(rows, own_text, has_start, masks, *refs):
    sharp, shift, speech = refs[0][0:1, 0:1], refs[0][1:2, 0:1], refs[1]
    total = refs[2][...] if has_start else None
    texts, out = list(refs[3 if has_start else 2 : -1]), refs[-1]
    groups = lax.axis_size("group")
    members = lax.axis_size("member")
    group = lax.axis_index("group")
    member = lax.axis_index("member")
    marks = jnp.broadcast_to(marks_of(speech, rows), (rows, rows)).T[:, 0:1]
    block = speech[0:rows, :]
    column = groups * own_text
    lane = lax.broadcasted_iota(jnp.int32, (1, column), 1)
    base = (group ^ (lane // own_text)) * members * own_text + lane % own_text
    for mask in masks:
        pieces = [texts.pop(0)[...]]
        while sum(v.shape[0] for v in pieces) < column:
            pieces.append(texts.pop(0)[...])
        text = jnp.concatenate(pieces, axis=0)
        ids = (base + (member ^ (2 * mask)) * own_text).astype(jnp.float32)
        coef = coefficients(dot_rows(block, text), marks == ids, sharp, shift)
        part = jnp.dot(coef, text, preferred_element_type=jnp.float32)
        total = part if total is None else total + part
    out[...] = total


def sum_keep_body(mine, came, kept, total, kept_out):
    total[...] = mine[...] + came[...]
    kept_out[...] = kept[...]


def add_sides_body(*refs):
    out = refs[-1]
    sides = [ref for ref in refs[:-1] if ref.shape != out.shape]
    whole = [ref for ref in refs[:-1] if ref.shape == out.shape]
    at = 0
    for ref in sides:
        columns = slice(at, at + ref.shape[1])
        total = ref[...]
        for other in whole:
            total = total + other[:, columns]
        out[:, columns] = total
        at += ref.shape[1]


def sum_body(*refs):
    total = refs[0][...]
    for ref in refs[1:-1]:
        total = total + ref[...]
    refs[-1][...] = total


def project(values, back, out):
    heading, norms = direction(values)
    along = jnp.sum(heading * back, axis=-1, keepdims=True)
    out[...] = (back - heading * along) / norms


def finish_body(audio, home, back, sentence, text_back, speech_grad, text_grad):
    project(sentence[...], text_back[...], text_grad)
    project(audio[...], home[...] + back[...], speech_grad)


def shards(audio_vectors, sentence_vectors, matching_indices, sharpness_array, offset_term):
    members = lax.axis_size("member")
    groups = lax.axis_size("group")
    chips = members // 2
    rows, width = audio_vectors.shape
    own_text = sentence_vectors.shape[0]
    label = matching_indices.reshape(1, rows)
    scalars = jnp.concatenate(
        [jnp.broadcast_to(v[:, None], (1, 128)) for v in (sharpness_array, offset_term)], axis=0
    )

    def bf16(*shape):
        return jax.ShapeDtypeStruct(shape, jnp.bfloat16)

    def f32(*shape):
        return jax.ShapeDtypeStruct(shape, jnp.float32)

    arguments = [audio_vectors, sentence_vectors, label]
    speech_own, text_own, audio, sentence = pl.pallas_call(
        prepare_body,
        out_shape=[
            bf16(rows + MARK_ROWS, width),
            bf16(own_text, width),
            bf16(rows, width),
            bf16(own_text, width),
        ],
        in_specs=[pl.BlockSpec(memory_space=pltpu.HBM)] * 3,
        out_specs=[pl.BlockSpec(memory_space=pltpu.VMEM)] * 4,
        scratch_shapes=[pltpu.VMEM((1, rows), jnp.int32), pltpu.SemaphoreType.DMA((3,))],
        compiler_params=pltpu.CompilerParams(vmem_limit_bytes=8 << 20),
        name="unit_rows",
    )(*[pltpu.with_memory_space_constraint(v, pltpu.HBM) for v in arguments])

    def passed_on(block):
        return call(join_body, bf16(own_text, width), [block], (scalars,), 1 << 29, name="pass_on")

    text_blocks = [text_own] + [None] * (groups - 1)
    for k in [1 << i for i in reversed(range(groups.bit_length() - 1))]:
        for j in range(0, groups, 2 * k):
            came = exchanged(text_blocks[j], "group", k)
            text_blocks[j + k] = passed_on(came) if k > 1 else came
    square = chips == 4
    masks = [1, 2] if square else list(range(1, chips))

    def far_halves(near, middle, after=()):
        sizes = [middle, near[0].shape[0] - middle]
        halves = call(
            halves_body, [bf16(size, width) for size in sizes], near[::-1], after, name="halves"
        )
        return [exchanged(half, "member", 2 * k) for half, k in zip(halves, masks)]

    speech_blocks = [exchanged(speech_own, "member", 2 * k) for k in reversed(range(1, chips))]
    column = groups * own_text
    text, speech = call(
        functools.partial(join_both_body, groups),
        [bf16(column, width), bf16(chips * (rows + MARK_ROWS), width)],
        [*text_blocks, speech_own, *speech_blocks[::-1]],
        name="join_rows",
    )
    other = exchanged(speech, "member", 1)
    text_near = [exchanged(text, "member", 2 * k) for k in masks]

    temporary = 4 * column * (6 * CHUNK + 3 * width)

    def text_part(outs, blocks, start, ks=range(groups)):
        count = sum(v.shape[0] for v in blocks) // (rows + MARK_ROWS)
        body = functools.partial(text_part_body, rows, own_text, list(ks), bool(start), len(blocks))
        operands = [scalars, text, *start, *blocks]
        work = 4 * len(ks) * own_text * count * rows * width
        return call(body, outs, operands, (), work, temporary, "text_part")

    half = text_part([f32(column, width)], [speech], [])
    sides = 2
    side = f32(own_text, width // sides)
    outs = [f32(own_text, width)] * (groups // 2) + [side] * (groups // 2 * sides)
    parts = list(text_part(outs, [other], half))
    far = [parts[groups // 2 + i * sides :][:sides] for i in range(groups // 2)]

    bit = 1
    while bit < groups // 2:
        for k in reversed(range(bit, groups // 2, 2 * bit)):
            came = [exchanged(v, "group", bit) for v in far[k]]
            mine = far[k - bit]
            first, parts[bit] = call(
                sum_keep_body,
                [side, f32(own_text, width)],
                [mine[0], came[0], parts[bit]],
                name="sum_near",
            )
            last = call(sum_body, side, [mine[1], came[1]], name="sum_near")
            far[k - bit] = [first, last]
        bit *= 2
    from_far = [exchanged(v, "group", groups // 2) for v in far[0]]
    from_near = [exchanged(parts[k], "group", k) for k in range(1, groups // 2)]

    def speech_part(block, start, columns, texts, after=()):
        body = functools.partial(speech_part_body, rows, own_text, bool(start), columns)
        operands = [scalars, block, *start, *texts]
        work = 40 * rows * column * len(columns) * width
        return call(body, f32(rows, width), operands, after, work, temporary, "speech_part")

    near = [[0, *masks], [text, *text_near], tuple(far[0])]
    away = speech_part(other[0 : rows + MARK_ROWS], [], *near)
    home = speech_part(speech_own, [], *near)
    if square:
        text_far = far_halves(text_near, column // 2, tuple(far[0]))
        away = speech_part(other[0 : rows + MARK_ROWS], [away], [3], text_far)
        home = speech_part(speech_own, [home], [3], text_far)
    back = exchanged(away, "member", 1)
    text_back = call(
        add_sides_body,
        f32(own_text, width),
        [*from_far, *from_near, parts[0]],
        (),
        EARLY,
        name="text_sum",
    )
    speech_grad, text_grad = call(
        finish_body,
        [f32(rows, width), f32(own_text, width)],
        [audio, home, back, sentence, text_back],
        name="finish",
    )
    return (speech_grad, text_grad)


def solution(mesh):
    in_specs = (
        P(("group", "member"), None),
        P(("group", "member"), None),
        P(("group", "member")),
        P(),
        P(),
    )
    out_specs = (P(("group", "member"), None), P(("group", "member"), None))
    return jax.shard_map(shards, mesh=mesh, in_specs=in_specs, out_specs=out_specs, check_vma=False)
```

```python
import functools
import jax
import jax.numpy as jnp
from jax import lax
from jax.experimental import pallas as pl
from jax.experimental.pallas import tpu as pltpu
from jax.sharding import PartitionSpec as P

MARK_ROWS = 16
RADIX = 256
CHUNK = 512
EARLY = 1 << 33


def exchanged(value, axis, mask):
    size = lax.axis_size(axis)
    return lax.ppermute(value, axis, [(i, i ^ mask) for i in range(size)])


def total_bytes(values):
    return sum(v.size * v.dtype.itemsize for v in jax.tree.leaves(values))


def call(body, out_shape, operands, after=(), flops=0, temporary=0, name="kernel"):
    specs = [pl.BlockSpec(memory_space=pltpu.VMEM) for _ in operands]
    specs += [pl.BlockSpec(memory_space=pl.ANY) for _ in after]
    used = len(operands)

    def whole(*refs):
        body(*refs[:used], *refs[used + len(after) :])

    moved = total_bytes(operands) + total_bytes(out_shape)
    return pl.pallas_call(
        whole,
        out_shape=out_shape,
        in_specs=specs,
        out_specs=jax.tree.map(lambda _: pl.BlockSpec(memory_space=pltpu.VMEM), out_shape),
        compiler_params=pltpu.CompilerParams(vmem_limit_bytes=(4 << 20) + 2 * moved + temporary),
        cost_estimate=pl.CostEstimate(flops=flops, bytes_accessed=moved, transcendentals=0),
        name=name,
    )(*operands, *after)


def direction(values):
    floats = values.astype(jnp.float32)
    norms = jnp.sqrt(jnp.sum(floats * floats, axis=-1, keepdims=True) + 1e-06)
    return floats / norms, norms


def prepare_body(*refs):
    sources, (speech, text) = refs[:3], refs[3:5]
    held, done = refs[5:8], refs[8]
    copies = [pltpu.make_async_copy(sources[i], held[i], done.at[i]) for i in range(3)]
    for copy in copies:
        copy.start()
    for copy in copies:
        copy.wait()
    audio, sentence, label = held
    rows = audio.shape[0]
    speech[0:rows, :] = direction(audio[...])[0].astype(jnp.bfloat16)
    text[...] = direction(sentence[...])[0].astype(jnp.bfloat16)
    number = label[...]
    digits = jnp.concatenate([number % RADIX, number // RADIX], axis=1).astype(jnp.float32)
    wide = jnp.concatenate(
        [digits, jnp.zeros((1, speech.shape[1] - 2 * rows), jnp.float32)], axis=1
    )
    speech[rows : rows + MARK_ROWS, :] = jnp.broadcast_to(
        wide, (MARK_ROWS, speech.shape[1])
    ).astype(jnp.bfloat16)


def join_body(*refs):
    out = refs[-1]
    at = 0
    for ref in refs[:-1]:
        out[at : at + ref.shape[0], :] = ref[...]
        at += ref.shape[0]


def join_both_body(count, *refs):
    join_body(*refs[:count], refs[-2])
    join_body(*refs[count:-2], refs[-1])


def halves_body(upper, lower, upper_out, lower_out):
    upper_out[...] = upper[: upper_out.shape[0], :]
    lower_out[...] = lower[upper_out.shape[0] :, :]


def marks_of(block, rows):
    digits = block[rows : rows + MARK_ROWS, 0 : 2 * rows][0:1, :].astype(jnp.float32)
    return digits[:, 0:rows] + RADIX * digits[:, rows : 2 * rows]


def coefficients(dots, match, sharp, shift):
    logits = sharp * dots + shift
    probs = 1.0 / (1.0 + jnp.exp(-logits))
    return (sharp * (probs - jnp.where(match, 1.0, 0.0))).astype(jnp.bfloat16)


def dot_rows(left, right):
    return lax.dot_general(left, right, (((1,), (1,)), ((), ())), preferred_element_type=jnp.float32)


def text_part_body(rows, own_text, ks, has_start, speeches, *refs):
    sharp, shift = refs[0][0:1, 0:1], refs[0][1:2, 0:1]
    some_text = slice(ks[0] * own_text, (ks[-1] + 1) * own_text)
    text = refs[1][some_text, :]
    total = refs[2][some_text, :] if has_start else None
    at = 3 if has_start else 2
    blocks = refs[at : at + speeches]
    outs = refs[at + speeches :]
    groups = lax.axis_size("group")
    members = lax.axis_size("member")
    group = lax.axis_index("group")
    member = lax.axis_index("member")
    stride = rows + MARK_ROWS
    for speech in blocks:
        count = speech.shape[0] // stride
        for first in range(0, count, CHUNK // rows):
            some = range(first, min(count, first + CHUNK // rows))
            chunk = [speech[k * stride : k * stride + rows, :] for k in some]
            marks = [marks_of(speech.at[k * stride : (k + 1) * stride, :], rows) for k in some]
            chunk = jnp.concatenate(chunk, axis=0)
            marks = jnp.concatenate(marks, axis=1)
            iota = lax.broadcasted_iota(jnp.int32, (own_text, marks.shape[1]), 0)
            ids = [((group ^ k) * members + member) * own_text + iota for k in ks]
            match = jnp.concatenate(ids, axis=0).astype(jnp.float32) == marks
            coef = coefficients(dot_rows(text, chunk), match, sharp, shift)
            part = jnp.dot(coef, chunk, preferred_element_type=jnp.float32)
            total = part if total is None else total + part
    row, at = 0, 0
    for out in outs:
        out[...] = total[row : row + out.shape[0], at : at + out.shape[1]]
        at += out.shape[1]
        if at == total.shape[1]:
            row, at = row + out.shape[0], 0


def speech_part_body(rows, own_text, has_start, masks, *refs):
    sharp, shift, speech = refs[0][0:1, 0:1], refs[0][1:2, 0:1], refs[1]
    total = refs[2][...] if has_start else None
    texts, out = list(refs[3 if has_start else 2 : -1]), refs[-1]
    groups = lax.axis_size("group")
    members = lax.axis_size("member")
    group = lax.axis_index("group")
    member = lax.axis_index("member")
    marks = jnp.broadcast_to(marks_of(speech, rows), (rows, rows)).T[:, 0:1]
    block = speech[0:rows, :]
    column = groups * own_text
    lane = lax.broadcasted_iota(jnp.int32, (1, column), 1)
    base = (group ^ (lane // own_text)) * members * own_text + lane % own_text
    for mask in masks:
        pieces = [texts.pop(0)[...]]
        while sum(v.shape[0] for v in pieces) < column:
            pieces.append(texts.pop(0)[...])
        text = jnp.concatenate(pieces, axis=0)
        ids = (base + (member ^ (2 * mask)) * own_text).astype(jnp.float32)
        coef = coefficients(dot_rows(block, text), marks == ids, sharp, shift)
        part = jnp.dot(coef, text, preferred_element_type=jnp.float32)
        total = part if total is None else total + part
    out[...] = total


def add_sides_body(*refs):
    out = refs[-1]
    sides = [ref for ref in refs[:-1] if ref.shape != out.shape]
    whole = [ref for ref in refs[:-1] if ref.shape == out.shape]
    at = 0
    for ref in sides:
        columns = slice(at, at + ref.shape[1])
        total = ref[...]
        for other in whole:
            total = total + other[:, columns]
        out[:, columns] = total
        at += ref.shape[1]


def sum_body(*refs):
    total = refs[0][...]
    for ref in refs[1:-1]:
        total = total + ref[...]
    refs[-1][...] = total


def project(values, back, out):
    heading, norms = direction(values)
    along = jnp.sum(heading * back, axis=-1, keepdims=True)
    out[...] = (back - heading * along) / norms


def finish_body(audio, home, back, sentence, text_back, speech_grad, text_grad):
    project(sentence[...], text_back[...], text_grad)
    project(audio[...], home[...] + back[...], speech_grad)


def shards(audio_vectors, sentence_vectors, matching_indices, sharpness_array, offset_term):
    members = lax.axis_size("member")
    groups = lax.axis_size("group")
    chips = members // 2
    rows, width = audio_vectors.shape
    own_text = sentence_vectors.shape[0]
    label = matching_indices.reshape(1, rows)
    scalars = jnp.concatenate(
        [jnp.broadcast_to(v[:, None], (1, 128)) for v in (sharpness_array, offset_term)], axis=0
    )

    def bf16(*shape):
        return jax.ShapeDtypeStruct(shape, jnp.bfloat16)

    def f32(*shape):
        return jax.ShapeDtypeStruct(shape, jnp.float32)

    arguments = [audio_vectors, sentence_vectors, label]
    speech_own, text_own, audio, sentence = pl.pallas_call(
        prepare_body,
        out_shape=[
            bf16(rows + MARK_ROWS, width),
            bf16(own_text, width),
            bf16(rows, width),
            bf16(own_text, width),
        ],
        in_specs=[pl.BlockSpec(memory_space=pltpu.HBM)] * 3,
        out_specs=[pl.BlockSpec(memory_space=pltpu.VMEM)] * 4,
        scratch_shapes=[pltpu.VMEM((1, rows), jnp.int32), pltpu.SemaphoreType.DMA((3,))],
        compiler_params=pltpu.CompilerParams(vmem_limit_bytes=8 << 20),
        name="unit_rows",
    )(*[pltpu.with_memory_space_constraint(v, pltpu.HBM) for v in arguments])

    def passed_on(block):
        return call(join_body, bf16(own_text, width), [block], (scalars,), 1 << 29, name="pass_on")

    text_blocks = [text_own] + [None] * (groups - 1)
    for k in [1 << i for i in reversed(range(groups.bit_length() - 1))]:
        for j in range(0, groups, 2 * k):
            came = exchanged(text_blocks[j], "group", k)
            text_blocks[j + k] = passed_on(came) if k > 1 else came
    square = chips == 4
    masks = [1, 2] if square else list(range(1, chips))

    def far_halves(near, middle, after=()):
        sizes = [middle, near[0].shape[0] - middle]
        halves = call(
            halves_body, [bf16(size, width) for size in sizes], near[::-1], after, name="halves"
        )
        return [exchanged(half, "member", 2 * k) for half, k in zip(halves, masks)]

    speech_blocks = [exchanged(speech_own, "member", 2 * k) for k in reversed(range(1, chips))]
    column = groups * own_text
    text, speech = call(
        functools.partial(join_both_body, groups),
        [bf16(column, width), bf16(chips * (rows + MARK_ROWS), width)],
        [*text_blocks, speech_own, *speech_blocks[::-1]],
        name="join_rows",
    )
    other = exchanged(speech, "member", 1)
    text_near = [exchanged(text, "member", 2 * k) for k in masks]

    temporary = 4 * column * (6 * CHUNK + 3 * width)

    def text_part(outs, blocks, start, ks=range(groups)):
        count = sum(v.shape[0] for v in blocks) // (rows + MARK_ROWS)
        body = functools.partial(text_part_body, rows, own_text, list(ks), bool(start), len(blocks))
        operands = [scalars, text, *start, *blocks]
        work = 4 * len(ks) * own_text * count * rows * width
        return call(body, outs, operands, (), work, temporary, "text_part")

    half = text_part([f32(column, width)], [speech], [])
    sides = 2
    side = f32(own_text, width // sides)
    outs = [f32(own_text, width)] * (groups // 2) + [side] * (groups // 2 * sides)
    parts = list(text_part(outs, [other], half))
    far = [parts[groups // 2 + i * sides :][:sides] for i in range(groups // 2)]

    bit = 1
    while bit < groups // 2:
        for k in reversed(range(bit, groups // 2, 2 * bit)):
            came = [exchanged(v, "group", bit) for v in far[k]]
            far[k - bit] = [
                call(sum_body, side, [mine, v], name="sum_near") for mine, v in zip(far[k - bit], came)
            ]
        bit *= 2
    from_far = [exchanged(v, "group", groups // 2) for v in far[0]]
    from_near = [exchanged(parts[k], "group", k) for k in range(1, groups // 2)]

    def speech_part(block, start, columns, texts, after=()):
        body = functools.partial(speech_part_body, rows, own_text, bool(start), columns)
        operands = [scalars, block, *start, *texts]
        work = 40 * rows * column * len(columns) * width
        return call(body, f32(rows, width), operands, after, work, temporary, "speech_part")

    near = [[0, *masks], [text, *text_near], tuple(far[0])]
    away = speech_part(other[0 : rows + MARK_ROWS], [], *near)
    home = speech_part(speech_own, [], *near)
    if square:
        text_far = far_halves(text_near, column // 2, tuple(far[0]))
        away = speech_part(other[0 : rows + MARK_ROWS], [away], [3], text_far)
        home = speech_part(speech_own, [home], [3], text_far)
    back = exchanged(away, "member", 1)
    text_back = call(
        add_sides_body,
        f32(own_text, width),
        [*from_far, *from_near, parts[0]],
        (),
        EARLY,
        name="text_sum",
    )
    speech_grad, text_grad = call(
        finish_body,
        [f32(rows, width), f32(own_text, width)],
        [audio, home, back, sentence, text_back],
        name="finish",
    )
    return (speech_grad, text_grad)


def solution(mesh):
    in_specs = (
        P(("group", "member"), None),
        P(("group", "member"), None),
        P(("group", "member")),
        P(),
        P(),
    )
    out_specs = (P(("group", "member"), None), P(("group", "member"), None))
    return jax.shard_map(shards, mesh=mesh, in_specs=in_specs, out_specs=out_specs, check_vma=False)
```

```python
import functools
import jax
import jax.numpy as jnp
from jax import lax
from jax.experimental import pallas as pl
from jax.experimental.pallas import tpu as pltpu
from jax.sharding import PartitionSpec as P

MARK_ROWS = 16
RADIX = 256
CHUNK = 512
EARLY = 1 << 33


def exchanged(value, axis, mask):
    size = lax.axis_size(axis)
    return lax.ppermute(value, axis, [(i, i ^ mask) for i in range(size)])


def total_bytes(values):
    return sum(v.size * v.dtype.itemsize for v in jax.tree.leaves(values))


def call(body, out_shape, operands, after=(), flops=0, temporary=0, name="kernel"):
    specs = [pl.BlockSpec(memory_space=pltpu.VMEM) for _ in operands]
    specs += [pl.BlockSpec(memory_space=pl.ANY) for _ in after]
    used = len(operands)

    def whole(*refs):
        body(*refs[:used], *refs[used + len(after) :])

    moved = total_bytes(operands) + total_bytes(out_shape)
    return pl.pallas_call(
        whole,
        out_shape=out_shape,
        in_specs=specs,
        out_specs=jax.tree.map(lambda _: pl.BlockSpec(memory_space=pltpu.VMEM), out_shape),
        compiler_params=pltpu.CompilerParams(vmem_limit_bytes=(4 << 20) + 2 * moved + temporary),
        cost_estimate=pl.CostEstimate(flops=flops, bytes_accessed=moved, transcendentals=0),
        name=name,
    )(*operands, *after)


def direction(values):
    floats = values.astype(jnp.float32)
    norms = jnp.sqrt(jnp.sum(floats * floats, axis=-1, keepdims=True) + 1e-06)
    return floats / norms, norms


def prepare_body(*refs):
    sources, (speech, text) = refs[:3], refs[3:5]
    held, done = refs[5:8], refs[8]
    copies = [pltpu.make_async_copy(sources[i], held[i], done.at[i]) for i in range(3)]
    for copy in copies:
        copy.start()
    for copy in copies:
        copy.wait()
    audio, sentence, label = held
    rows = audio.shape[0]
    speech[0:rows, :] = direction(audio[...])[0].astype(jnp.bfloat16)
    text[...] = direction(sentence[...])[0].astype(jnp.bfloat16)
    number = label[...]
    digits = jnp.concatenate([number % RADIX, number // RADIX], axis=1).astype(jnp.float32)
    wide = jnp.concatenate(
        [digits, jnp.zeros((1, speech.shape[1] - 2 * rows), jnp.float32)], axis=1
    )
    speech[rows : rows + MARK_ROWS, :] = jnp.broadcast_to(
        wide, (MARK_ROWS, speech.shape[1])
    ).astype(jnp.bfloat16)


def join_body(*refs):
    out = refs[-1]
    at = 0
    for ref in refs[:-1]:
        out[at : at + ref.shape[0], :] = ref[...]
        at += ref.shape[0]


def join_both_body(count, *refs):
    join_body(*refs[:count], refs[-2])
    join_body(*refs[count:-2], refs[-1])


def halves_body(upper, lower, upper_out, lower_out):
    upper_out[...] = upper[: upper_out.shape[0], :]
    lower_out[...] = lower[upper_out.shape[0] :, :]


def marks_of(block, rows):
    digits = block[rows : rows + MARK_ROWS, 0 : 2 * rows][0:1, :].astype(jnp.float32)
    return digits[:, 0:rows] + RADIX * digits[:, rows : 2 * rows]


def coefficients(dots, match, sharp, shift):
    logits = sharp * dots + shift
    probs = 1.0 / (1.0 + jnp.exp(-logits))
    return (sharp * (probs - jnp.where(match, 1.0, 0.0))).astype(jnp.bfloat16)


def dot_rows(left, right):
    return lax.dot_general(left, right, (((1,), (1,)), ((), ())), preferred_element_type=jnp.float32)


def text_part_body(rows, own_text, ks, has_start, speeches, *refs):
    sharp, shift = refs[0][0:1, 0:1], refs[0][1:2, 0:1]
    some_text = slice(ks[0] * own_text, (ks[-1] + 1) * own_text)
    text = refs[1][some_text, :]
    total = refs[2][some_text, :] if has_start else None
    at = 3 if has_start else 2
    blocks = refs[at : at + speeches]
    outs = refs[at + speeches :]
    groups = lax.axis_size("group")
    members = lax.axis_size("member")
    group = lax.axis_index("group")
    member = lax.axis_index("member")
    stride = rows + MARK_ROWS
    for speech in blocks:
        count = speech.shape[0] // stride
        for first in range(0, count, CHUNK // rows):
            some = range(first, min(count, first + CHUNK // rows))
            chunk = [speech[k * stride : k * stride + rows, :] for k in some]
            marks = [marks_of(speech.at[k * stride : (k + 1) * stride, :], rows) for k in some]
            chunk = jnp.concatenate(chunk, axis=0)
            marks = jnp.concatenate(marks, axis=1)
            iota = lax.broadcasted_iota(jnp.int32, (own_text, marks.shape[1]), 0)
            ids = [((group ^ k) * members + member) * own_text + iota for k in ks]
            match = jnp.concatenate(ids, axis=0).astype(jnp.float32) == marks
            coef = coefficients(dot_rows(text, chunk), match, sharp, shift)
            part = jnp.dot(coef, chunk, preferred_element_type=jnp.float32)
            total = part if total is None else total + part
    row, at = 0, 0
    for out in outs:
        out[...] = total[row : row + out.shape[0], at : at + out.shape[1]]
        at += out.shape[1]
        if at == total.shape[1]:
            row, at = row + out.shape[0], 0


def speech_part_body(rows, own_text, has_start, masks, *refs):
    sharp, shift, speech = refs[0][0:1, 0:1], refs[0][1:2, 0:1], refs[1]
    total = refs[2][...] if has_start else None
    texts, out = list(refs[3 if has_start else 2 : -1]), refs[-1]
    groups = lax.axis_size("group")
    members = lax.axis_size("member")
    group = lax.axis_index("group")
    member = lax.axis_index("member")
    marks = jnp.broadcast_to(marks_of(speech, rows), (rows, rows)).T[:, 0:1]
    block = speech[0:rows, :]
    column = groups * own_text
    lane = lax.broadcasted_iota(jnp.int32, (1, column), 1)
    base = (group ^ (lane // own_text)) * members * own_text + lane % own_text
    for mask in masks:
        pieces = [texts.pop(0)[...]]
        while sum(v.shape[0] for v in pieces) < column:
            pieces.append(texts.pop(0)[...])
        text = jnp.concatenate(pieces, axis=0)
        ids = (base + (member ^ (2 * mask)) * own_text).astype(jnp.float32)
        coef = coefficients(dot_rows(block, text), marks == ids, sharp, shift)
        part = jnp.dot(coef, text, preferred_element_type=jnp.float32)
        total = part if total is None else total + part
    out[...] = total


def add_sides_body(*refs):
    out = refs[-1]
    sides = [ref for ref in refs[:-1] if ref.shape != out.shape]
    whole = [ref for ref in refs[:-1] if ref.shape == out.shape]
    at = 0
    for ref in sides:
        columns = slice(at, at + ref.shape[1])
        total = ref[...]
        for other in whole:
            total = total + other[:, columns]
        out[:, columns] = total
        at += ref.shape[1]


def sum_body(*refs):
    total = refs[0][...]
    for ref in refs[1:-1]:
        total = total + ref[...]
    refs[-1][...] = total


def project(values, back, out):
    heading, norms = direction(values)
    along = jnp.sum(heading * back, axis=-1, keepdims=True)
    out[...] = (back - heading * along) / norms


def finish_body(audio, home, back, sentence, text_back, speech_grad, text_grad):
    project(sentence[...], text_back[...], text_grad)
    project(audio[...], home[...] + back[...], speech_grad)


def shards(audio_vectors, sentence_vectors, matching_indices, sharpness_array, offset_term):
    members = lax.axis_size("member")
    groups = lax.axis_size("group")
    chips = members // 2
    rows, width = audio_vectors.shape
    own_text = sentence_vectors.shape[0]
    label = matching_indices.reshape(1, rows)
    scalars = jnp.concatenate(
        [jnp.broadcast_to(v[:, None], (1, 128)) for v in (sharpness_array, offset_term)], axis=0
    )

    def bf16(*shape):
        return jax.ShapeDtypeStruct(shape, jnp.bfloat16)

    def f32(*shape):
        return jax.ShapeDtypeStruct(shape, jnp.float32)

    arguments = [audio_vectors, sentence_vectors, label]
    speech_own, text_own, audio, sentence = pl.pallas_call(
        prepare_body,
        out_shape=[
            bf16(rows + MARK_ROWS, width),
            bf16(own_text, width),
            bf16(rows, width),
            bf16(own_text, width),
        ],
        in_specs=[pl.BlockSpec(memory_space=pltpu.HBM)] * 3,
        out_specs=[pl.BlockSpec(memory_space=pltpu.VMEM)] * 4,
        scratch_shapes=[pltpu.VMEM((1, rows), jnp.int32), pltpu.SemaphoreType.DMA((3,))],
        compiler_params=pltpu.CompilerParams(vmem_limit_bytes=8 << 20),
        name="unit_rows",
    )(*[pltpu.with_memory_space_constraint(v, pltpu.HBM) for v in arguments])

    def passed_on(block):
        return call(join_body, bf16(own_text, width), [block], (), 1 << 20, name="pass_on")

    text_blocks = [text_own] + [None] * (groups - 1)
    for k in [1 << i for i in reversed(range(groups.bit_length() - 1))]:
        for j in range(0, groups, 2 * k):
            came = exchanged(text_blocks[j], "group", k)
            text_blocks[j + k] = passed_on(came) if k > 1 else came
    square = chips == 4
    masks = [1, 2] if square else list(range(1, chips))

    def far_halves(near, middle, after=()):
        sizes = [middle, near[0].shape[0] - middle]
        halves = call(
            halves_body, [bf16(size, width) for size in sizes], near[::-1], after, name="halves"
        )
        return [(half, exchanged(half, "member", 2 * k)) for half, k in zip(halves, masks)]

    speech_blocks = [exchanged(speech_own, "member", 2 * k) for k in reversed(range(1, chips))]
    column = groups * own_text
    text, speech = call(
        functools.partial(join_both_body, groups),
        [bf16(column, width), bf16(chips * (rows + MARK_ROWS), width)],
        [*text_blocks, speech_own, *speech_blocks[::-1]],
        (scalars,),
        name="join_rows",
    )
    other = exchanged(speech, "member", 1)
    text_near = [exchanged(text, "member", 2 * k) for k in masks]

    temporary = 4 * column * (6 * CHUNK + 3 * width)

    def text_part(outs, blocks, start, ks=range(groups)):
        count = sum(v.shape[0] for v in blocks) // (rows + MARK_ROWS)
        body = functools.partial(text_part_body, rows, own_text, list(ks), bool(start), len(blocks))
        operands = [scalars, text, *start, *blocks]
        work = 4 * len(ks) * own_text * count * rows * width
        return call(body, outs, operands, (), work, temporary, "text_part")

    half = text_part([f32(column, width)], [speech], [])
    sides = 2
    side = f32(own_text, width // sides)
    outs = [f32(own_text, width)] * (groups // 2) + [side] * (groups // 2 * sides)
    parts = list(text_part(outs, [other], half))
    far = [parts[groups // 2 + i * sides :][:sides] for i in range(groups // 2)]

    text_far = []
    bit = 1
    while bit < groups // 2:
        for k in reversed(range(bit, groups // 2, 2 * bit)):
            came = [exchanged(v, "group", bit) for v in far[k]]
            sums = []
            for mine, v in zip(far[k - bit], came):
                if sums and square and not text_far:
                    text_far = far_halves(text_near, column // 2, tuple(sums))
                    gate = (text_far[0][0],)
                else:
                    gate = ()
                sums.append(call(sum_body, side, [mine, v], gate, name="sum_near"))
            far[k - bit] = sums
        bit *= 2
    if square:
        text_far = [came for _, came in text_far]
    from_far = [exchanged(v, "group", groups // 2) for v in far[0]]
    from_near = [exchanged(parts[k], "group", k) for k in range(1, groups // 2)]

    def speech_part(block, start, columns, texts, after=()):
        body = functools.partial(speech_part_body, rows, own_text, bool(start), columns)
        operands = [scalars, block, *start, *texts]
        work = 40 * rows * column * len(columns) * width
        return call(body, f32(rows, width), operands, after, work, temporary, "speech_part")

    near = [[0, *masks], [text, *text_near], tuple(far[0])]
    away = speech_part(other[0 : rows + MARK_ROWS], [], *near)
    home = speech_part(speech_own, [], *near)
    if square:
        away = speech_part(other[0 : rows + MARK_ROWS], [away], [3], text_far)
        home = speech_part(speech_own, [home], [3], text_far)
    back = exchanged(away, "member", 1)
    text_back = call(
        add_sides_body,
        f32(own_text, width),
        [*from_far, *from_near, parts[0]],
        (),
        EARLY,
        name="text_sum",
    )
    speech_grad, text_grad = call(
        finish_body,
        [f32(rows, width), f32(own_text, width)],
        [audio, home, back, sentence, text_back],
        name="finish",
    )
    return (speech_grad, text_grad)


def solution(mesh):
    in_specs = (
        P(("group", "member"), None),
        P(("group", "member"), None),
        P(("group", "member")),
        P(),
        P(),
    )
    out_specs = (P(("group", "member"), None), P(("group", "member"), None))
    return jax.shard_map(shards, mesh=mesh, in_specs=in_specs, out_specs=out_specs, check_vma=False)
```

```python
import functools
import jax
import jax.numpy as jnp
from jax import lax
from jax.experimental import pallas as pl
from jax.experimental.pallas import tpu as pltpu
from jax.sharding import PartitionSpec as P

MARK_ROWS = 16
RADIX = 256
CHUNK = 512
EARLY = 1 << 33


def exchanged(value, axis, mask):
    size = lax.axis_size(axis)
    return lax.ppermute(value, axis, [(i, i ^ mask) for i in range(size)])


def total_bytes(values):
    return sum(v.size * v.dtype.itemsize for v in jax.tree.leaves(values))


def call(body, out_shape, operands, after=(), flops=0, temporary=0, name="kernel"):
    specs = [pl.BlockSpec(memory_space=pltpu.VMEM) for _ in operands]
    specs += [pl.BlockSpec(memory_space=pl.ANY) for _ in after]
    used = len(operands)

    def whole(*refs):
        body(*refs[:used], *refs[used + len(after) :])

    moved = total_bytes(operands) + total_bytes(out_shape)
    return pl.pallas_call(
        whole,
        out_shape=out_shape,
        in_specs=specs,
        out_specs=jax.tree.map(lambda _: pl.BlockSpec(memory_space=pltpu.VMEM), out_shape),
        compiler_params=pltpu.CompilerParams(vmem_limit_bytes=(4 << 20) + 2 * moved + temporary),
        cost_estimate=pl.CostEstimate(flops=flops, bytes_accessed=moved, transcendentals=0),
        name=name,
    )(*operands, *after)


def direction(values):
    floats = values.astype(jnp.float32)
    norms = jnp.sqrt(jnp.sum(floats * floats, axis=-1, keepdims=True) + 1e-06)
    return floats / norms, norms


def prepare_body(*refs):
    sources, (speech, text) = refs[:3], refs[3:5]
    held, done = refs[5:8], refs[8]
    copies = [pltpu.make_async_copy(sources[i], held[i], done.at[i]) for i in range(3)]
    for copy in copies:
        copy.start()
    for copy in copies:
        copy.wait()
    audio, sentence, label = held
    rows = audio.shape[0]
    speech[0:rows, :] = direction(audio[...])[0].astype(jnp.bfloat16)
    text[...] = direction(sentence[...])[0].astype(jnp.bfloat16)
    number = label[...]
    digits = jnp.concatenate([number % RADIX, number // RADIX], axis=1).astype(jnp.float32)
    wide = jnp.concatenate(
        [digits, jnp.zeros((1, speech.shape[1] - 2 * rows), jnp.float32)], axis=1
    )
    speech[rows : rows + MARK_ROWS, :] = jnp.broadcast_to(
        wide, (MARK_ROWS, speech.shape[1])
    ).astype(jnp.bfloat16)


def join_body(*refs):
    out = refs[-1]
    at = 0
    for ref in refs[:-1]:
        out[at : at + ref.shape[0], :] = ref[...]
        at += ref.shape[0]


def join_both_body(count, *refs):
    join_body(*refs[:count], refs[-2])
    join_body(*refs[count:-2], refs[-1])


def halves_body(upper, lower, upper_out, lower_out):
    upper_out[...] = upper[: upper_out.shape[0], :]
    lower_out[...] = lower[upper_out.shape[0] :, :]


def marks_of(block, rows):
    digits = block[rows : rows + MARK_ROWS, 0 : 2 * rows][0:1, :].astype(jnp.float32)
    return digits[:, 0:rows] + RADIX * digits[:, rows : 2 * rows]


def coefficients(dots, match, sharp, shift):
    logits = sharp * dots + shift
    probs = 1.0 / (1.0 + jnp.exp(-logits))
    return (sharp * (probs - jnp.where(match, 1.0, 0.0))).astype(jnp.bfloat16)


def dot_rows(left, right):
    return lax.dot_general(left, right, (((1,), (1,)), ((), ())), preferred_element_type=jnp.float32)


def text_part_body(rows, own_text, ks, has_start, speeches, *refs):
    sharp, shift = refs[0][0:1, 0:1], refs[0][1:2, 0:1]
    some_text = slice(ks[0] * own_text, (ks[-1] + 1) * own_text)
    text = refs[1][some_text, :]
    total = refs[2][some_text, :] if has_start else None
    at = 3 if has_start else 2
    blocks = refs[at : at + speeches]
    outs = refs[at + speeches :]
    groups = lax.axis_size("group")
    members = lax.axis_size("member")
    group = lax.axis_index("group")
    member = lax.axis_index("member")
    stride = rows + MARK_ROWS
    for speech in blocks:
        count = speech.shape[0] // stride
        for first in range(0, count, CHUNK // rows):
            some = range(first, min(count, first + CHUNK // rows))
            chunk = [speech[k * stride : k * stride + rows, :] for k in some]
            marks = [marks_of(speech.at[k * stride : (k + 1) * stride, :], rows) for k in some]
            chunk = jnp.concatenate(chunk, axis=0)
            marks = jnp.concatenate(marks, axis=1)
            iota = lax.broadcasted_iota(jnp.int32, (own_text, marks.shape[1]), 0)
            ids = [((group ^ k) * members + member) * own_text + iota for k in ks]
            match = jnp.concatenate(ids, axis=0).astype(jnp.float32) == marks
            coef = coefficients(dot_rows(text, chunk), match, sharp, shift)
            part = jnp.dot(coef, chunk, preferred_element_type=jnp.float32)
            total = part if total is None else total + part
    row, at = 0, 0
    for out in outs:
        out[...] = total[row : row + out.shape[0], at : at + out.shape[1]]
        at += out.shape[1]
        if at == total.shape[1]:
            row, at = row + out.shape[0], 0


def speech_part_body(rows, own_text, has_start, masks, *refs):
    sharp, shift, speech = refs[0][0:1, 0:1], refs[0][1:2, 0:1], refs[1]
    total = refs[2][...] if has_start else None
    texts, out = list(refs[3 if has_start else 2 : -1]), refs[-1]
    groups = lax.axis_size("group")
    members = lax.axis_size("member")
    group = lax.axis_index("group")
    member = lax.axis_index("member")
    marks = jnp.broadcast_to(marks_of(speech, rows), (rows, rows)).T[:, 0:1]
    block = speech[0:rows, :]
    column = groups * own_text
    lane = lax.broadcasted_iota(jnp.int32, (1, column), 1)
    base = (group ^ (lane // own_text)) * members * own_text + lane % own_text
    for mask in masks:
        pieces = [texts.pop(0)[...]]
        while sum(v.shape[0] for v in pieces) < column:
            pieces.append(texts.pop(0)[...])
        text = jnp.concatenate(pieces, axis=0)
        ids = (base + (member ^ (2 * mask)) * own_text).astype(jnp.float32)
        coef = coefficients(dot_rows(block, text), marks == ids, sharp, shift)
        part = jnp.dot(coef, text, preferred_element_type=jnp.float32)
        total = part if total is None else total + part
    out[...] = total


def add_sides_body(*refs):
    out = refs[-1]
    sides = [ref for ref in refs[:-1] if ref.shape != out.shape]
    whole = [ref for ref in refs[:-1] if ref.shape == out.shape]
    at = 0
    for ref in sides:
        columns = slice(at, at + ref.shape[1])
        total = ref[...]
        for other in whole:
            total = total + other[:, columns]
        out[:, columns] = total
        at += ref.shape[1]


def sum_body(*refs):
    total = refs[0][...]
    for ref in refs[1:-1]:
        total = total + ref[...]
    refs[-1][...] = total


def project(values, back, out):
    heading, norms = direction(values)
    along = jnp.sum(heading * back, axis=-1, keepdims=True)
    out[...] = (back - heading * along) / norms


def finish_body(audio, home, back, sentence, text_back, speech_grad, text_grad):
    project(sentence[...], text_back[...], text_grad)
    project(audio[...], home[...] + back[...], speech_grad)


def shards(audio_vectors, sentence_vectors, matching_indices, sharpness_array, offset_term):
    members = lax.axis_size("member")
    groups = lax.axis_size("group")
    chips = members // 2
    rows, width = audio_vectors.shape
    own_text = sentence_vectors.shape[0]
    label = matching_indices.reshape(1, rows)
    scalars = jnp.concatenate(
        [jnp.broadcast_to(v[:, None], (1, 128)) for v in (sharpness_array, offset_term)], axis=0
    )

    def bf16(*shape):
        return jax.ShapeDtypeStruct(shape, jnp.bfloat16)

    def f32(*shape):
        return jax.ShapeDtypeStruct(shape, jnp.float32)

    arguments = [audio_vectors, sentence_vectors, label]
    speech_own, text_own, audio, sentence = pl.pallas_call(
        prepare_body,
        out_shape=[
            bf16(rows + MARK_ROWS, width),
            bf16(own_text, width),
            bf16(rows, width),
            bf16(own_text, width),
        ],
        in_specs=[pl.BlockSpec(memory_space=pltpu.HBM)] * 3,
        out_specs=[pl.BlockSpec(memory_space=pltpu.VMEM)] * 4,
        scratch_shapes=[pltpu.VMEM((1, rows), jnp.int32), pltpu.SemaphoreType.DMA((3,))],
        compiler_params=pltpu.CompilerParams(vmem_limit_bytes=8 << 20),
        name="unit_rows",
    )(*[pltpu.with_memory_space_constraint(v, pltpu.HBM) for v in arguments])

    def passed_on(block):
        return call(join_body, bf16(own_text, width), [block], (), 1 << 29, name="pass_on")

    text_blocks = [text_own] + [None] * (groups - 1)
    for k in [1 << i for i in reversed(range(groups.bit_length() - 1))]:
        for j in range(0, groups, 2 * k):
            came = exchanged(text_blocks[j], "group", k)
            text_blocks[j + k] = passed_on(came) if k > 1 else came
    square = chips == 4
    masks = [1, 2] if square else list(range(1, chips))

    def far_halves(near, middle, after=()):
        sizes = [middle, near[0].shape[0] - middle]
        halves = call(
            halves_body, [bf16(size, width) for size in sizes], near[::-1], after, name="halves"
        )
        return [(half, exchanged(half, "member", 2 * k)) for half, k in zip(halves, masks)]

    speech_blocks = [exchanged(speech_own, "member", 2 * k) for k in reversed(range(1, chips))]
    column = groups * own_text
    text, speech = call(
        functools.partial(join_both_body, groups),
        [bf16(column, width), bf16(chips * (rows + MARK_ROWS), width)],
        [*text_blocks, speech_own, *speech_blocks[::-1]],
        (scalars,),
        name="join_rows",
    )
    other = exchanged(speech, "member", 1)
    text_near = [exchanged(text, "member", 2 * k) for k in masks]

    temporary = 4 * column * (6 * CHUNK + 3 * width)

    def text_part(outs, blocks, start, ks=range(groups)):
        count = sum(v.shape[0] for v in blocks) // (rows + MARK_ROWS)
        body = functools.partial(text_part_body, rows, own_text, list(ks), bool(start), len(blocks))
        operands = [scalars, text, *start, *blocks]
        work = 4 * len(ks) * own_text * count * rows * width
        return call(body, outs, operands, (), work, temporary, "text_part")

    half = text_part([f32(column, width)], [speech], [])
    sides = 2
    side = f32(own_text, width // sides)
    outs = [f32(own_text, width)] * (groups // 2) + [side] * (groups // 2 * sides)
    parts = list(text_part(outs, [other], half))
    far = [parts[groups // 2 + i * sides :][:sides] for i in range(groups // 2)]

    text_far = []
    bit = 1
    while bit < groups // 2:
        for k in reversed(range(bit, groups // 2, 2 * bit)):
            came = [exchanged(v, "group", bit) for v in far[k]]
            sums = []
            for mine, v in zip(far[k - bit], came):
                if sums and square and not text_far:
                    text_far = far_halves(text_near, column // 2, tuple(sums))
                    gate = (text_far[0][0],)
                else:
                    gate = ()
                sums.append(call(sum_body, side, [mine, v], gate, name="sum_near"))
            far[k - bit] = sums
        bit *= 2
    if square:
        text_far = [came for _, came in text_far]
    from_far = [exchanged(v, "group", groups // 2) for v in far[0]]
    from_near = [exchanged(parts[k], "group", k) for k in range(1, groups // 2)]

    def speech_part(block, start, columns, texts, after=()):
        body = functools.partial(speech_part_body, rows, own_text, bool(start), columns)
        operands = [scalars, block, *start, *texts]
        work = 40 * rows * column * len(columns) * width
        return call(body, f32(rows, width), operands, after, work, temporary, "speech_part")

    near = [[0, *masks], [text, *text_near], tuple(far[0])]
    away = speech_part(other[0 : rows + MARK_ROWS], [], *near)
    home = speech_part(speech_own, [], *near)
    if square:
        away = speech_part(other[0 : rows + MARK_ROWS], [away], [3], text_far)
        home = speech_part(speech_own, [home], [3], text_far)
    back = exchanged(away, "member", 1)
    text_back = call(
        add_sides_body,
        f32(own_text, width),
        [*from_far, *from_near, parts[0]],
        (),
        EARLY,
        name="text_sum",
    )
    speech_grad, text_grad = call(
        finish_body,
        [f32(rows, width), f32(own_text, width)],
        [audio, home, back, sentence, text_back],
        name="finish",
    )
    return (speech_grad, text_grad)


def solution(mesh):
    in_specs = (
        P(("group", "member"), None),
        P(("group", "member"), None),
        P(("group", "member")),
        P(),
        P(),
    )
    out_specs = (P(("group", "member"), None), P(("group", "member"), None))
    return jax.shard_map(shards, mesh=mesh, in_specs=in_specs, out_specs=out_specs, check_vma=False)
```

```python
import functools
import jax
import jax.numpy as jnp
from jax import lax
from jax.experimental import pallas as pl
from jax.experimental.pallas import tpu as pltpu
from jax.sharding import PartitionSpec as P

MARK_ROWS = 8
TILE_ROWS = 16
RADIX = 256
CHUNK = 512
EARLY = 1 << 33


def exchanged(value, axis, mask):
    size = lax.axis_size(axis)
    return lax.ppermute(value, axis, [(i, i ^ mask) for i in range(size)])


def total_bytes(values):
    return sum(v.size * v.dtype.itemsize for v in jax.tree.leaves(values))


def call(body, out_shape, operands, after=(), flops=0, temporary=0, name="kernel"):
    specs = [pl.BlockSpec(memory_space=pltpu.VMEM) for _ in operands]
    specs += [pl.BlockSpec(memory_space=pl.ANY) for _ in after]
    used = len(operands)

    def whole(*refs):
        body(*refs[:used], *refs[used + len(after) :])

    moved = total_bytes(operands) + total_bytes(out_shape)
    return pl.pallas_call(
        whole,
        out_shape=out_shape,
        in_specs=specs,
        out_specs=jax.tree.map(lambda _: pl.BlockSpec(memory_space=pltpu.VMEM), out_shape),
        compiler_params=pltpu.CompilerParams(vmem_limit_bytes=(4 << 20) + 2 * moved + temporary),
        cost_estimate=pl.CostEstimate(flops=flops, bytes_accessed=moved, transcendentals=0),
        name=name,
    )(*operands, *after)


def direction(values):
    floats = values.astype(jnp.float32)
    norms = jnp.sqrt(jnp.sum(floats * floats, axis=-1, keepdims=True) + 1e-06)
    return floats / norms, norms


def prepare_body(*refs):
    sources, (speech, text) = refs[:3], refs[3:5]
    held, done = refs[5:8], refs[8]
    copies = [pltpu.make_async_copy(sources[i], held[i], done.at[i]) for i in range(3)]
    for copy in copies:
        copy.start()
    for copy in copies:
        copy.wait()
    audio, sentence, label = held
    rows = audio.shape[0]
    speech[0:rows, :] = direction(audio[...])[0].astype(jnp.bfloat16)
    text[...] = direction(sentence[...])[0].astype(jnp.bfloat16)
    number = label[...]
    digits = jnp.concatenate([number % RADIX, number // RADIX], axis=1).astype(jnp.float32)
    wide = jnp.concatenate(
        [digits, jnp.zeros((1, speech.shape[1] - 2 * rows), jnp.float32)], axis=1
    )
    speech[rows : rows + MARK_ROWS, :] = jnp.broadcast_to(
        wide, (MARK_ROWS, speech.shape[1])
    ).astype(jnp.bfloat16)


def join_body(*refs):
    out = refs[-1]
    at = 0
    for ref in refs[:-1]:
        out[at : at + ref.shape[0], :] = ref[...]
        at += ref.shape[0]


def digits_of(rows, block):
    digits = block[rows : rows + MARK_ROWS, 0 : 2 * rows].astype(jnp.float32)
    return digits[0:1, 0:rows], digits[0:1, rows : 2 * rows]


def mark_rows_of(chips, rows):
    chunks = -(-chips // (CHUNK // rows))
    return -(-2 * chunks // TILE_ROWS) * TILE_ROWS


def join_both_body(count, *refs):
    text, speech = refs[-2:]
    join_body(*refs[:count], text)
    blocks = refs[count:-2]
    rows = blocks[0].shape[0] - MARK_ROWS
    width = speech.shape[1]
    for k, ref in enumerate(blocks):
        speech[k * rows : (k + 1) * rows, :] = ref[0:rows, :]
    per = CHUNK // rows
    height = mark_rows_of(len(blocks), rows)
    place = lax.broadcasted_iota(jnp.int32, (height, width), 0)
    table = jnp.zeros((height, width), jnp.float32)
    for chunk in range(0, len(blocks), per):
        both = [digits_of(rows, ref) for ref in blocks[chunk : chunk + per]]
        for i in range(2):
            parts = [digits[i] for digits in both]
            rest = width - rows * len(parts)
            line = jnp.concatenate([*parts, jnp.zeros((1, rest), jnp.float32)], axis=1)
            table = jnp.where(place == 2 * (chunk // per) + i, line, table)
    speech[len(blocks) * rows :, :] = table.astype(jnp.bfloat16)


def halves_body(upper, lower, upper_out, lower_out):
    upper_out[...] = upper[: upper_out.shape[0], :]
    lower_out[...] = lower[upper_out.shape[0] :, :]


def marks_of(table, chunk, count):
    digits = table[2 * chunk : 2 * chunk + 2, 0:count]
    return digits[0:1, :] + RADIX * digits[1:2, :]


def coefficients(dots, match, sharp, shift):
    logits = sharp * dots + shift
    probs = 1.0 / (1.0 + jnp.exp(-logits))
    return (sharp * (probs - jnp.where(match, 1.0, 0.0))).astype(jnp.bfloat16)


def dot_rows(left, right):
    return lax.dot_general(left, right, (((1,), (1,)), ((), ())), preferred_element_type=jnp.float32)


def text_part_body(rows, own_text, has_start, chips, *refs):
    sharp, shift = refs[0][0:1, 0:1], refs[0][1:2, 0:1]
    text, speech = refs[1][...], refs[2]
    total = refs[3][...] if has_start else None
    outs = refs[4 if has_start else 3 :]
    groups = lax.axis_size("group")
    members = lax.axis_size("member")
    group = lax.axis_index("group")
    member = lax.axis_index("member")
    table = speech[chips * rows :, :].astype(jnp.float32)
    for first in range(0, chips * rows, CHUNK):
        chunk = speech[first : min(first + CHUNK, chips * rows), :]
        marks = marks_of(table, first // CHUNK, chunk.shape[0])
        iota = lax.broadcasted_iota(jnp.int32, (own_text, chunk.shape[0]), 0)
        ids = [((group ^ k) * members + member) * own_text + iota for k in range(groups)]
        match = jnp.concatenate(ids, axis=0).astype(jnp.float32) == marks
        coef = coefficients(dot_rows(text, chunk), match, sharp, shift)
        part = jnp.dot(coef, chunk, preferred_element_type=jnp.float32)
        total = part if total is None else total + part
    row, at = 0, 0
    for out in outs:
        out[...] = total[row : row + out.shape[0], at : at + out.shape[1]]
        at += out.shape[1]
        if at == total.shape[1]:
            row, at = row + out.shape[0], 0


def speech_part_body(rows, own_text, has_start, chips, masks, outputs, *refs):
    sharp, shift, speech = refs[0][0:1, 0:1], refs[0][1:2, 0:1], refs[1]
    total = refs[2][...] if has_start else None
    texts, outs = list(refs[3 if has_start else 2 : -outputs]), refs[-outputs:]
    groups = lax.axis_size("group")
    members = lax.axis_size("member")
    group = lax.axis_index("group")
    member = lax.axis_index("member")
    table = speech[chips * rows :, :].astype(jnp.float32)
    marks = jnp.broadcast_to(marks_of(table, 0, rows), (rows, rows)).T[:, 0:1]
    block = speech[0:rows, :]
    column = groups * own_text
    lane = lax.broadcasted_iota(jnp.int32, (1, column), 1)
    base = (group ^ (lane // own_text)) * members * own_text + lane % own_text
    for mask in masks:
        pieces = [texts.pop(0)[...]]
        while sum(v.shape[0] for v in pieces) < column:
            pieces.append(texts.pop(0)[...])
        text = jnp.concatenate(pieces, axis=0)
        ids = (base + (member ^ (2 * mask)) * own_text).astype(jnp.float32)
        coef = coefficients(dot_rows(block, text), marks == ids, sharp, shift)
        part = jnp.dot(coef, text, preferred_element_type=jnp.float32)
        total = part if total is None else total + part
    for k, out in enumerate(outs):
        out[...] = total[k * out.shape[0] : (k + 1) * out.shape[0], :]


def add_sides_body(*refs):
    out = refs[-1]
    sides = [ref for ref in refs[:-1] if ref.shape != out.shape]
    whole = [ref for ref in refs[:-1] if ref.shape == out.shape]
    at = 0
    for ref in sides:
        columns = slice(at, at + ref.shape[1])
        total = ref[...]
        for other in whole:
            total = total + other[:, columns]
        out[:, columns] = total
        at += ref.shape[1]


def sum_body(*refs):
    total = refs[0][...]
    for ref in refs[1:-1]:
        total = total + ref[...]
    refs[-1][...] = total


def project(values, back):
    heading, norms = direction(values)
    along = jnp.sum(heading * back, axis=-1, keepdims=True)
    return (back - heading * along) / norms


def finish_body(pieces, audio, home, *refs):
    backs, (sentence, text_back) = refs[:pieces], refs[pieces : pieces + 2]
    speech_grad, text_grad, speech_held, text_held, done = refs[pieces + 2 :]
    text_held[...] = project(sentence[...], text_back[...])
    copies = [pltpu.make_async_copy(text_held, text_grad, done.at[0])]
    copies[0].start()
    for i, back in enumerate(backs):
        size = back.shape[0]
        some = slice(i * size, (i + 1) * size)
        speech_held[some, :] = project(audio[some, :], home[some, :] + back[...])
        copy = pltpu.make_async_copy(
            speech_held.at[some, :], speech_grad.at[some, :], done.at[i + 1]
        )
        copy.start()
        copies.append(copy)
    for copy in copies:
        copy.wait()


def shards(audio_vectors, sentence_vectors, matching_indices, sharpness_array, offset_term):
    members = lax.axis_size("member")
    groups = lax.axis_size("group")
    chips = members // 2
    rows, width = audio_vectors.shape
    own_text = sentence_vectors.shape[0]
    label = matching_indices.reshape(1, rows)
    scalars = jnp.concatenate(
        [jnp.broadcast_to(v[:, None], (1, 128)) for v in (sharpness_array, offset_term)], axis=0
    )

    def bf16(*shape):
        return jax.ShapeDtypeStruct(shape, jnp.bfloat16)

    def f32(*shape):
        return jax.ShapeDtypeStruct(shape, jnp.float32)

    arguments = [audio_vectors, sentence_vectors, label]
    speech_own, text_own, audio, sentence = pl.pallas_call(
        prepare_body,
        out_shape=[
            bf16(rows + MARK_ROWS, width),
            bf16(own_text, width),
            bf16(rows, width),
            bf16(own_text, width),
        ],
        in_specs=[pl.BlockSpec(memory_space=pltpu.HBM)] * 3,
        out_specs=[pl.BlockSpec(memory_space=pltpu.VMEM)] * 4,
        scratch_shapes=[pltpu.VMEM((1, rows), jnp.int32), pltpu.SemaphoreType.DMA((3,))],
        compiler_params=pltpu.CompilerParams(vmem_limit_bytes=8 << 20),
        name="unit_rows",
    )(*[pltpu.with_memory_space_constraint(v, pltpu.HBM) for v in arguments])

    def passed_on(block):
        return call(join_body, bf16(own_text, width), [block], (), 1 << 29, name="pass_on")

    text_blocks = [text_own] + [None] * (groups - 1)
    for k in [1 << i for i in reversed(range(groups.bit_length() - 1))]:
        for j in range(0, groups, 2 * k):
            came = exchanged(text_blocks[j], "group", k)
            text_blocks[j + k] = passed_on(came) if k > 1 else came
    square = chips == 4
    masks = [1, 2] if square else list(range(1, chips))

    def far_halves(near, middle, after=()):
        sizes = [middle, near[0].shape[0] - middle]
        halves = call(
            halves_body, [bf16(size, width) for size in sizes], near[::-1], after, name="halves"
        )
        return [(half, exchanged(half, "member", 2 * k)) for half, k in zip(halves, masks)]

    speech_blocks = [exchanged(speech_own, "member", 2 * k) for k in reversed(range(1, chips))]
    column = groups * own_text
    text, speech = call(
        functools.partial(join_both_body, groups),
        [bf16(column, width), bf16(chips * rows + mark_rows_of(chips, rows), width)],
        [*text_blocks, speech_own, *speech_blocks[::-1]],
        (scalars,),
        name="join_rows",
    )
    other = exchanged(speech, "member", 1)
    text_near = [exchanged(text, "member", 2 * k) for k in masks]

    temporary = 4 * column * (6 * CHUNK + 3 * width)

    def text_part(outs, speech, start):
        body = functools.partial(text_part_body, rows, own_text, bool(start), chips)
        work = 4 * column * chips * rows * width
        return call(body, outs, [scalars, text, speech, *start], (), work, temporary, "text_part")

    half = text_part([f32(column, width)], speech, [])
    sides = 2
    side = f32(own_text, width // sides)
    outs = [f32(own_text, width)] * (groups // 2) + [side] * (groups // 2 * sides)
    parts = list(text_part(outs, other, half))
    far = [parts[groups // 2 + i * sides :][:sides] for i in range(groups // 2)]

    text_far = []
    bit = 1
    while bit < groups // 2:
        for k in reversed(range(bit, groups // 2, 2 * bit)):
            came = [exchanged(v, "group", bit) for v in far[k]]
            sums = []
            for mine, v in zip(far[k - bit], came):
                if sums and square and not text_far:
                    text_far = far_halves(text_near, column // 2, tuple(sums))
                    gate = (text_far[0][0],)
                else:
                    gate = ()
                sums.append(call(sum_body, side, [mine, v], gate, name="sum_near"))
            far[k - bit] = sums
        bit *= 2
    if square:
        text_far = [came for _, came in text_far]
    from_far = [exchanged(v, "group", groups // 2) for v in far[0]]
    from_near = [exchanged(parts[k], "group", k) for k in range(1, groups // 2)]

    def speech_part(speech, start, columns, texts, after=(), pieces=1):
        body = functools.partial(
            speech_part_body, rows, own_text, bool(start), chips, columns, pieces
        )
        work = 40 * rows * column * len(columns) * width
        outs = [f32(rows // pieces, width)] * pieces
        operands = [scalars, speech, *start, *texts]
        return call(body, outs, operands, after, work, temporary, "speech_part")

    near = [[0, *masks], [text, *text_near], tuple(far[0])]
    if square:
        away = speech_part(other, [], *near)
        home = speech_part(speech, [], *near)
        away = speech_part(other, away, [3], text_far, pieces=2)
        home = speech_part(speech, home, [3], text_far)
    else:
        away = speech_part(other, [], *near, pieces=2)
        home = speech_part(speech, [], *near)
    back = [exchanged(piece, "member", 1) for piece in away]
    text_back = call(
        add_sides_body,
        f32(own_text, width),
        [*from_far, *from_near, parts[0]],
        (),
        EARLY,
        name="text_sum",
    )
    results = [f32(rows, width), f32(own_text, width)]
    speech_grad, text_grad = pl.pallas_call(
        functools.partial(finish_body, len(back)),
        out_shape=results,
        in_specs=[pl.BlockSpec(memory_space=pltpu.VMEM)] * (4 + len(back)),
        out_specs=[pl.BlockSpec(memory_space=pltpu.HBM)] * 2,
        scratch_shapes=[
            *[pltpu.VMEM(v.shape, v.dtype) for v in results],
            pltpu.SemaphoreType.DMA((1 + len(back),)),
        ],
        compiler_params=pltpu.CompilerParams(vmem_limit_bytes=8 << 20),
        name="finish",
    )(audio, *home, *back, sentence, text_back)
    return (speech_grad, text_grad)


def solution(mesh):
    in_specs = (
        P(("group", "member"), None),
        P(("group", "member"), None),
        P(("group", "member")),
        P(),
        P(),
    )
    out_specs = (P(("group", "member"), None), P(("group", "member"), None))
    return jax.shard_map(shards, mesh=mesh, in_specs=in_specs, out_specs=out_specs, check_vma=False)
```

```python
import functools
import jax
import jax.numpy as jnp
from jax import lax
from jax.experimental import pallas as pl
from jax.experimental.pallas import tpu as pltpu
from jax.sharding import PartitionSpec as P

MARK_ROWS = 8
TILE_ROWS = 16
RADIX = 256
CHUNK = 512
EARLY = 1 << 33


def exchanged(value, axis, mask):
    size = lax.axis_size(axis)
    return lax.ppermute(value, axis, [(i, i ^ mask) for i in range(size)])


def total_bytes(values):
    return sum(v.size * v.dtype.itemsize for v in jax.tree.leaves(values))


def call(body, out_shape, operands, after=(), flops=0, temporary=0, name="kernel"):
    specs = [pl.BlockSpec(memory_space=pltpu.VMEM) for _ in operands]
    specs += [pl.BlockSpec(memory_space=pl.ANY) for _ in after]
    used = len(operands)

    def whole(*refs):
        body(*refs[:used], *refs[used + len(after) :])

    moved = total_bytes(operands) + total_bytes(out_shape)
    return pl.pallas_call(
        whole,
        out_shape=out_shape,
        in_specs=specs,
        out_specs=jax.tree.map(lambda _: pl.BlockSpec(memory_space=pltpu.VMEM), out_shape),
        compiler_params=pltpu.CompilerParams(vmem_limit_bytes=(4 << 20) + 2 * moved + temporary),
        cost_estimate=pl.CostEstimate(flops=flops, bytes_accessed=moved, transcendentals=0),
        name=name,
    )(*operands, *after)


def direction(values):
    floats = values.astype(jnp.float32)
    norms = jnp.sqrt(jnp.sum(floats * floats, axis=-1, keepdims=True) + 1e-06)
    return floats / norms, norms


def prepare_body(*refs):
    sources, (speech, text) = refs[:3], refs[3:5]
    held, done = refs[5:8], refs[8]
    copies = [pltpu.make_async_copy(sources[i], held[i], done.at[i]) for i in range(3)]
    for copy in copies:
        copy.start()
    for copy in copies:
        copy.wait()
    audio, sentence, label = held
    rows = audio.shape[0]
    speech[0:rows, :] = direction(audio[...])[0].astype(jnp.bfloat16)
    text[...] = direction(sentence[...])[0].astype(jnp.bfloat16)
    number = label[...]
    digits = jnp.concatenate([number % RADIX, number // RADIX], axis=1).astype(jnp.float32)
    wide = jnp.concatenate(
        [digits, jnp.zeros((1, speech.shape[1] - 2 * rows), jnp.float32)], axis=1
    )
    speech[rows : rows + MARK_ROWS, :] = jnp.broadcast_to(
        wide, (MARK_ROWS, speech.shape[1])
    ).astype(jnp.bfloat16)


def join_body(*refs):
    out = refs[-1]
    at = 0
    for ref in refs[:-1]:
        out[at : at + ref.shape[0], :] = ref[...]
        at += ref.shape[0]


def digits_of(rows, block):
    digits = block[rows : rows + MARK_ROWS, 0 : 2 * rows].astype(jnp.float32)
    return digits[0:1, 0:rows], digits[0:1, rows : 2 * rows]


def mark_rows_of(chips, rows):
    chunks = -(-chips // (CHUNK // rows))
    return -(-2 * chunks // TILE_ROWS) * TILE_ROWS


def join_both_body(count, *refs):
    text, speech = refs[-2:]
    join_body(*refs[:count], text)
    blocks = refs[count:-2]
    rows = blocks[0].shape[0] - MARK_ROWS
    width = speech.shape[1]
    for k, ref in enumerate(blocks):
        speech[k * rows : (k + 1) * rows, :] = ref[0:rows, :]
    per = CHUNK // rows
    height = mark_rows_of(len(blocks), rows)
    place = lax.broadcasted_iota(jnp.int32, (height, width), 0)
    table = jnp.zeros((height, width), jnp.float32)
    for chunk in range(0, len(blocks), per):
        both = [digits_of(rows, ref) for ref in blocks[chunk : chunk + per]]
        for i in range(2):
            parts = [digits[i] for digits in both]
            rest = width - rows * len(parts)
            line = jnp.concatenate([*parts, jnp.zeros((1, rest), jnp.float32)], axis=1)
            table = jnp.where(place == 2 * (chunk // per) + i, line, table)
    speech[len(blocks) * rows :, :] = table.astype(jnp.bfloat16)


def cut_body(first, source, out):
    out[...] = source[first : first + out.shape[0], :]


def marks_of(table, chunk, count):
    digits = table[2 * chunk : 2 * chunk + 2, 0:count]
    return digits[0:1, :] + RADIX * digits[1:2, :]


def coefficients(dots, match, sharp, shift):
    logits = sharp * dots + shift
    probs = 1.0 / (1.0 + jnp.exp(-logits))
    return (sharp * (probs - jnp.where(match, 1.0, 0.0))).astype(jnp.bfloat16)


def dot_rows(left, right):
    return lax.dot_general(left, right, (((1,), (1,)), ((), ())), preferred_element_type=jnp.float32)


def text_part_body(rows, own_text, has_start, chips, *refs):
    sharp, shift = refs[0][0:1, 0:1], refs[0][1:2, 0:1]
    text, speech = refs[1][...], refs[2]
    total = refs[3][...] if has_start else None
    outs = refs[4 if has_start else 3 :]
    groups = lax.axis_size("group")
    members = lax.axis_size("member")
    group = lax.axis_index("group")
    member = lax.axis_index("member")
    table = speech[chips * rows :, :].astype(jnp.float32)
    for first in range(0, chips * rows, CHUNK):
        chunk = speech[first : min(first + CHUNK, chips * rows), :]
        marks = marks_of(table, first // CHUNK, chunk.shape[0])
        iota = lax.broadcasted_iota(jnp.int32, (own_text, chunk.shape[0]), 0)
        ids = [((group ^ k) * members + member) * own_text + iota for k in range(groups)]
        match = jnp.concatenate(ids, axis=0).astype(jnp.float32) == marks
        coef = coefficients(dot_rows(text, chunk), match, sharp, shift)
        part = jnp.dot(coef, chunk, preferred_element_type=jnp.float32)
        total = part if total is None else total + part
    row, at = 0, 0
    for out in outs:
        out[...] = total[row : row + out.shape[0], at : at + out.shape[1]]
        at += out.shape[1]
        if at == total.shape[1]:
            row, at = row + out.shape[0], 0


def speech_part_body(rows, own_text, has_start, chips, masks, outputs, *refs):
    sharp, shift, speech = refs[0][0:1, 0:1], refs[0][1:2, 0:1], refs[1]
    total = refs[2][...] if has_start else None
    texts, outs = list(refs[3 if has_start else 2 : -outputs]), refs[-outputs:]
    groups = lax.axis_size("group")
    members = lax.axis_size("member")
    group = lax.axis_index("group")
    member = lax.axis_index("member")
    table = speech[chips * rows :, :].astype(jnp.float32)
    marks = jnp.broadcast_to(marks_of(table, 0, rows), (rows, rows)).T[:, 0:1]
    block = speech[0:rows, :]
    column = groups * own_text
    lane = lax.broadcasted_iota(jnp.int32, (1, column), 1)
    base = (group ^ (lane // own_text)) * members * own_text + lane % own_text
    for mask in masks:
        pieces = [texts.pop(0)[...]]
        while sum(v.shape[0] for v in pieces) < column:
            pieces.append(texts.pop(0)[...])
        text = jnp.concatenate(pieces, axis=0)
        ids = (base + (member ^ (2 * mask)) * own_text).astype(jnp.float32)
        coef = coefficients(dot_rows(block, text), marks == ids, sharp, shift)
        part = jnp.dot(coef, text, preferred_element_type=jnp.float32)
        total = part if total is None else total + part
    for k, out in enumerate(outs):
        out[...] = total[k * out.shape[0] : (k + 1) * out.shape[0], :]


def add_sides_body(*refs):
    out = refs[-1]
    sides = [ref for ref in refs[:-1] if ref.shape != out.shape]
    whole = [ref for ref in refs[:-1] if ref.shape == out.shape]
    at = 0
    for ref in sides:
        columns = slice(at, at + ref.shape[1])
        total = ref[...]
        for other in whole:
            total = total + other[:, columns]
        out[:, columns] = total
        at += ref.shape[1]


def sum_body(*refs):
    total = refs[0][...]
    for ref in refs[1:-1]:
        total = total + ref[...]
    refs[-1][...] = total


def project(values, back):
    heading, norms = direction(values)
    along = jnp.sum(heading * back, axis=-1, keepdims=True)
    return (back - heading * along) / norms


def finish_body(pieces, audio, home, *refs):
    backs, (sentence, text_back) = refs[:pieces], refs[pieces : pieces + 2]
    speech_grad, text_grad, speech_held, text_held, done = refs[pieces + 2 :]
    text_held[...] = project(sentence[...], text_back[...])
    copies = [pltpu.make_async_copy(text_held, text_grad, done.at[0])]
    copies[0].start()
    for i, back in enumerate(backs):
        size = back.shape[0]
        some = slice(i * size, (i + 1) * size)
        speech_held[some, :] = project(audio[some, :], home[some, :] + back[...])
        copy = pltpu.make_async_copy(
            speech_held.at[some, :], speech_grad.at[some, :], done.at[i + 1]
        )
        copy.start()
        copies.append(copy)
    for copy in copies:
        copy.wait()


def shards(audio_vectors, sentence_vectors, matching_indices, sharpness_array, offset_term):
    members = lax.axis_size("member")
    groups = lax.axis_size("group")
    chips = members // 2
    rows, width = audio_vectors.shape
    own_text = sentence_vectors.shape[0]
    label = matching_indices.reshape(1, rows)
    scalars = jnp.concatenate(
        [jnp.broadcast_to(v[:, None], (1, 128)) for v in (sharpness_array, offset_term)], axis=0
    )

    def bf16(*shape):
        return jax.ShapeDtypeStruct(shape, jnp.bfloat16)

    def f32(*shape):
        return jax.ShapeDtypeStruct(shape, jnp.float32)

    arguments = [audio_vectors, sentence_vectors, label]
    speech_own, text_own, audio, sentence = pl.pallas_call(
        prepare_body,
        out_shape=[
            bf16(rows + MARK_ROWS, width),
            bf16(own_text, width),
            bf16(rows, width),
            bf16(own_text, width),
        ],
        in_specs=[pl.BlockSpec(memory_space=pltpu.HBM)] * 3,
        out_specs=[pl.BlockSpec(memory_space=pltpu.VMEM)] * 4,
        scratch_shapes=[pltpu.VMEM((1, rows), jnp.int32), pltpu.SemaphoreType.DMA((3,))],
        compiler_params=pltpu.CompilerParams(vmem_limit_bytes=8 << 20),
        name="unit_rows",
    )(*[pltpu.with_memory_space_constraint(v, pltpu.HBM) for v in arguments])

    def passed_on(block):
        return call(join_body, bf16(own_text, width), [block], (), 1 << 29, name="pass_on")

    text_blocks = [text_own] + [None] * (groups - 1)
    for k in [1 << i for i in reversed(range(groups.bit_length() - 1))]:
        for j in range(0, groups, 2 * k):
            came = exchanged(text_blocks[j], "group", k)
            text_blocks[j + k] = passed_on(came) if k > 1 else came
    square = chips == 4
    masks = [1, 2] if square else list(range(1, chips))

    def far_halves(near, middle, after=()):
        pairs = []
        for i, (source, k) in enumerate(zip(near[::-1], masks)):
            half = call(
                functools.partial(cut_body, i * middle), bf16(middle, width), [source], after, name="cut"
            )
            pairs.append((half, exchanged(half, "member", 2 * k)))
        return pairs

    speech_blocks = [exchanged(speech_own, "member", 2 * k) for k in reversed(range(1, chips))]
    column = groups * own_text
    text, speech = call(
        functools.partial(join_both_body, groups),
        [bf16(column, width), bf16(chips * rows + mark_rows_of(chips, rows), width)],
        [*text_blocks, speech_own, *speech_blocks[::-1]],
        (scalars,),
        name="join_rows",
    )
    other = exchanged(speech, "member", 1)
    text_near = [exchanged(text, "member", 2 * k) for k in masks]

    temporary = 4 * column * (6 * CHUNK + 3 * width)

    def text_part(outs, speech, start):
        body = functools.partial(text_part_body, rows, own_text, bool(start), chips)
        work = 4 * column * chips * rows * width
        return call(body, outs, [scalars, text, speech, *start], (), work, temporary, "text_part")

    half = text_part([f32(column, width)], speech, [])
    sides = 2
    side = f32(own_text, width // sides)
    outs = [f32(own_text, width)] * (groups // 2) + [side] * (groups // 2 * sides)
    parts = list(text_part(outs, other, half))
    far = [parts[groups // 2 + i * sides :][:sides] for i in range(groups // 2)]

    text_far = []
    bit = 1
    while bit < groups // 2:
        for k in reversed(range(bit, groups // 2, 2 * bit)):
            came = [exchanged(v, "group", bit) for v in far[k]]
            sums = []
            for mine, v in zip(far[k - bit], came):
                if sums and square and not text_far:
                    text_far = far_halves(text_near, column // 2, tuple(sums))
                    gate = tuple(half for half, _ in text_far)
                else:
                    gate = ()
                sums.append(call(sum_body, side, [mine, v], gate, name="sum_near"))
            far[k - bit] = sums
        bit *= 2
    if square:
        text_far = [came for _, came in text_far]
    from_far = [exchanged(v, "group", groups // 2) for v in far[0]]
    from_near = [exchanged(parts[k], "group", k) for k in range(1, groups // 2)]

    def speech_part(speech, start, columns, texts, after=(), pieces=1):
        body = functools.partial(
            speech_part_body, rows, own_text, bool(start), chips, columns, pieces
        )
        work = 40 * rows * column * len(columns) * width
        outs = [f32(rows // pieces, width)] * pieces
        operands = [scalars, speech, *start, *texts]
        return call(body, outs, operands, after, work, temporary, "speech_part")

    near = [[0, *masks], [text, *text_near], tuple(far[0])]
    if square:
        away = speech_part(other, [], *near)
        home = speech_part(speech, [], *near)
        away = speech_part(other, away, [3], text_far, pieces=2)
        home = speech_part(speech, home, [3], text_far)
    else:
        away = speech_part(other, [], *near, pieces=2)
        home = speech_part(speech, [], *near)
    back = [exchanged(piece, "member", 1) for piece in away]
    text_back = call(
        add_sides_body,
        f32(own_text, width),
        [*from_far, *from_near, parts[0]],
        tuple(home),
        EARLY,
        name="text_sum",
    )
    results = [f32(rows, width), f32(own_text, width)]
    speech_grad, text_grad = pl.pallas_call(
        functools.partial(finish_body, len(back)),
        out_shape=results,
        in_specs=[pl.BlockSpec(memory_space=pltpu.VMEM)] * (4 + len(back)),
        out_specs=[pl.BlockSpec(memory_space=pltpu.HBM)] * 2,
        scratch_shapes=[
            *[pltpu.VMEM(v.shape, v.dtype) for v in results],
            pltpu.SemaphoreType.DMA((1 + len(back),)),
        ],
        compiler_params=pltpu.CompilerParams(vmem_limit_bytes=8 << 20),
        name="finish",
    )(audio, *home, *back, sentence, text_back)
    return (speech_grad, text_grad)


def solution(mesh):
    in_specs = (
        P(("group", "member"), None),
        P(("group", "member"), None),
        P(("group", "member")),
        P(),
        P(),
    )
    out_specs = (P(("group", "member"), None), P(("group", "member"), None))
    return jax.shard_map(shards, mesh=mesh, in_specs=in_specs, out_specs=out_specs, check_vma=False)
```

```python
import functools
import jax
import jax.numpy as jnp
from jax import lax
from jax.experimental import pallas as pl
from jax.experimental.pallas import tpu as pltpu
from jax.sharding import PartitionSpec as P

MARK_ROWS = 8
TILE_ROWS = 16
RADIX = 256
CHUNK = 512
EARLY = 1 << 33


def exchanged(value, axis, mask):
    size = lax.axis_size(axis)
    return lax.ppermute(value, axis, [(i, i ^ mask) for i in range(size)])


def total_bytes(values):
    return sum(v.size * v.dtype.itemsize for v in jax.tree.leaves(values))


def call(body, out_shape, operands, after=(), flops=0, temporary=0, name="kernel"):
    specs = [pl.BlockSpec(memory_space=pltpu.VMEM) for _ in operands]
    specs += [pl.BlockSpec(memory_space=pl.ANY) for _ in after]
    used = len(operands)

    def whole(*refs):
        body(*refs[:used], *refs[used + len(after) :])

    moved = total_bytes(operands) + total_bytes(out_shape)
    return pl.pallas_call(
        whole,
        out_shape=out_shape,
        in_specs=specs,
        out_specs=jax.tree.map(lambda _: pl.BlockSpec(memory_space=pltpu.VMEM), out_shape),
        compiler_params=pltpu.CompilerParams(vmem_limit_bytes=(4 << 20) + 2 * moved + temporary),
        cost_estimate=pl.CostEstimate(flops=flops, bytes_accessed=moved, transcendentals=0),
        name=name,
    )(*operands, *after)


def direction(values):
    floats = values.astype(jnp.float32)
    norms = jnp.sqrt(jnp.sum(floats * floats, axis=-1, keepdims=True) + 1e-06)
    inverse = 1.0 / norms
    return floats * inverse, inverse


def prepare_body(*refs):
    sources, (speech, text) = refs[:3], refs[3:5]
    held, done = refs[5:8], refs[8]
    copies = [pltpu.make_async_copy(sources[i], held[i], done.at[i]) for i in range(3)]
    for copy in copies:
        copy.start()
    for copy in copies:
        copy.wait()
    audio, sentence, label = held
    rows = audio.shape[0]
    speech[0:rows, :] = direction(audio[...])[0].astype(jnp.bfloat16)
    text[...] = direction(sentence[...])[0].astype(jnp.bfloat16)
    number = label[...]
    digits = jnp.concatenate([number % RADIX, number // RADIX], axis=1).astype(jnp.float32)
    wide = jnp.concatenate(
        [digits, jnp.zeros((1, speech.shape[1] - 2 * rows), jnp.float32)], axis=1
    )
    speech[rows : rows + MARK_ROWS, :] = jnp.broadcast_to(
        wide, (MARK_ROWS, speech.shape[1])
    ).astype(jnp.bfloat16)


def join_body(*refs):
    out = refs[-1]
    at = 0
    for ref in refs[:-1]:
        out[at : at + ref.shape[0], :] = ref[...]
        at += ref.shape[0]


def digits_of(rows, block):
    digits = block[rows : rows + MARK_ROWS, 0 : 2 * rows].astype(jnp.float32)
    return digits[0:1, 0:rows], digits[0:1, rows : 2 * rows]


def mark_rows_of(chips, rows):
    chunks = -(-chips // (CHUNK // rows))
    return -(-2 * chunks // TILE_ROWS) * TILE_ROWS


def join_both_body(count, *refs):
    text, speech = refs[-2:]
    join_body(*refs[:count], text)
    blocks = refs[count:-2]
    rows = blocks[0].shape[0] - MARK_ROWS
    width = speech.shape[1]
    for k, ref in enumerate(blocks):
        speech[k * rows : (k + 1) * rows, :] = ref[0:rows, :]
    per = CHUNK // rows
    height = mark_rows_of(len(blocks), rows)
    place = lax.broadcasted_iota(jnp.int32, (height, width), 0)
    table = jnp.zeros((height, width), jnp.float32)
    for chunk in range(0, len(blocks), per):
        both = [digits_of(rows, ref) for ref in blocks[chunk : chunk + per]]
        for i in range(2):
            parts = [digits[i] for digits in both]
            rest = width - rows * len(parts)
            line = jnp.concatenate([*parts, jnp.zeros((1, rest), jnp.float32)], axis=1)
            table = jnp.where(place == 2 * (chunk // per) + i, line, table)
    speech[len(blocks) * rows :, :] = table.astype(jnp.bfloat16)


def cut_body(first, source, out):
    out[...] = source[first : first + out.shape[0], :]


def marks_of(table, chunk, count):
    digits = table[2 * chunk : 2 * chunk + 2, 0:count]
    return digits[0:1, :] + RADIX * digits[1:2, :]


def coefficients(dots, match, sharp, shift):
    below = 1.0 + jnp.exp((-sharp) * dots - shift)
    probs = pl.reciprocal(below, approx=True)
    probs = probs * (2.0 - below * probs)
    return (sharp * jnp.where(match, probs - 1.0, probs)).astype(jnp.bfloat16)


def dot_rows(left, right):
    return lax.dot_general(left, right, (((1,), (1,)), ((), ())), preferred_element_type=jnp.float32)


def text_part_body(rows, own_text, has_start, chips, *refs):
    sharp, shift = refs[0][0:1, 0:1], refs[0][1:2, 0:1]
    text, speech = refs[1][...], refs[2]
    total = refs[3][...] if has_start else None
    outs = refs[4 if has_start else 3 :]
    groups = lax.axis_size("group")
    members = lax.axis_size("member")
    group = lax.axis_index("group")
    member = lax.axis_index("member")
    table = speech[chips * rows :, :].astype(jnp.float32)
    for first in range(0, chips * rows, CHUNK):
        chunk = speech[first : min(first + CHUNK, chips * rows), :]
        marks = marks_of(table, first // CHUNK, chunk.shape[0])
        iota = lax.broadcasted_iota(jnp.int32, (own_text, 1), 0)
        ids = [((group ^ k) * members + member) * own_text + iota for k in range(groups)]
        match = jnp.concatenate(ids, axis=0).astype(jnp.float32) == marks
        coef = coefficients(dot_rows(text, chunk), match, sharp, shift)
        part = jnp.dot(coef, chunk, preferred_element_type=jnp.float32)
        total = part if total is None else total + part
    row, at = 0, 0
    for out in outs:
        out[...] = total[row : row + out.shape[0], at : at + out.shape[1]]
        at += out.shape[1]
        if at == total.shape[1]:
            row, at = row + out.shape[0], 0


def speech_part_body(rows, own_text, has_start, chips, masks, *refs):
    sharp, shift, speech = refs[0][0:1, 0:1], refs[0][1:2, 0:1], refs[1]
    total = refs[2][...] if has_start else None
    texts, out = list(refs[3 if has_start else 2 : -1]), refs[-1]
    groups = lax.axis_size("group")
    members = lax.axis_size("member")
    group = lax.axis_index("group")
    member = lax.axis_index("member")
    table = speech[chips * rows :, :].astype(jnp.float32)
    marks = jnp.broadcast_to(marks_of(table, 0, rows), (rows, rows)).T[:, 0:1]
    block = speech[0:rows, :]
    column = groups * own_text
    lane = lax.broadcasted_iota(jnp.int32, (1, column), 1)
    base = (group ^ (lane // own_text)) * members * own_text + lane % own_text
    for mask in masks:
        pieces = [texts.pop(0)[...]]
        while sum(v.shape[0] for v in pieces) < column:
            pieces.append(texts.pop(0)[...])
        text = jnp.concatenate(pieces, axis=0)
        ids = (base + (member ^ (2 * mask)) * own_text).astype(jnp.float32)
        coef = coefficients(dot_rows(block, text), marks == ids, sharp, shift)
        part = jnp.dot(coef, text, preferred_element_type=jnp.float32)
        total = part if total is None else total + part
    out[...] = total


def add_sides_body(*refs):
    out = refs[-1]
    sides = [ref for ref in refs[:-1] if ref.shape != out.shape]
    whole = [ref for ref in refs[:-1] if ref.shape == out.shape]
    at = 0
    for ref in sides:
        columns = slice(at, at + ref.shape[1])
        total = ref[...]
        for other in whole:
            total = total + other[:, columns]
        out[:, columns] = total
        at += ref.shape[1]


def sum_body(*refs):
    total = refs[0][...]
    for ref in refs[1:-1]:
        total = total + ref[...]
    refs[-1][...] = total


def project(values, back):
    heading, inverse = direction(values)
    along = jnp.sum(heading * back, axis=-1, keepdims=True)
    return (back - heading * along) * inverse


def finish_body(
    audio, home, back, sentence, text_back, speech_grad, text_grad, speech_held, text_held, done
):
    text_held[...] = project(sentence[...], text_back[...])
    copies = [pltpu.make_async_copy(text_held, text_grad, done.at[0])]
    copies[0].start()
    size = audio.shape[0] // 2
    for i in range(2):
        some = slice(i * size, (i + 1) * size)
        speech_held[some, :] = project(audio[some, :], home[some, :] + back[some, :])
        copy = pltpu.make_async_copy(
            speech_held.at[some, :], speech_grad.at[some, :], done.at[i + 1]
        )
        copy.start()
        copies.append(copy)
    for copy in copies:
        copy.wait()


def shards(audio_vectors, sentence_vectors, matching_indices, sharpness_array, offset_term):
    members = lax.axis_size("member")
    groups = lax.axis_size("group")
    chips = members // 2
    rows, width = audio_vectors.shape
    own_text = sentence_vectors.shape[0]
    label = matching_indices.reshape(1, rows)
    scalars = jnp.concatenate(
        [jnp.broadcast_to(v[:, None], (1, 128)) for v in (sharpness_array, offset_term)], axis=0
    )

    def bf16(*shape):
        return jax.ShapeDtypeStruct(shape, jnp.bfloat16)

    def f32(*shape):
        return jax.ShapeDtypeStruct(shape, jnp.float32)

    arguments = [audio_vectors, sentence_vectors, label]
    speech_own, text_own, audio, sentence = pl.pallas_call(
        prepare_body,
        out_shape=[
            bf16(rows + MARK_ROWS, width),
            bf16(own_text, width),
            bf16(rows, width),
            bf16(own_text, width),
        ],
        in_specs=[pl.BlockSpec(memory_space=pltpu.HBM)] * 3,
        out_specs=[pl.BlockSpec(memory_space=pltpu.VMEM)] * 4,
        scratch_shapes=[pltpu.VMEM((1, rows), jnp.int32), pltpu.SemaphoreType.DMA((3,))],
        compiler_params=pltpu.CompilerParams(vmem_limit_bytes=8 << 20),
        name="unit_rows",
    )(*[pltpu.with_memory_space_constraint(v, pltpu.HBM) for v in arguments])

    def passed_on(block):
        return call(join_body, bf16(own_text, width), [block], (), 1 << 29, name="pass_on")

    text_blocks = [text_own] + [None] * (groups - 1)
    for k in [1 << i for i in reversed(range(groups.bit_length() - 1))]:
        for j in range(0, groups, 2 * k):
            came = exchanged(text_blocks[j], "group", k)
            text_blocks[j + k] = passed_on(came) if k > 1 else came
    square = chips == 4
    masks = [1, 2] if square else list(range(1, chips))

    def far_halves(near, middle, after=()):
        pairs = []
        for i, (source, k) in enumerate(zip(near[::-1], masks)):
            half = call(
                functools.partial(cut_body, i * middle), bf16(middle, width), [source], after, name="cut"
            )
            pairs.append((half, exchanged(half, "member", 2 * k)))
        return pairs

    speech_blocks = [exchanged(speech_own, "member", 2 * k) for k in reversed(range(1, chips))]
    column = groups * own_text
    text, speech = call(
        functools.partial(join_both_body, groups),
        [bf16(column, width), bf16(chips * rows + mark_rows_of(chips, rows), width)],
        [*text_blocks, speech_own, *speech_blocks[::-1]],
        (scalars,),
        name="join_rows",
    )
    other = exchanged(speech, "member", 1)
    text_near = [exchanged(text, "member", 2 * k) for k in masks]

    temporary = 4 * column * (6 * CHUNK + 3 * width)

    def text_part(outs, speech, start):
        body = functools.partial(text_part_body, rows, own_text, bool(start), chips)
        work = 4 * column * chips * rows * width
        return call(body, outs, [scalars, text, speech, *start], (), work, temporary, "text_part")

    half = text_part([f32(column, width)], speech, [])
    sides = 2
    side = f32(own_text, width // sides)
    outs = [f32(own_text, width)] * (groups // 2) + [side] * (groups // 2 * sides)
    parts = list(text_part(outs, other, half))
    far = [parts[groups // 2 + i * sides :][:sides] for i in range(groups // 2)]

    text_far = []
    bit = 1
    while bit < groups // 2:
        for k in reversed(range(bit, groups // 2, 2 * bit)):
            came = [exchanged(v, "group", bit) for v in far[k]]
            sums = []
            for mine, v in zip(far[k - bit], came):
                if sums and square and not text_far:
                    text_far = far_halves(text_near, column // 2, tuple(sums))
                    gate = tuple(half for half, _ in text_far)
                else:
                    gate = ()
                sums.append(call(sum_body, side, [mine, v], gate, name="sum_near"))
            far[k - bit] = sums
        bit *= 2
    if square:
        text_far = [came for _, came in text_far]
    from_far = [exchanged(v, "group", groups // 2) for v in far[0]]
    from_near = [exchanged(parts[k], "group", k) for k in range(1, groups // 2)]

    def speech_part(speech, start, columns, texts, after=()):
        body = functools.partial(speech_part_body, rows, own_text, bool(start), chips, columns)
        work = 40 * rows * column * len(columns) * width
        operands = [scalars, speech, *start, *texts]
        return call(body, [f32(rows, width)], operands, after, work, temporary, "speech_part")

    near = [[0, *masks], [text, *text_near], tuple(far[0])]
    if square:
        away = speech_part(other, [], *near)
        home = speech_part(speech, [], *near)
        away = speech_part(other, away, [3], text_far)
        home = speech_part(speech, home, [3], text_far)
    else:
        away = speech_part(other, [], *near)
        home = speech_part(speech, [], *near)
    back = exchanged(away[0], "member", 1)
    text_back = call(
        add_sides_body,
        f32(own_text, width),
        [*from_far, *from_near, parts[0]],
        tuple(home),
        EARLY,
        name="text_sum",
    )
    results = [f32(rows, width), f32(own_text, width)]
    speech_grad, text_grad = pl.pallas_call(
        finish_body,
        out_shape=results,
        in_specs=[pl.BlockSpec(memory_space=pltpu.VMEM)] * 5,
        out_specs=[pl.BlockSpec(memory_space=pltpu.HBM)] * 2,
        scratch_shapes=[
            *[pltpu.VMEM(v.shape, v.dtype) for v in results],
            pltpu.SemaphoreType.DMA((3,)),
        ],
        compiler_params=pltpu.CompilerParams(vmem_limit_bytes=8 << 20),
        name="finish",
    )(audio, *home, back, sentence, text_back)
    return (speech_grad, text_grad)


def solution(mesh):
    in_specs = (
        P(("group", "member"), None),
        P(("group", "member"), None),
        P(("group", "member")),
        P(),
        P(),
    )
    out_specs = (P(("group", "member"), None), P(("group", "member"), None))
    return jax.shard_map(shards, mesh=mesh, in_specs=in_specs, out_specs=out_specs, check_vma=False)
```

```python
import functools
import jax
import jax.numpy as jnp
from jax import lax
from jax.experimental import pallas as pl
from jax.experimental.pallas import tpu as pltpu
from jax.sharding import PartitionSpec as P

MARK_ROWS = 8
TILE_ROWS = 16
PIECE_ROWS = 32
RADIX = 256
CHUNK = 512
EARLY = 1 << 33


def exchanged(value, axis, mask):
    size = lax.axis_size(axis)
    return lax.ppermute(value, axis, [(i, i ^ mask) for i in range(size)])


def total_bytes(values):
    return sum(v.size * v.dtype.itemsize for v in jax.tree.leaves(values))


def call(body, out_shape, operands, after=(), flops=0, temporary=0, name="kernel"):
    specs = [pl.BlockSpec(memory_space=pltpu.VMEM) for _ in operands]
    specs += [pl.BlockSpec(memory_space=pl.ANY) for _ in after]
    used = len(operands)

    def whole(*refs):
        body(*refs[:used], *refs[used + len(after) :])

    moved = total_bytes(operands) + total_bytes(out_shape)
    return pl.pallas_call(
        whole,
        out_shape=out_shape,
        in_specs=specs,
        out_specs=jax.tree.map(lambda _: pl.BlockSpec(memory_space=pltpu.VMEM), out_shape),
        compiler_params=pltpu.CompilerParams(vmem_limit_bytes=(4 << 20) + 2 * moved + temporary),
        cost_estimate=pl.CostEstimate(flops=flops, bytes_accessed=moved, transcendentals=0),
        name=name,
    )(*operands, *after)


def direction(values):
    floats = values.astype(jnp.float32)
    norms = jnp.sqrt(jnp.sum(floats * floats, axis=-1, keepdims=True) + 1e-06)
    return floats / norms, norms


def prepare_body(*refs):
    sources, (speech, text) = refs[:3], refs[3:5]
    held, done = refs[5:8], refs[8]
    pieces = []
    for source, target, out in zip(sources, held, (speech, text, None)):
        size = source.shape[0] if out is None else PIECE_ROWS
        for first in range(0, source.shape[0], size):
            pieces.append((source, target, out, slice(first, first + size)))
    copies = [
        pltpu.make_async_copy(source.at[some, :], target.at[some, :], done.at[i])
        for i, (source, target, _, some) in enumerate(pieces)
    ]
    order = sorted(range(len(pieces)), key=lambda i: (pieces[i][2] is speech, i))
    for i in order:
        copies[i].start()
    for i in order:
        copies[i].wait()
        _, target, out, some = pieces[i]
        if out is not None:
            out[some, :] = direction(target[some, :])[0].astype(jnp.bfloat16)
    rows = held[0].shape[0]
    number = held[2][...]
    digits = jnp.concatenate([number % RADIX, number // RADIX], axis=1).astype(jnp.float32)
    wide = jnp.concatenate(
        [digits, jnp.zeros((1, speech.shape[1] - 2 * rows), jnp.float32)], axis=1
    )
    speech[rows : rows + MARK_ROWS, :] = jnp.broadcast_to(
        wide, (MARK_ROWS, speech.shape[1])
    ).astype(jnp.bfloat16)


def join_body(*refs):
    out = refs[-1]
    at = 0
    for ref in refs[:-1]:
        out[at : at + ref.shape[0], :] = ref[...]
        at += ref.shape[0]


def digits_of(rows, block):
    digits = block[rows : rows + MARK_ROWS, 0 : 2 * rows].astype(jnp.float32)
    return digits[0:1, 0:rows], digits[0:1, rows : 2 * rows]


def mark_rows_of(chips, rows):
    chunks = -(-chips // (CHUNK // rows))
    return -(-2 * chunks // TILE_ROWS) * TILE_ROWS


def join_both_body(count, *refs):
    text, speech = refs[-2:]
    join_body(*refs[:count], text)
    blocks = refs[count:-2]
    rows = blocks[0].shape[0] - MARK_ROWS
    width = speech.shape[1]
    for k, ref in enumerate(blocks):
        speech[k * rows : (k + 1) * rows, :] = ref[0:rows, :]
    per = CHUNK // rows
    height = mark_rows_of(len(blocks), rows)
    place = lax.broadcasted_iota(jnp.int32, (height, width), 0)
    table = jnp.zeros((height, width), jnp.float32)
    for chunk in range(0, len(blocks), per):
        both = [digits_of(rows, ref) for ref in blocks[chunk : chunk + per]]
        for i in range(2):
            parts = [digits[i] for digits in both]
            rest = width - rows * len(parts)
            line = jnp.concatenate([*parts, jnp.zeros((1, rest), jnp.float32)], axis=1)
            table = jnp.where(place == 2 * (chunk // per) + i, line, table)
    speech[len(blocks) * rows :, :] = table.astype(jnp.bfloat16)


def cut_body(first, source, out):
    out[...] = source[first : first + out.shape[0], :]


def marks_of(table, chunk, count):
    digits = table[2 * chunk : 2 * chunk + 2, 0:count]
    return digits[0:1, :] + RADIX * digits[1:2, :]


def coefficients(dots, match, sharp, shift):
    logits = sharp * dots + shift
    probs = 1.0 / (1.0 + jnp.exp(-logits))
    return (sharp * (probs - jnp.where(match, 1.0, 0.0))).astype(jnp.bfloat16)


def dot_rows(left, right):
    return lax.dot_general(left, right, (((1,), (1,)), ((), ())), preferred_element_type=jnp.float32)


def text_part_body(rows, own_text, has_start, chips, *refs):
    sharp, shift = refs[0][0:1, 0:1], refs[0][1:2, 0:1]
    text, speech = refs[1][...], refs[2]
    total = refs[3][...] if has_start else None
    outs = refs[4 if has_start else 3 :]
    groups = lax.axis_size("group")
    members = lax.axis_size("member")
    group = lax.axis_index("group")
    member = lax.axis_index("member")
    table = speech[chips * rows :, :].astype(jnp.float32)
    for first in range(0, chips * rows, CHUNK):
        chunk = speech[first : min(first + CHUNK, chips * rows), :]
        marks = marks_of(table, first // CHUNK, chunk.shape[0])
        iota = lax.broadcasted_iota(jnp.int32, (own_text, chunk.shape[0]), 0)
        ids = [((group ^ k) * members + member) * own_text + iota for k in range(groups)]
        match = jnp.concatenate(ids, axis=0).astype(jnp.float32) == marks
        coef = coefficients(dot_rows(text, chunk), match, sharp, shift)
        part = jnp.dot(coef, chunk, preferred_element_type=jnp.float32)
        total = part if total is None else total + part
    row, at = 0, 0
    for out in outs:
        out[...] = total[row : row + out.shape[0], at : at + out.shape[1]]
        at += out.shape[1]
        if at == total.shape[1]:
            row, at = row + out.shape[0], 0


def speech_part_body(rows, own_text, has_start, chips, masks, outputs, *refs):
    sharp, shift, speech = refs[0][0:1, 0:1], refs[0][1:2, 0:1], refs[1]
    total = refs[2][...] if has_start else None
    texts, outs = list(refs[3 if has_start else 2 : -outputs]), refs[-outputs:]
    groups = lax.axis_size("group")
    members = lax.axis_size("member")
    group = lax.axis_index("group")
    member = lax.axis_index("member")
    table = speech[chips * rows :, :].astype(jnp.float32)
    marks = jnp.broadcast_to(marks_of(table, 0, rows), (rows, rows)).T[:, 0:1]
    block = speech[0:rows, :]
    column = groups * own_text
    lane = lax.broadcasted_iota(jnp.int32, (1, column), 1)
    base = (group ^ (lane // own_text)) * members * own_text + lane % own_text
    for mask in masks:
        pieces = [texts.pop(0)[...]]
        while sum(v.shape[0] for v in pieces) < column:
            pieces.append(texts.pop(0)[...])
        text = jnp.concatenate(pieces, axis=0)
        ids = (base + (member ^ (2 * mask)) * own_text).astype(jnp.float32)
        coef = coefficients(dot_rows(block, text), marks == ids, sharp, shift)
        part = jnp.dot(coef, text, preferred_element_type=jnp.float32)
        total = part if total is None else total + part
    for k, out in enumerate(outs):
        out[...] = total[k * out.shape[0] : (k + 1) * out.shape[0], :]


def add_sides_body(*refs):
    out = refs[-1]
    sides = [ref for ref in refs[:-1] if ref.shape != out.shape]
    whole = [ref for ref in refs[:-1] if ref.shape == out.shape]
    at = 0
    for ref in sides:
        columns = slice(at, at + ref.shape[1])
        total = ref[...]
        for other in whole:
            total = total + other[:, columns]
        out[:, columns] = total
        at += ref.shape[1]


def sum_body(*refs):
    total = refs[0][...]
    for ref in refs[1:-1]:
        total = total + ref[...]
    refs[-1][...] = total


def project(values, back):
    heading, norms = direction(values)
    along = jnp.sum(heading * back, axis=-1, keepdims=True)
    return (back - heading * along) / norms


def finish_body(pieces, audio, home, *refs):
    backs, (sentence, text_back) = refs[:pieces], refs[pieces : pieces + 2]
    speech_grad, text_grad, speech_held, text_held, done = refs[pieces + 2 :]
    text_held[...] = project(sentence[...], text_back[...])
    copies = [pltpu.make_async_copy(text_held, text_grad, done.at[0])]
    copies[0].start()
    for i, back in enumerate(backs):
        size = back.shape[0]
        some = slice(i * size, (i + 1) * size)
        speech_held[some, :] = project(audio[some, :], home[some, :] + back[...])
        copy = pltpu.make_async_copy(
            speech_held.at[some, :], speech_grad.at[some, :], done.at[i + 1]
        )
        copy.start()
        copies.append(copy)
    for copy in copies:
        copy.wait()


def shards(audio_vectors, sentence_vectors, matching_indices, sharpness_array, offset_term):
    members = lax.axis_size("member")
    groups = lax.axis_size("group")
    chips = members // 2
    rows, width = audio_vectors.shape
    own_text = sentence_vectors.shape[0]
    label = matching_indices.reshape(1, rows)
    scalars = jnp.concatenate(
        [jnp.broadcast_to(v[:, None], (1, 128)) for v in (sharpness_array, offset_term)], axis=0
    )

    def bf16(*shape):
        return jax.ShapeDtypeStruct(shape, jnp.bfloat16)

    def f32(*shape):
        return jax.ShapeDtypeStruct(shape, jnp.float32)

    arguments = [audio_vectors, sentence_vectors, label]
    speech_own, text_own, audio, sentence = pl.pallas_call(
        prepare_body,
        out_shape=[
            bf16(rows + MARK_ROWS, width),
            bf16(own_text, width),
            bf16(rows, width),
            bf16(own_text, width),
        ],
        in_specs=[pl.BlockSpec(memory_space=pltpu.HBM)] * 3,
        out_specs=[pl.BlockSpec(memory_space=pltpu.VMEM)] * 4,
        scratch_shapes=[
            pltpu.VMEM((1, rows), jnp.int32),
            pltpu.SemaphoreType.DMA(((rows + own_text) // PIECE_ROWS + 1,)),
        ],
        compiler_params=pltpu.CompilerParams(vmem_limit_bytes=8 << 20),
        name="unit_rows",
    )(*[pltpu.with_memory_space_constraint(v, pltpu.HBM) for v in arguments])

    def passed_on(block):
        return call(join_body, bf16(own_text, width), [block], (), 1 << 29, name="pass_on")

    text_blocks = [text_own] + [None] * (groups - 1)
    for k in [1 << i for i in reversed(range(groups.bit_length() - 1))]:
        for j in range(0, groups, 2 * k):
            came = exchanged(text_blocks[j], "group", k)
            text_blocks[j + k] = passed_on(came) if k > 1 else came
    square = chips == 4
    masks = [1, 2] if square else list(range(1, chips))

    def far_halves(near, middle, after=()):
        pairs = []
        for i, (source, k) in enumerate(zip(near[::-1], masks)):
            half = call(
                functools.partial(cut_body, i * middle), bf16(middle, width), [source], after, name="cut"
            )
            pairs.append((half, exchanged(half, "member", 2 * k)))
        return pairs

    speech_blocks = [exchanged(speech_own, "member", 2 * k) for k in reversed(range(1, chips))]
    column = groups * own_text
    text, speech = call(
        functools.partial(join_both_body, groups),
        [bf16(column, width), bf16(chips * rows + mark_rows_of(chips, rows), width)],
        [*text_blocks, speech_own, *speech_blocks],
        (scalars,),
        name="join_rows",
    )
    other = exchanged(speech, "member", 1)
    text_near = [exchanged(text, "member", 2 * k) for k in masks]

    temporary = 4 * column * (6 * CHUNK + 3 * width)

    def text_part(outs, speech, start):
        body = functools.partial(text_part_body, rows, own_text, bool(start), chips)
        work = 4 * column * chips * rows * width
        return call(body, outs, [scalars, text, speech, *start], (), work, temporary, "text_part")

    half = text_part([f32(column, width)], speech, [])
    sides = 2
    side = f32(own_text, width // sides)
    outs = [f32(own_text, width)] * (groups // 2) + [side] * (groups // 2 * sides)
    parts = list(text_part(outs, other, half))
    far = [parts[groups // 2 + i * sides :][:sides] for i in range(groups // 2)]

    text_far = []
    bit = 1
    while bit < groups // 2:
        for k in reversed(range(bit, groups // 2, 2 * bit)):
            came = [exchanged(v, "group", bit) for v in far[k]]
            sums = []
            for mine, v in zip(far[k - bit], came):
                if sums and square and not text_far:
                    text_far = far_halves(text_near, column // 2, tuple(sums))
                    gate = tuple(half for half, _ in text_far)
                else:
                    gate = ()
                sums.append(call(sum_body, side, [mine, v], gate, name="sum_near"))
            far[k - bit] = sums
        bit *= 2
    if square:
        text_far = [came for _, came in text_far]
    from_far = [exchanged(v, "group", groups // 2) for v in far[0]]
    from_near = [exchanged(parts[k], "group", k) for k in range(1, groups // 2)]

    def speech_part(speech, start, columns, texts, after=(), pieces=1):
        body = functools.partial(
            speech_part_body, rows, own_text, bool(start), chips, columns, pieces
        )
        work = 40 * rows * column * len(columns) * width
        outs = [f32(rows // pieces, width)] * pieces
        operands = [scalars, speech, *start, *texts]
        return call(body, outs, operands, after, work, temporary, "speech_part")

    near = [[0, *masks], [text, *text_near], tuple(far[0])]
    if square:
        away = speech_part(other, [], *near)
        home = speech_part(speech, [], *near)
        away = speech_part(other, away, [3], text_far, pieces=2)
        home = speech_part(speech, home, [3], text_far)
    else:
        away = speech_part(other, [], *near, pieces=2)
        home = speech_part(speech, [], *near)
    back = [exchanged(piece, "member", 1) for piece in away]
    text_back = call(
        add_sides_body,
        f32(own_text, width),
        [*from_far, *from_near, parts[0]],
        tuple(home),
        EARLY,
        name="text_sum",
    )
    results = [f32(rows, width), f32(own_text, width)]
    speech_grad, text_grad = pl.pallas_call(
        functools.partial(finish_body, len(back)),
        out_shape=results,
        in_specs=[pl.BlockSpec(memory_space=pltpu.VMEM)] * (4 + len(back)),
        out_specs=[pl.BlockSpec(memory_space=pltpu.HBM)] * 2,
        scratch_shapes=[
            *[pltpu.VMEM(v.shape, v.dtype) for v in results],
            pltpu.SemaphoreType.DMA((1 + len(back),)),
        ],
        compiler_params=pltpu.CompilerParams(vmem_limit_bytes=8 << 20),
        name="finish",
    )(audio, *home, *back, sentence, text_back)
    return (speech_grad, text_grad)


def solution(mesh):
    in_specs = (
        P(("group", "member"), None),
        P(("group", "member"), None),
        P(("group", "member")),
        P(),
        P(),
    )
    out_specs = (P(("group", "member"), None), P(("group", "member"), None))
    return jax.shard_map(shards, mesh=mesh, in_specs=in_specs, out_specs=out_specs, check_vma=False)
```

```python
import functools
import jax
import jax.numpy as jnp
from jax import lax
from jax.experimental import pallas as pl
from jax.experimental.pallas import tpu as pltpu
from jax.sharding import PartitionSpec as P

MARK_ROWS = 8
TILE_ROWS = 16
RADIX = 256
CHUNK = 512
EARLY = 1 << 33


def exchanged(value, axis, mask):
    size = lax.axis_size(axis)
    return lax.ppermute(value, axis, [(i, i ^ mask) for i in range(size)])


def total_bytes(values):
    return sum(v.size * v.dtype.itemsize for v in jax.tree.leaves(values))


def call(body, out_shape, operands, after=(), flops=0, temporary=0, name="kernel"):
    specs = [pl.BlockSpec(memory_space=pltpu.VMEM) for _ in operands]
    specs += [pl.BlockSpec(memory_space=pl.ANY) for _ in after]
    used = len(operands)

    def whole(*refs):
        body(*refs[:used], *refs[used + len(after) :])

    moved = total_bytes(operands) + total_bytes(out_shape)
    return pl.pallas_call(
        whole,
        out_shape=out_shape,
        in_specs=specs,
        out_specs=jax.tree.map(lambda _: pl.BlockSpec(memory_space=pltpu.VMEM), out_shape),
        compiler_params=pltpu.CompilerParams(vmem_limit_bytes=(4 << 20) + 2 * moved + temporary),
        cost_estimate=pl.CostEstimate(flops=flops, bytes_accessed=moved, transcendentals=0),
        name=name,
    )(*operands, *after)


def direction(values):
    floats = values.astype(jnp.float32)
    norms = jnp.sqrt(jnp.sum(floats * floats, axis=-1, keepdims=True) + 1e-06)
    return floats / norms, norms


def prepare_body(*refs):
    sources, (speech, text) = refs[:3], refs[3:5]
    held, done = refs[5:8], refs[8]
    copies = [pltpu.make_async_copy(sources[i], held[i], done.at[i]) for i in range(3)]
    for copy in copies:
        copy.start()
    for copy in copies:
        copy.wait()
    audio, sentence, label = held
    rows = audio.shape[0]
    speech[0:rows, :] = direction(audio[...])[0].astype(jnp.bfloat16)
    text[...] = direction(sentence[...])[0].astype(jnp.bfloat16)
    number = label[...]
    digits = jnp.concatenate([number % RADIX, number // RADIX], axis=1).astype(jnp.float32)
    wide = jnp.concatenate(
        [digits, jnp.zeros((1, speech.shape[1] - 2 * rows), jnp.float32)], axis=1
    )
    speech[rows : rows + MARK_ROWS, :] = jnp.broadcast_to(
        wide, (MARK_ROWS, speech.shape[1])
    ).astype(jnp.bfloat16)


def join_body(*refs):
    out = refs[-1]
    at = 0
    for ref in refs[:-1]:
        out[at : at + ref.shape[0], :] = ref[...]
        at += ref.shape[0]


def digits_of(rows, block):
    digits = block[rows : rows + MARK_ROWS, 0 : 2 * rows].astype(jnp.float32)
    return digits[0:1, 0:rows], digits[0:1, rows : 2 * rows]


def mark_rows_of(chips, rows):
    chunks = -(-chips // (CHUNK // rows))
    return -(-2 * chunks // TILE_ROWS) * TILE_ROWS


def join_both_body(count, *refs):
    text, speech = refs[-2:]
    join_body(*refs[:count], text)
    blocks = refs[count:-2]
    rows = blocks[0].shape[0] - MARK_ROWS
    width = speech.shape[1]
    for k, ref in enumerate(blocks):
        speech[k * rows : (k + 1) * rows, :] = ref[0:rows, :]
    per = CHUNK // rows
    height = mark_rows_of(len(blocks), rows)
    place = lax.broadcasted_iota(jnp.int32, (height, width), 0)
    table = jnp.zeros((height, width), jnp.float32)
    for chunk in range(0, len(blocks), per):
        both = [digits_of(rows, ref) for ref in blocks[chunk : chunk + per]]
        for i in range(2):
            parts = [digits[i] for digits in both]
            rest = width - rows * len(parts)
            line = jnp.concatenate([*parts, jnp.zeros((1, rest), jnp.float32)], axis=1)
            table = jnp.where(place == 2 * (chunk // per) + i, line, table)
    speech[len(blocks) * rows :, :] = table.astype(jnp.bfloat16)


def cut_body(first, source, out):
    out[...] = source[first : first + out.shape[0], :]


def marks_of(table, chunk, count):
    digits = table[2 * chunk : 2 * chunk + 2, 0:count]
    return digits[0:1, :] + RADIX * digits[1:2, :]


def coefficients(dots, match, sharp, shift):
    logits = sharp * dots + shift
    probs = 1.0 / (1.0 + jnp.exp(-logits))
    return (sharp * (probs - jnp.where(match, 1.0, 0.0))).astype(jnp.bfloat16)


def dot_rows(left, right):
    return lax.dot_general(left, right, (((1,), (1,)), ((), ())), preferred_element_type=jnp.float32)


def text_part_body(rows, own_text, has_start, chips, *refs):
    sharp, shift = refs[0][0:1, 0:1], refs[0][1:2, 0:1]
    text, speech = refs[1][...], refs[2]
    total = refs[3][...] if has_start else None
    outs = refs[4 if has_start else 3 :]
    groups = lax.axis_size("group")
    members = lax.axis_size("member")
    group = lax.axis_index("group")
    member = lax.axis_index("member")
    table = speech[chips * rows :, :].astype(jnp.float32)
    for first in range(0, chips * rows, CHUNK):
        chunk = speech[first : min(first + CHUNK, chips * rows), :]
        marks = marks_of(table, first // CHUNK, chunk.shape[0])
        iota = lax.broadcasted_iota(jnp.int32, (own_text, chunk.shape[0]), 0)
        ids = [((group ^ k) * members + member) * own_text + iota for k in range(groups)]
        match = jnp.concatenate(ids, axis=0).astype(jnp.float32) == marks
        coef = coefficients(dot_rows(text, chunk), match, sharp, shift)
        part = jnp.dot(coef, chunk, preferred_element_type=jnp.float32)
        total = part if total is None else total + part
    row, at = 0, 0
    for out in outs:
        out[...] = total[row : row + out.shape[0], at : at + out.shape[1]]
        at += out.shape[1]
        if at == total.shape[1]:
            row, at = row + out.shape[0], 0


def speech_part_body(rows, own_text, has_start, chips, masks, outputs, *refs):
    sharp, shift, speech = refs[0][0:1, 0:1], refs[0][1:2, 0:1], refs[1]
    total = refs[2][...] if has_start else None
    texts, outs = list(refs[3 if has_start else 2 : -outputs]), refs[-outputs:]
    groups = lax.axis_size("group")
    members = lax.axis_size("member")
    group = lax.axis_index("group")
    member = lax.axis_index("member")
    table = speech[chips * rows :, :].astype(jnp.float32)
    marks = jnp.broadcast_to(marks_of(table, 0, rows), (rows, rows)).T[:, 0:1]
    block = speech[0:rows, :]
    column = groups * own_text
    lane = lax.broadcasted_iota(jnp.int32, (1, column), 1)
    base = (group ^ (lane // own_text)) * members * own_text + lane % own_text
    for mask in masks:
        pieces = [texts.pop(0)[...]]
        while sum(v.shape[0] for v in pieces) < column:
            pieces.append(texts.pop(0)[...])
        text = jnp.concatenate(pieces, axis=0)
        ids = (base + (member ^ (2 * mask)) * own_text).astype(jnp.float32)
        coef = coefficients(dot_rows(block, text), marks == ids, sharp, shift)
        part = jnp.dot(coef, text, preferred_element_type=jnp.float32)
        total = part if total is None else total + part
    for k, out in enumerate(outs):
        out[...] = total[k * out.shape[0] : (k + 1) * out.shape[0], :]


def add_sides_body(*refs):
    out = refs[-1]
    sides = [ref for ref in refs[:-1] if ref.shape != out.shape]
    whole = [ref for ref in refs[:-1] if ref.shape == out.shape]
    at = 0
    for ref in sides:
        columns = slice(at, at + ref.shape[1])
        total = ref[...]
        for other in whole:
            total = total + other[:, columns]
        out[:, columns] = total
        at += ref.shape[1]


def sum_body(*refs):
    total = refs[0][...]
    for ref in refs[1:-1]:
        total = total + ref[...]
    refs[-1][...] = total


def project(values, back):
    heading, norms = direction(values)
    along = jnp.sum(heading * back, axis=-1, keepdims=True)
    return (back - heading * along) / norms


def finish_body(pieces, audio, home, *refs):
    backs, (sentence, text_back) = refs[:pieces], refs[pieces : pieces + 2]
    speech_grad, text_grad, speech_held, text_held, done = refs[pieces + 2 :]
    text_held[...] = project(sentence[...], text_back[...])
    copies = [pltpu.make_async_copy(text_held, text_grad, done.at[0])]
    copies[0].start()
    for i, back in enumerate(backs):
        size = back.shape[0]
        some = slice(i * size, (i + 1) * size)
        speech_held[some, :] = project(audio[some, :], home[some, :] + back[...])
        copy = pltpu.make_async_copy(
            speech_held.at[some, :], speech_grad.at[some, :], done.at[i + 1]
        )
        copy.start()
        copies.append(copy)
    for copy in copies:
        copy.wait()


def shards(audio_vectors, sentence_vectors, matching_indices, sharpness_array, offset_term):
    members = lax.axis_size("member")
    groups = lax.axis_size("group")
    chips = members // 2
    rows, width = audio_vectors.shape
    own_text = sentence_vectors.shape[0]
    label = matching_indices.reshape(1, rows)
    scalars = jnp.concatenate(
        [jnp.broadcast_to(v[:, None], (1, 128)) for v in (sharpness_array, offset_term)], axis=0
    )

    def bf16(*shape):
        return jax.ShapeDtypeStruct(shape, jnp.bfloat16)

    def f32(*shape):
        return jax.ShapeDtypeStruct(shape, jnp.float32)

    arguments = [audio_vectors, sentence_vectors, label]
    speech_own, text_own, audio, sentence = pl.pallas_call(
        prepare_body,
        out_shape=[
            bf16(rows + MARK_ROWS, width),
            bf16(own_text, width),
            bf16(rows, width),
            bf16(own_text, width),
        ],
        in_specs=[pl.BlockSpec(memory_space=pltpu.HBM)] * 3,
        out_specs=[pl.BlockSpec(memory_space=pltpu.VMEM)] * 4,
        scratch_shapes=[pltpu.VMEM((1, rows), jnp.int32), pltpu.SemaphoreType.DMA((3,))],
        compiler_params=pltpu.CompilerParams(vmem_limit_bytes=8 << 20),
        name="unit_rows",
    )(*[pltpu.with_memory_space_constraint(v, pltpu.HBM) for v in arguments])

    def passed_on(block):
        return call(join_body, bf16(own_text, width), [block], (), 1 << 29, name="pass_on")

    text_blocks = [text_own] + [None] * (groups - 1)
    for k in [1 << i for i in reversed(range(groups.bit_length() - 1))]:
        for j in range(0, groups, 2 * k):
            came = exchanged(text_blocks[j], "group", k)
            text_blocks[j + k] = passed_on(came) if k > 1 else came
    square = chips == 4
    masks = [1, 2] if square else list(range(1, chips))

    def far_halves(near, middle, after=()):
        pairs = []
        for i, (source, k) in enumerate(zip(near[::-1], masks)):
            half = call(
                functools.partial(cut_body, i * middle), bf16(middle, width), [source], after, name="cut"
            )
            pairs.append((half, exchanged(half, "member", 2 * k)))
        return pairs

    speech_blocks = [exchanged(speech_own, "member", 2 * k) for k in reversed(range(1, chips))]
    column = groups * own_text
    text, speech = call(
        functools.partial(join_both_body, groups),
        [bf16(column, width), bf16(chips * rows + mark_rows_of(chips, rows), width)],
        [*text_blocks, speech_own, *speech_blocks],
        (scalars,),
        name="join_rows",
    )
    other = exchanged(speech, "member", 1)
    text_near = [exchanged(text, "member", 2 * k) for k in masks]

    temporary = 4 * column * (6 * CHUNK + 3 * width)

    def text_part(outs, speech, start):
        body = functools.partial(text_part_body, rows, own_text, bool(start), chips)
        work = 4 * column * chips * rows * width
        return call(body, outs, [scalars, text, speech, *start], (), work, temporary, "text_part")

    half = text_part([f32(column, width)], speech, [])
    sides = 2
    side = f32(own_text, width // sides)
    outs = [f32(own_text, width)] * (groups // 2) + [side] * (groups // 2 * sides)
    parts = list(text_part(outs, other, half))
    far = [parts[groups // 2 + i * sides :][:sides] for i in range(groups // 2)]

    text_far = []
    bit = 1
    while bit < groups // 2:
        for k in reversed(range(bit, groups // 2, 2 * bit)):
            came = [exchanged(v, "group", bit) for v in far[k]]
            sums = []
            for mine, v in zip(far[k - bit], came):
                if sums and square and not text_far:
                    text_far = far_halves(text_near, column // 2, tuple(sums))
                    gate = tuple(half for half, _ in text_far)
                else:
                    gate = ()
                sums.append(call(sum_body, side, [mine, v], gate, name="sum_near"))
            far[k - bit] = sums
        bit *= 2
    if square:
        text_far = [came for _, came in text_far]
    from_far = [exchanged(v, "group", groups // 2) for v in far[0]]
    from_near = [exchanged(parts[k], "group", k) for k in range(1, groups // 2)]

    def speech_part(speech, start, columns, texts, after=(), pieces=1):
        body = functools.partial(
            speech_part_body, rows, own_text, bool(start), chips, columns, pieces
        )
        work = 40 * rows * column * len(columns) * width
        outs = [f32(rows // pieces, width)] * pieces
        operands = [scalars, speech, *start, *texts]
        return call(body, outs, operands, after, work, temporary, "speech_part")

    near = [[0, *masks], [text, *text_near], tuple(far[0])]
    if square:
        away = speech_part(other, [], *near)
        home = speech_part(speech, [], *near)
        away = speech_part(other, away, [3], text_far, pieces=2)
        home = speech_part(speech, home, [3], text_far)
    else:
        away = speech_part(other, [], *near, pieces=2)
        home = speech_part(speech, [], *near)
    back = [exchanged(piece, "member", 1) for piece in away]
    text_back = call(
        add_sides_body,
        f32(own_text, width),
        [*from_far, *from_near, parts[0]],
        tuple(home),
        EARLY,
        name="text_sum",
    )
    results = [f32(rows, width), f32(own_text, width)]
    speech_grad, text_grad = pl.pallas_call(
        functools.partial(finish_body, len(back)),
        out_shape=results,
        in_specs=[pl.BlockSpec(memory_space=pltpu.VMEM)] * (4 + len(back)),
        out_specs=[pl.BlockSpec(memory_space=pltpu.HBM)] * 2,
        scratch_shapes=[
            *[pltpu.VMEM(v.shape, v.dtype) for v in results],
            pltpu.SemaphoreType.DMA((1 + len(back),)),
        ],
        compiler_params=pltpu.CompilerParams(vmem_limit_bytes=8 << 20),
        name="finish",
    )(audio, *home, *back, sentence, text_back)
    return (speech_grad, text_grad)


def solution(mesh):
    in_specs = (
        P(("group", "member"), None),
        P(("group", "member"), None),
        P(("group", "member")),
        P(),
        P(),
    )
    out_specs = (P(("group", "member"), None), P(("group", "member"), None))
    return jax.shard_map(shards, mesh=mesh, in_specs=in_specs, out_specs=out_specs, check_vma=False)
```

```python
import functools
import jax
import jax.numpy as jnp
from jax import lax
from jax.experimental import pallas as pl
from jax.experimental.pallas import tpu as pltpu
from jax.sharding import PartitionSpec as P

MARK_ROWS = 8
TILE_ROWS = 16
RADIX = 256
CHUNK = 512
EARLY = 1 << 33


def exchanged(value, axis, mask):
    size = lax.axis_size(axis)
    return lax.ppermute(value, axis, [(i, i ^ mask) for i in range(size)])


def total_bytes(values):
    return sum(v.size * v.dtype.itemsize for v in jax.tree.leaves(values))


def call(body, out_shape, operands, after=(), flops=0, temporary=0, name="kernel"):
    specs = [pl.BlockSpec(memory_space=pltpu.VMEM) for _ in operands]
    specs += [pl.BlockSpec(memory_space=pl.ANY) for _ in after]
    used = len(operands)

    def whole(*refs):
        body(*refs[:used], *refs[used + len(after) :])

    moved = total_bytes(operands) + total_bytes(out_shape)
    return pl.pallas_call(
        whole,
        out_shape=out_shape,
        in_specs=specs,
        out_specs=jax.tree.map(lambda _: pl.BlockSpec(memory_space=pltpu.VMEM), out_shape),
        compiler_params=pltpu.CompilerParams(vmem_limit_bytes=(4 << 20) + 2 * moved + temporary),
        cost_estimate=pl.CostEstimate(flops=flops, bytes_accessed=moved, transcendentals=0),
        name=name,
    )(*operands, *after)


def direction(values):
    floats = values.astype(jnp.float32)
    norms = jnp.sqrt(jnp.sum(floats * floats, axis=-1, keepdims=True) + 1e-06)
    return floats / norms, norms


def prepare_body(*refs):
    sources, (speech, text) = refs[:3], refs[3:5]
    held, done = refs[5:8], refs[8]
    copies = [pltpu.make_async_copy(sources[i], held[i], done.at[i]) for i in range(3)]
    for copy in copies:
        copy.start()
    for copy in copies:
        copy.wait()
    audio, sentence, label = held
    rows = audio.shape[0]
    speech[0:rows, :] = direction(audio[...])[0].astype(jnp.bfloat16)
    text[...] = direction(sentence[...])[0].astype(jnp.bfloat16)
    number = label[...]
    digits = jnp.concatenate([number % RADIX, number // RADIX], axis=1).astype(jnp.float32)
    wide = jnp.concatenate(
        [digits, jnp.zeros((1, speech.shape[1] - 2 * rows), jnp.float32)], axis=1
    )
    speech[rows : rows + MARK_ROWS, :] = jnp.broadcast_to(
        wide, (MARK_ROWS, speech.shape[1])
    ).astype(jnp.bfloat16)


def join_body(*refs):
    out = refs[-1]
    at = 0
    for ref in refs[:-1]:
        out[at : at + ref.shape[0], :] = ref[...]
        at += ref.shape[0]


def digits_of(rows, block):
    digits = block[rows : rows + MARK_ROWS, 0 : 2 * rows].astype(jnp.float32)
    return digits[0:1, 0:rows], digits[0:1, rows : 2 * rows]


def mark_rows_of(chips, rows):
    chunks = -(-chips // (CHUNK // rows))
    return -(-2 * chunks // TILE_ROWS) * TILE_ROWS


def join_both_body(count, *refs):
    text, speech = refs[-2:]
    join_body(*refs[:count], text)
    blocks = refs[count:-2]
    rows = blocks[0].shape[0] - MARK_ROWS
    width = speech.shape[1]
    for k, ref in enumerate(blocks):
        speech[k * rows : (k + 1) * rows, :] = ref[0:rows, :]
    per = CHUNK // rows
    height = mark_rows_of(len(blocks), rows)
    place = lax.broadcasted_iota(jnp.int32, (height, width), 0)
    table = jnp.zeros((height, width), jnp.float32)
    for chunk in range(0, len(blocks), per):
        both = [digits_of(rows, ref) for ref in blocks[chunk : chunk + per]]
        for i in range(2):
            parts = [digits[i] for digits in both]
            rest = width - rows * len(parts)
            line = jnp.concatenate([*parts, jnp.zeros((1, rest), jnp.float32)], axis=1)
            table = jnp.where(place == 2 * (chunk // per) + i, line, table)
    speech[len(blocks) * rows :, :] = table.astype(jnp.bfloat16)


def cut_body(first, source, out):
    out[...] = source[first : first + out.shape[0], :]


def marks_of(table, chunk, count):
    digits = table[2 * chunk : 2 * chunk + 2, 0:count]
    return digits[0:1, :] + RADIX * digits[1:2, :]


def coefficients(dots, match, sharp, shift):
    logits = sharp * dots + shift
    probs = 1.0 / (1.0 + jnp.exp(-logits))
    return (sharp * (probs - jnp.where(match, 1.0, 0.0))).astype(jnp.bfloat16)


def dot_rows(left, right):
    return lax.dot_general(left, right, (((1,), (1,)), ((), ())), preferred_element_type=jnp.float32)


def text_part_body(rows, own_text, chips, *refs):
    sharp, shift = refs[0][0:1, 0:1], refs[0][1:2, 0:1]
    text, speeches, outs = refs[1][...], refs[2:4], refs[4:]
    groups = lax.axis_size("group")
    members = lax.axis_size("member")
    group = lax.axis_index("group")
    member = lax.axis_index("member")
    total = None
    for speech in speeches:
        table = speech[chips * rows :, :].astype(jnp.float32)
        for first in range(0, chips * rows, CHUNK):
            chunk = speech[first : min(first + CHUNK, chips * rows), :]
            marks = marks_of(table, first // CHUNK, chunk.shape[0])
            iota = lax.broadcasted_iota(jnp.int32, (own_text, chunk.shape[0]), 0)
            ids = [((group ^ k) * members + member) * own_text + iota for k in range(groups)]
            match = jnp.concatenate(ids, axis=0).astype(jnp.float32) == marks
            coef = coefficients(dot_rows(text, chunk), match, sharp, shift)
            part = jnp.dot(coef, chunk, preferred_element_type=jnp.float32)
            total = part if total is None else total + part
    row, at = 0, 0
    for out in outs:
        out[...] = total[row : row + out.shape[0], at : at + out.shape[1]]
        at += out.shape[1]
        if at == total.shape[1]:
            row, at = row + out.shape[0], 0


def speech_part_body(rows, own_text, has_start, chips, masks, outputs, *refs):
    sharp, shift, speech = refs[0][0:1, 0:1], refs[0][1:2, 0:1], refs[1]
    total = refs[2][...] if has_start else None
    texts, outs = list(refs[3 if has_start else 2 : -outputs]), refs[-outputs:]
    groups = lax.axis_size("group")
    members = lax.axis_size("member")
    group = lax.axis_index("group")
    member = lax.axis_index("member")
    table = speech[chips * rows :, :].astype(jnp.float32)
    marks = jnp.broadcast_to(marks_of(table, 0, rows), (rows, rows)).T[:, 0:1]
    block = speech[0:rows, :]
    column = groups * own_text
    lane = lax.broadcasted_iota(jnp.int32, (1, column), 1)
    base = (group ^ (lane // own_text)) * members * own_text + lane % own_text
    for mask in masks:
        pieces = [texts.pop(0)[...]]
        while sum(v.shape[0] for v in pieces) < column:
            pieces.append(texts.pop(0)[...])
        text = jnp.concatenate(pieces, axis=0)
        ids = (base + (member ^ (2 * mask)) * own_text).astype(jnp.float32)
        coef = coefficients(dot_rows(block, text), marks == ids, sharp, shift)
        part = jnp.dot(coef, text, preferred_element_type=jnp.float32)
        total = part if total is None else total + part
    for k, out in enumerate(outs):
        out[...] = total[k * out.shape[0] : (k + 1) * out.shape[0], :]


def add_sides_body(*refs):
    out = refs[-1]
    sides = [ref for ref in refs[:-1] if ref.shape != out.shape]
    whole = [ref for ref in refs[:-1] if ref.shape == out.shape]
    at = 0
    for ref in sides:
        columns = slice(at, at + ref.shape[1])
        total = ref[...]
        for other in whole:
            total = total + other[:, columns]
        out[:, columns] = total
        at += ref.shape[1]


def sum_body(*refs):
    total = refs[0][...]
    for ref in refs[1:-1]:
        total = total + ref[...]
    refs[-1][...] = total


def project(values, back):
    floats = values.astype(jnp.float32)
    along = jnp.sum(floats * back, axis=-1, keepdims=True)
    square = jnp.sum(floats * floats, axis=-1, keepdims=True) + 1e-06
    return (back - floats * (along / square)) * (1.0 / jnp.sqrt(square))


def finish_body(pieces, audio, home, *refs):
    backs, (sentence, text_back) = refs[:pieces], refs[pieces : pieces + 2]
    speech_grad, text_grad, speech_held, text_held, done = refs[pieces + 2 :]
    text_held[...] = project(sentence[...], text_back[...])
    copies = [pltpu.make_async_copy(text_held, text_grad, done.at[0])]
    copies[0].start()
    for i, back in enumerate(backs):
        size = back.shape[0]
        some = slice(i * size, (i + 1) * size)
        speech_held[some, :] = project(audio[some, :], home[some, :] + back[...])
        copy = pltpu.make_async_copy(
            speech_held.at[some, :], speech_grad.at[some, :], done.at[i + 1]
        )
        copy.start()
        copies.append(copy)
    for copy in copies:
        copy.wait()


def shards(audio_vectors, sentence_vectors, matching_indices, sharpness_array, offset_term):
    members = lax.axis_size("member")
    groups = lax.axis_size("group")
    chips = members // 2
    rows, width = audio_vectors.shape
    own_text = sentence_vectors.shape[0]
    label = matching_indices.reshape(1, rows)
    scalars = jnp.concatenate(
        [jnp.broadcast_to(v[:, None], (1, 128)) for v in (sharpness_array, offset_term)], axis=0
    )

    def bf16(*shape):
        return jax.ShapeDtypeStruct(shape, jnp.bfloat16)

    def f32(*shape):
        return jax.ShapeDtypeStruct(shape, jnp.float32)

    arguments = [audio_vectors, sentence_vectors, label]
    speech_own, text_own, audio, sentence = pl.pallas_call(
        prepare_body,
        out_shape=[
            bf16(rows + MARK_ROWS, width),
            bf16(own_text, width),
            bf16(rows, width),
            bf16(own_text, width),
        ],
        in_specs=[pl.BlockSpec(memory_space=pltpu.HBM)] * 3,
        out_specs=[pl.BlockSpec(memory_space=pltpu.VMEM)] * 4,
        scratch_shapes=[pltpu.VMEM((1, rows), jnp.int32), pltpu.SemaphoreType.DMA((3,))],
        compiler_params=pltpu.CompilerParams(vmem_limit_bytes=8 << 20),
        name="unit_rows",
    )(*[pltpu.with_memory_space_constraint(v, pltpu.HBM) for v in arguments])

    def passed_on(block):
        return call(join_body, bf16(own_text, width), [block], (), 1 << 29, name="pass_on")

    text_blocks = [text_own] + [None] * (groups - 1)
    for k in [1 << i for i in reversed(range(groups.bit_length() - 1))]:
        for j in range(0, groups, 2 * k):
            came = exchanged(text_blocks[j], "group", k)
            text_blocks[j + k] = passed_on(came) if k > 1 else came
    square = chips == 4
    masks = [1, 2] if square else list(range(1, chips))

    def far_halves(near, middle, after=()):
        pairs = []
        for i, (source, k) in enumerate(zip(near[::-1], masks)):
            half = call(
                functools.partial(cut_body, i * middle), bf16(middle, width), [source], after, name="cut"
            )
            pairs.append((half, exchanged(half, "member", 2 * k)))
        return pairs

    speech_blocks = [exchanged(speech_own, "member", 2 * k) for k in reversed(range(1, chips))]
    column = groups * own_text
    text, speech = call(
        functools.partial(join_both_body, groups),
        [bf16(column, width), bf16(chips * rows + mark_rows_of(chips, rows), width)],
        [*text_blocks, speech_own, *speech_blocks],
        (scalars,),
        name="join_rows",
    )
    other = exchanged(speech, "member", 1)
    text_near = [exchanged(text, "member", 2 * k) for k in masks]

    temporary = 4 * column * (6 * CHUNK + 3 * width)

    sides = 2
    side = f32(own_text, width // sides)
    outs = [f32(own_text, width)] * (groups // 2) + [side] * (groups // 2 * sides)
    body = functools.partial(text_part_body, rows, own_text, chips)
    work = 8 * column * chips * rows * width
    operands = [scalars, text, speech, other]
    parts = list(call(body, outs, operands, (), work, temporary, "text_part"))
    far = [parts[groups // 2 + i * sides :][:sides] for i in range(groups // 2)]

    text_far = []
    bit = 1
    while bit < groups // 2:
        for k in reversed(range(bit, groups // 2, 2 * bit)):
            came = [exchanged(v, "group", bit) for v in far[k]]
            sums = []
            for mine, v in zip(far[k - bit], came):
                if sums and square and not text_far:
                    text_far = far_halves(text_near, column // 2, tuple(sums))
                    gate = tuple(half for half, _ in text_far)
                else:
                    gate = ()
                sums.append(call(sum_body, side, [mine, v], gate, name="sum_near"))
            far[k - bit] = sums
        bit *= 2
    if square:
        text_far = [came for _, came in text_far]
    from_far = [exchanged(v, "group", groups // 2) for v in far[0]]
    from_near = [exchanged(parts[k], "group", k) for k in range(1, groups // 2)]

    def speech_part(speech, start, columns, texts, after=(), pieces=1):
        body = functools.partial(
            speech_part_body, rows, own_text, bool(start), chips, columns, pieces
        )
        work = 40 * rows * column * len(columns) * width
        outs = [f32(rows // pieces, width)] * pieces
        operands = [scalars, speech, *start, *texts]
        return call(body, outs, operands, after, work, temporary, "speech_part")

    near = [[0, *masks], [text, *text_near], tuple(far[0])]
    if square:
        away = speech_part(other, [], *near)
        home = speech_part(speech, [], *near)
        away = speech_part(other, away, [3], text_far, pieces=2)
        home = speech_part(speech, home, [3], text_far)
    else:
        away = speech_part(other, [], *near, pieces=2)
        home = speech_part(speech, [], *near)
    back = [exchanged(piece, "member", 1) for piece in away]
    text_back = call(
        add_sides_body,
        f32(own_text, width),
        [*from_far, *from_near, parts[0]],
        tuple(home),
        EARLY,
        name="text_sum",
    )
    results = [f32(rows, width), f32(own_text, width)]
    speech_grad, text_grad = pl.pallas_call(
        functools.partial(finish_body, len(back)),
        out_shape=results,
        in_specs=[pl.BlockSpec(memory_space=pltpu.VMEM)] * (4 + len(back)),
        out_specs=[pl.BlockSpec(memory_space=pltpu.HBM)] * 2,
        scratch_shapes=[
            *[pltpu.VMEM(v.shape, v.dtype) for v in results],
            pltpu.SemaphoreType.DMA((1 + len(back),)),
        ],
        compiler_params=pltpu.CompilerParams(vmem_limit_bytes=8 << 20),
        name="finish",
    )(audio, *home, *back, sentence, text_back)
    return (speech_grad, text_grad)


def solution(mesh):
    in_specs = (
        P(("group", "member"), None),
        P(("group", "member"), None),
        P(("group", "member")),
        P(),
        P(),
    )
    out_specs = (P(("group", "member"), None), P(("group", "member"), None))
    return jax.shard_map(shards, mesh=mesh, in_specs=in_specs, out_specs=out_specs, check_vma=False)
```

```python
import functools
import jax
import jax.numpy as jnp
from jax import lax
from jax.experimental import pallas as pl
from jax.experimental.pallas import tpu as pltpu
from jax.sharding import PartitionSpec as P

MARK_ROWS = 8
TILE_ROWS = 16
RADIX = 256
CHUNK = 512
EARLY = 1 << 33


def exchanged(value, axis, mask):
    size = lax.axis_size(axis)
    return lax.ppermute(value, axis, [(i, i ^ mask) for i in range(size)])


def total_bytes(values):
    return sum(v.size * v.dtype.itemsize for v in jax.tree.leaves(values))


def call(body, out_shape, operands, after=(), flops=0, temporary=0, name="kernel"):
    specs = [pl.BlockSpec(memory_space=pltpu.VMEM) for _ in operands]
    specs += [pl.BlockSpec(memory_space=pl.ANY) for _ in after]
    used = len(operands)

    def whole(*refs):
        body(*refs[:used], *refs[used + len(after) :])

    moved = total_bytes(operands) + total_bytes(out_shape)
    return pl.pallas_call(
        whole,
        out_shape=out_shape,
        in_specs=specs,
        out_specs=jax.tree.map(lambda _: pl.BlockSpec(memory_space=pltpu.VMEM), out_shape),
        compiler_params=pltpu.CompilerParams(vmem_limit_bytes=(4 << 20) + 2 * moved + temporary),
        cost_estimate=pl.CostEstimate(flops=flops, bytes_accessed=moved, transcendentals=0),
        name=name,
    )(*operands, *after)


def direction(values):
    floats = values.astype(jnp.float32)
    norms = jnp.sqrt(jnp.sum(floats * floats, axis=-1, keepdims=True) + 1e-06)
    return floats / norms, norms


def prepare_body(*refs):
    sources, (speech, text) = refs[:3], refs[3:5]
    held, done = refs[5:8], refs[8]
    copies = [pltpu.make_async_copy(sources[i], held[i], done.at[i]) for i in range(3)]
    for copy in copies:
        copy.start()
    for copy in copies:
        copy.wait()
    audio, sentence, label = held
    rows = audio.shape[0]
    speech[0:rows, :] = direction(audio[...])[0].astype(jnp.bfloat16)
    text[...] = direction(sentence[...])[0].astype(jnp.bfloat16)
    number = label[...]
    digits = jnp.concatenate([number % RADIX, number // RADIX], axis=1).astype(jnp.float32)
    wide = jnp.concatenate(
        [digits, jnp.zeros((1, speech.shape[1] - 2 * rows), jnp.float32)], axis=1
    )
    speech[rows : rows + MARK_ROWS, :] = jnp.broadcast_to(
        wide, (MARK_ROWS, speech.shape[1])
    ).astype(jnp.bfloat16)


def join_body(*refs):
    out = refs[-1]
    at = 0
    for ref in refs[:-1]:
        out[at : at + ref.shape[0], :] = ref[...]
        at += ref.shape[0]


def digits_of(rows, block):
    digits = block[rows : rows + MARK_ROWS, 0 : 2 * rows].astype(jnp.float32)
    return digits[0:1, 0:rows], digits[0:1, rows : 2 * rows]


def mark_rows_of(chips, rows):
    chunks = -(-chips // (CHUNK // rows))
    return -(-2 * chunks // TILE_ROWS) * TILE_ROWS


def join_both_body(count, *refs):
    text, speech = refs[-2:]
    join_body(*refs[:count], text)
    blocks = refs[count:-2]
    rows = blocks[0].shape[0] - MARK_ROWS
    width = speech.shape[1]
    for k, ref in enumerate(blocks):
        speech[k * rows : (k + 1) * rows, :] = ref[0:rows, :]
    per = CHUNK // rows
    height = mark_rows_of(len(blocks), rows)
    place = lax.broadcasted_iota(jnp.int32, (height, width), 0)
    table = jnp.zeros((height, width), jnp.float32)
    for chunk in range(0, len(blocks), per):
        both = [digits_of(rows, ref) for ref in blocks[chunk : chunk + per]]
        for i in range(2):
            parts = [digits[i] for digits in both]
            rest = width - rows * len(parts)
            line = jnp.concatenate([*parts, jnp.zeros((1, rest), jnp.float32)], axis=1)
            table = jnp.where(place == 2 * (chunk // per) + i, line, table)
    speech[len(blocks) * rows :, :] = table.astype(jnp.bfloat16)


def cut_body(first, source, out):
    out[...] = source[first : first + out.shape[0], :]


def marks_of(table, chunk, count):
    digits = table[2 * chunk : 2 * chunk + 2, 0:count]
    return digits[0:1, :] + RADIX * digits[1:2, :]


def coefficients(dots, match, sharp, shift):
    logits = sharp * dots + shift
    probs = 1.0 / (1.0 + jnp.exp(-logits))
    return (sharp * (probs - jnp.where(match, 1.0, 0.0))).astype(jnp.bfloat16)


def dot_rows(left, right):
    return lax.dot_general(left, right, (((1,), (1,)), ((), ())), preferred_element_type=jnp.float32)


def text_part_body(rows, own_text, chips, *refs):
    sharp, shift = refs[0][0:1, 0:1], refs[0][1:2, 0:1]
    text, speeches, outs = refs[1][...], refs[2:4], refs[4:]
    groups = lax.axis_size("group")
    members = lax.axis_size("member")
    group = lax.axis_index("group")
    member = lax.axis_index("member")
    total = None
    for speech in speeches:
        table = speech[chips * rows :, :].astype(jnp.float32)
        for first in range(0, chips * rows, CHUNK):
            chunk = speech[first : min(first + CHUNK, chips * rows), :]
            marks = marks_of(table, first // CHUNK, chunk.shape[0])
            iota = lax.broadcasted_iota(jnp.int32, (own_text, chunk.shape[0]), 0)
            ids = [((group ^ k) * members + member) * own_text + iota for k in range(groups)]
            match = jnp.concatenate(ids, axis=0).astype(jnp.float32) == marks
            coef = coefficients(dot_rows(text, chunk), match, sharp, shift)
            part = jnp.dot(coef, chunk, preferred_element_type=jnp.float32)
            total = part if total is None else total + part
    row, at = 0, 0
    for out in outs:
        out[...] = total[row : row + out.shape[0], at : at + out.shape[1]]
        at += out.shape[1]
        if at == total.shape[1]:
            row, at = row + out.shape[0], 0


def speech_part_body(rows, own_text, has_start, chips, masks, outputs, *refs):
    sharp, shift, speech = refs[0][0:1, 0:1], refs[0][1:2, 0:1], refs[1]
    total = refs[2][...] if has_start else None
    texts, outs = list(refs[3 if has_start else 2 : -outputs]), refs[-outputs:]
    groups = lax.axis_size("group")
    members = lax.axis_size("member")
    group = lax.axis_index("group")
    member = lax.axis_index("member")
    table = speech[chips * rows :, :].astype(jnp.float32)
    marks = jnp.broadcast_to(marks_of(table, 0, rows), (rows, rows)).T[:, 0:1]
    block = speech[0:rows, :]
    column = groups * own_text
    lane = lax.broadcasted_iota(jnp.int32, (1, column), 1)
    base = (group ^ (lane // own_text)) * members * own_text + lane % own_text
    for mask in masks:
        pieces = [texts.pop(0)[...]]
        while sum(v.shape[0] for v in pieces) < column:
            pieces.append(texts.pop(0)[...])
        text = jnp.concatenate(pieces, axis=0)
        ids = (base + (member ^ (2 * mask)) * own_text).astype(jnp.float32)
        coef = coefficients(dot_rows(block, text), marks == ids, sharp, shift)
        part = jnp.dot(coef, text, preferred_element_type=jnp.float32)
        total = part if total is None else total + part
    for k, out in enumerate(outs):
        out[...] = total[k * out.shape[0] : (k + 1) * out.shape[0], :]


def add_sides_body(*refs):
    out = refs[-1]
    sides = [ref for ref in refs[:-1] if ref.shape != out.shape]
    whole = [ref for ref in refs[:-1] if ref.shape == out.shape]
    at = 0
    for ref in sides:
        columns = slice(at, at + ref.shape[1])
        total = ref[...]
        for other in whole:
            total = total + other[:, columns]
        out[:, columns] = total
        at += ref.shape[1]


def sum_body(*refs):
    total = refs[0][...]
    for ref in refs[1:-1]:
        total = total + ref[...]
    refs[-1][...] = total


def project(values, back):
    floats = values.astype(jnp.float32)
    along = jnp.sum(floats * back, axis=-1, keepdims=True)
    square = jnp.sum(floats * floats, axis=-1, keepdims=True) + 1e-06
    return (back - floats * (along / square)) * (1.0 / jnp.sqrt(square))


def finish_body(pieces, audio, home, *refs):
    backs, (sentence, text_back) = refs[:pieces], refs[pieces : pieces + 2]
    speech_grad, text_grad, speech_held, text_held, done = refs[pieces + 2 :]
    text_held[...] = project(sentence[...], text_back[...])
    copies = [pltpu.make_async_copy(text_held, text_grad, done.at[0])]
    copies[0].start()
    for i, back in enumerate(backs):
        size = back.shape[0]
        some = slice(i * size, (i + 1) * size)
        speech_held[some, :] = project(audio[some, :], home[some, :] + back[...])
        copy = pltpu.make_async_copy(
            speech_held.at[some, :], speech_grad.at[some, :], done.at[i + 1]
        )
        copy.start()
        copies.append(copy)
    for copy in copies:
        copy.wait()


def shards(audio_vectors, sentence_vectors, matching_indices, sharpness_array, offset_term):
    members = lax.axis_size("member")
    groups = lax.axis_size("group")
    chips = members // 2
    rows, width = audio_vectors.shape
    own_text = sentence_vectors.shape[0]
    label = matching_indices.reshape(1, rows)
    scalars = jnp.concatenate(
        [v[:, None] for v in (sharpness_array, offset_term)], axis=0
    )

    def bf16(*shape):
        return jax.ShapeDtypeStruct(shape, jnp.bfloat16)

    def f32(*shape):
        return jax.ShapeDtypeStruct(shape, jnp.float32)

    arguments = [audio_vectors, sentence_vectors, label]
    speech_own, text_own, audio, sentence = pl.pallas_call(
        prepare_body,
        out_shape=[
            bf16(rows + MARK_ROWS, width),
            bf16(own_text, width),
            bf16(rows, width),
            bf16(own_text, width),
        ],
        in_specs=[pl.BlockSpec(memory_space=pltpu.HBM)] * 3,
        out_specs=[pl.BlockSpec(memory_space=pltpu.VMEM)] * 4,
        scratch_shapes=[pltpu.VMEM((1, rows), jnp.int32), pltpu.SemaphoreType.DMA((3,))],
        compiler_params=pltpu.CompilerParams(vmem_limit_bytes=8 << 20),
        name="unit_rows",
    )(*[pltpu.with_memory_space_constraint(v, pltpu.HBM) for v in arguments])

    def passed_on(block):
        return call(join_body, bf16(own_text, width), [block], (), 1 << 29, name="pass_on")

    text_blocks = [text_own] + [None] * (groups - 1)
    for k in [1 << i for i in reversed(range(groups.bit_length() - 1))]:
        for j in range(0, groups, 2 * k):
            came = exchanged(text_blocks[j], "group", k)
            text_blocks[j + k] = passed_on(came) if k > 1 else came
    square = chips == 4
    masks = [1, 2] if square else list(range(1, chips))

    def far_halves(near, middle, after=()):
        pairs = []
        for i, (source, k) in enumerate(zip(near[::-1], masks)):
            half = call(
                functools.partial(cut_body, i * middle), bf16(middle, width), [source], after, name="cut"
            )
            pairs.append((half, exchanged(half, "member", 2 * k)))
        return pairs

    speech_blocks = [exchanged(speech_own, "member", 2 * k) for k in reversed(range(1, chips))]
    column = groups * own_text
    text, speech = call(
        functools.partial(join_both_body, groups),
        [bf16(column, width), bf16(chips * rows + mark_rows_of(chips, rows), width)],
        [*text_blocks, speech_own, *speech_blocks],
        (scalars,),
        name="join_rows",
    )
    other = exchanged(speech, "member", 1)
    text_near = [exchanged(text, "member", 2 * k) for k in masks]

    temporary = 4 * column * (6 * CHUNK + 3 * width)

    sides = 2
    side = f32(own_text, width // sides)
    outs = [f32(own_text, width)] * (groups // 2) + [side] * (groups // 2 * sides)
    body = functools.partial(text_part_body, rows, own_text, chips)
    work = 8 * column * chips * rows * width
    operands = [scalars, text, speech, other]
    parts = list(call(body, outs, operands, (), work, temporary, "text_part"))
    far = [parts[groups // 2 + i * sides :][:sides] for i in range(groups // 2)]

    text_far = []
    bit = 1
    while bit < groups // 2:
        for k in reversed(range(bit, groups // 2, 2 * bit)):
            came = [exchanged(v, "group", bit) for v in far[k]]
            sums = []
            for mine, v in zip(far[k - bit], came):
                if sums and square and not text_far:
                    text_far = far_halves(text_near, column // 2, tuple(sums))
                    gate = tuple(half for half, _ in text_far)
                else:
                    gate = ()
                sums.append(call(sum_body, side, [mine, v], gate, name="sum_near"))
            far[k - bit] = sums
        bit *= 2
    if square:
        text_far = [came for _, came in text_far]
    from_far = [exchanged(v, "group", groups // 2) for v in far[0]]
    from_near = [exchanged(parts[k], "group", k) for k in range(1, groups // 2)]

    def speech_part(speech, start, columns, texts, after=(), pieces=1):
        body = functools.partial(
            speech_part_body, rows, own_text, bool(start), chips, columns, pieces
        )
        work = 40 * rows * column * len(columns) * width
        outs = [f32(rows // pieces, width)] * pieces
        operands = [scalars, speech, *start, *texts]
        return call(body, outs, operands, after, work, temporary, "speech_part")

    near = [[0, *masks], [text, *text_near], tuple(far[0])]
    if square:
        away = speech_part(other, [], *near)
        home = speech_part(speech, [], *near)
        away = speech_part(other, away, [3], text_far, pieces=2)
        home = speech_part(speech, home, [3], text_far)
    else:
        away = speech_part(other, [], *near, pieces=2)
        home = speech_part(speech, [], *near)
    back = [exchanged(piece, "member", 1) for piece in away]
    text_back = call(
        add_sides_body,
        f32(own_text, width),
        [*from_far, *from_near, parts[0]],
        tuple(home),
        EARLY,
        name="text_sum",
    )
    results = [f32(rows, width), f32(own_text, width)]
    speech_grad, text_grad = pl.pallas_call(
        functools.partial(finish_body, len(back)),
        out_shape=results,
        in_specs=[pl.BlockSpec(memory_space=pltpu.VMEM)] * (4 + len(back)),
        out_specs=[pl.BlockSpec(memory_space=pltpu.HBM)] * 2,
        scratch_shapes=[
            *[pltpu.VMEM(v.shape, v.dtype) for v in results],
            pltpu.SemaphoreType.DMA((1 + len(back),)),
        ],
        compiler_params=pltpu.CompilerParams(vmem_limit_bytes=8 << 20),
        name="finish",
    )(audio, *home, *back, sentence, text_back)
    return (speech_grad, text_grad)


def solution(mesh):
    in_specs = (
        P(("group", "member"), None),
        P(("group", "member"), None),
        P(("group", "member")),
        P(),
        P(),
    )
    out_specs = (P(("group", "member"), None), P(("group", "member"), None))
    return jax.shard_map(shards, mesh=mesh, in_specs=in_specs, out_specs=out_specs, check_vma=False)
```

```python
import functools
import jax
import jax.numpy as jnp
from jax import lax
from jax.experimental import pallas as pl
from jax.experimental.pallas import tpu as pltpu
from jax.sharding import PartitionSpec as P

MARK_ROWS = 8
TILE_ROWS = 16
RADIX = 256
CHUNK = 512
EARLY = 1 << 33


def exchanged(value, axis, mask):
    size = lax.axis_size(axis)
    return lax.ppermute(value, axis, [(i, i ^ mask) for i in range(size)])


def total_bytes(values):
    return sum(v.size * v.dtype.itemsize for v in jax.tree.leaves(values))


def call(body, out_shape, operands, after=(), flops=0, temporary=0, name="kernel"):
    specs = [pl.BlockSpec(memory_space=pltpu.VMEM) for _ in operands]
    specs += [pl.BlockSpec(memory_space=pl.ANY) for _ in after]
    used = len(operands)

    def whole(*refs):
        body(*refs[:used], *refs[used + len(after) :])

    moved = total_bytes(operands) + total_bytes(out_shape)
    return pl.pallas_call(
        whole,
        out_shape=out_shape,
        in_specs=specs,
        out_specs=jax.tree.map(lambda _: pl.BlockSpec(memory_space=pltpu.VMEM), out_shape),
        compiler_params=pltpu.CompilerParams(vmem_limit_bytes=(4 << 20) + 2 * moved + temporary),
        cost_estimate=pl.CostEstimate(flops=flops, bytes_accessed=moved, transcendentals=0),
        name=name,
    )(*operands, *after)


def direction(values):
    floats = values.astype(jnp.float32)
    norms = jnp.sqrt(jnp.sum(floats * floats, axis=-1, keepdims=True) + 1e-06)
    return floats / norms, norms


def prepare_body(*refs):
    sources, (speech, text) = refs[:3], refs[3:5]
    held, done = refs[5:8], refs[8]
    copies = [pltpu.make_async_copy(sources[i], held[i], done.at[i]) for i in range(3)]
    for copy in copies:
        copy.start()
    for copy in copies:
        copy.wait()
    audio, sentence, label = held
    rows = audio.shape[0]
    speech[0:rows, :] = direction(audio[...])[0].astype(jnp.bfloat16)
    text[...] = direction(sentence[...])[0].astype(jnp.bfloat16)
    number = label[...]
    digits = jnp.concatenate([number % RADIX, number // RADIX], axis=1).astype(jnp.float32)
    wide = jnp.concatenate(
        [digits, jnp.zeros((1, speech.shape[1] - 2 * rows), jnp.float32)], axis=1
    )
    speech[rows : rows + MARK_ROWS, :] = jnp.broadcast_to(
        wide, (MARK_ROWS, speech.shape[1])
    ).astype(jnp.bfloat16)


def join_body(*refs):
    out = refs[-1]
    at = 0
    for ref in refs[:-1]:
        out[at : at + ref.shape[0], :] = ref[...]
        at += ref.shape[0]


def digits_of(rows, block):
    digits = block[rows : rows + MARK_ROWS, 0 : 2 * rows].astype(jnp.float32)
    return digits[0:1, 0:rows], digits[0:1, rows : 2 * rows]


def mark_rows_of(chips, rows):
    chunks = -(-chips // (CHUNK // rows))
    return -(-2 * chunks // TILE_ROWS) * TILE_ROWS


def join_both_body(count, *refs):
    text, speech = refs[-2:]
    join_body(*refs[:count], text)
    blocks = refs[count:-2]
    rows = blocks[0].shape[0] - MARK_ROWS
    width = speech.shape[1]
    for k, ref in enumerate(blocks):
        speech[k * rows : (k + 1) * rows, :] = ref[0:rows, :]
    per = CHUNK // rows
    height = mark_rows_of(len(blocks), rows)
    place = lax.broadcasted_iota(jnp.int32, (height, width), 0)
    table = jnp.zeros((height, width), jnp.float32)
    for chunk in range(0, len(blocks), per):
        both = [digits_of(rows, ref) for ref in blocks[chunk : chunk + per]]
        for i in range(2):
            parts = [digits[i] for digits in both]
            rest = width - rows * len(parts)
            line = jnp.concatenate([*parts, jnp.zeros((1, rest), jnp.float32)], axis=1)
            table = jnp.where(place == 2 * (chunk // per) + i, line, table)
    speech[len(blocks) * rows :, :] = table.astype(jnp.bfloat16)


def cut_body(first, source, out):
    out[...] = source[first : first + out.shape[0], :]


def marks_of(table, chunk, count):
    digits = table[2 * chunk : 2 * chunk + 2, 0:count]
    return digits[0:1, :] + RADIX * digits[1:2, :]


def coefficients(dots, match, sharp, shift):
    logits = sharp * dots + shift
    probs = 1.0 / (1.0 + jnp.exp(-logits))
    return (sharp * (probs - jnp.where(match, 1.0, 0.0))).astype(jnp.bfloat16)


def dot_rows(left, right):
    return lax.dot_general(left, right, (((1,), (1,)), ((), ())), preferred_element_type=jnp.float32)


def text_part_body(rows, own_text, chips, *refs):
    sharp, shift = refs[0][0:1, 0:1], refs[0][1:2, 0:1]
    text, speeches, outs = refs[1][...], refs[2:4], refs[4:]
    groups = lax.axis_size("group")
    members = lax.axis_size("member")
    group = lax.axis_index("group")
    member = lax.axis_index("member")
    total = None
    for speech in speeches:
        table = speech[chips * rows :, :].astype(jnp.float32)
        for first in range(0, chips * rows, CHUNK):
            chunk = speech[first : min(first + CHUNK, chips * rows), :]
            marks = marks_of(table, first // CHUNK, chunk.shape[0])
            iota = lax.broadcasted_iota(jnp.int32, (own_text, chunk.shape[0]), 0)
            ids = [((group ^ k) * members + member) * own_text + iota for k in range(groups)]
            match = jnp.concatenate(ids, axis=0).astype(jnp.float32) == marks
            coef = coefficients(dot_rows(text, chunk), match, sharp, shift)
            part = jnp.dot(coef, chunk, preferred_element_type=jnp.float32)
            total = part if total is None else total + part
    row, at = 0, 0
    for out in outs:
        out[...] = total[row : row + out.shape[0], at : at + out.shape[1]]
        at += out.shape[1]
        if at == total.shape[1]:
            row, at = row + out.shape[0], 0


def speech_part_body(rows, own_text, has_start, chips, places, outputs, *refs):
    sharp, shift, speech = refs[0][0:1, 0:1], refs[0][1:2, 0:1], refs[1]
    total = refs[2][...] if has_start else None
    texts, outs = refs[3 if has_start else 2 : -outputs], refs[-outputs:]
    members = lax.axis_size("member")
    group = lax.axis_index("group")
    member = lax.axis_index("member")
    table = speech[chips * rows :, :].astype(jnp.float32)
    marks = jnp.broadcast_to(marks_of(table, 0, rows), (rows, rows)).T[:, 0:1]
    block = speech[0:rows, :]
    for (mask, first), ref in zip(places, texts):
        text = ref[...]
        lane = lax.broadcasted_iota(jnp.int32, (1, text.shape[0]), 1)
        owner = (group ^ (first + lane // own_text)) * members + (member ^ (2 * mask))
        ids = (owner * own_text + lane % own_text).astype(jnp.float32)
        coef = coefficients(dot_rows(block, text), marks == ids, sharp, shift)
        part = jnp.dot(coef, text, preferred_element_type=jnp.float32)
        total = part if total is None else total + part
    for k, out in enumerate(outs):
        out[...] = total[k * out.shape[0] : (k + 1) * out.shape[0], :]


def add_sides_body(*refs):
    out = refs[-1]
    sides = [ref for ref in refs[:-1] if ref.shape != out.shape]
    whole = [ref for ref in refs[:-1] if ref.shape == out.shape]
    at = 0
    for ref in sides:
        columns = slice(at, at + ref.shape[1])
        total = ref[...]
        for other in whole:
            total = total + other[:, columns]
        out[:, columns] = total
        at += ref.shape[1]


def sum_body(*refs):
    total = refs[0][...]
    for ref in refs[1:-1]:
        total = total + ref[...]
    refs[-1][...] = total


def project(values, back):
    floats = values.astype(jnp.float32)
    along = jnp.sum(floats * back, axis=-1, keepdims=True)
    square = jnp.sum(floats * floats, axis=-1, keepdims=True) + 1e-06
    return (back - floats * (along / square)) * (1.0 / jnp.sqrt(square))


def finish_body(pieces, audio, home, *refs):
    backs, (sentence, text_back) = refs[:pieces], refs[pieces : pieces + 2]
    speech_grad, text_grad, speech_held, text_held, done = refs[pieces + 2 :]
    text_held[...] = project(sentence[...], text_back[...])
    copies = [pltpu.make_async_copy(text_held, text_grad, done.at[0])]
    copies[0].start()
    for i, back in enumerate(backs):
        size = back.shape[0]
        some = slice(i * size, (i + 1) * size)
        speech_held[some, :] = project(audio[some, :], home[some, :] + back[...])
        copy = pltpu.make_async_copy(
            speech_held.at[some, :], speech_grad.at[some, :], done.at[i + 1]
        )
        copy.start()
        copies.append(copy)
    for copy in copies:
        copy.wait()


def shards(audio_vectors, sentence_vectors, matching_indices, sharpness_array, offset_term):
    members = lax.axis_size("member")
    groups = lax.axis_size("group")
    chips = members // 2
    rows, width = audio_vectors.shape
    own_text = sentence_vectors.shape[0]
    label = matching_indices.reshape(1, rows)
    scalars = jnp.concatenate(
        [v[:, None] for v in (sharpness_array, offset_term)], axis=0
    )

    def bf16(*shape):
        return jax.ShapeDtypeStruct(shape, jnp.bfloat16)

    def f32(*shape):
        return jax.ShapeDtypeStruct(shape, jnp.float32)

    arguments = [audio_vectors, sentence_vectors, label]
    speech_own, text_own, audio, sentence = pl.pallas_call(
        prepare_body,
        out_shape=[
            bf16(rows + MARK_ROWS, width),
            bf16(own_text, width),
            bf16(rows, width),
            bf16(own_text, width),
        ],
        in_specs=[pl.BlockSpec(memory_space=pltpu.HBM)] * 3,
        out_specs=[pl.BlockSpec(memory_space=pltpu.VMEM)] * 4,
        scratch_shapes=[pltpu.VMEM((1, rows), jnp.int32), pltpu.SemaphoreType.DMA((3,))],
        compiler_params=pltpu.CompilerParams(vmem_limit_bytes=8 << 20),
        name="unit_rows",
    )(*[pltpu.with_memory_space_constraint(v, pltpu.HBM) for v in arguments])

    def passed_on(block):
        return call(join_body, bf16(own_text, width), [block], (), 1 << 29, name="pass_on")

    text_blocks = [text_own] + [None] * (groups - 1)
    for k in [1 << i for i in reversed(range(groups.bit_length() - 1))]:
        for j in range(0, groups, 2 * k):
            came = exchanged(text_blocks[j], "group", k)
            text_blocks[j + k] = passed_on(came) if k > 1 else came
    square = chips == 4
    masks = [1, 2] if square else list(range(1, chips))

    def far_halves(near, middle, after=()):
        pairs = []
        for i, (source, k) in enumerate(zip(near[::-1], masks)):
            half = call(
                functools.partial(cut_body, i * middle), bf16(middle, width), [source], after, name="cut"
            )
            pairs.append((half, exchanged(half, "member", 2 * k)))
        return pairs

    speech_blocks = [exchanged(speech_own, "member", 2 * k) for k in reversed(range(1, chips))]
    column = groups * own_text
    text, speech = call(
        functools.partial(join_both_body, groups),
        [bf16(column, width), bf16(chips * rows + mark_rows_of(chips, rows), width)],
        [*text_blocks, speech_own, *speech_blocks],
        (scalars,),
        name="join_rows",
    )
    other = exchanged(speech, "member", 1)
    text_near = [exchanged(text, "member", 2 * k) for k in masks]

    temporary = 4 * column * (6 * CHUNK + 3 * width)

    sides = 2
    side = f32(own_text, width // sides)
    outs = [f32(own_text, width)] * (groups // 2) + [side] * (groups // 2 * sides)
    body = functools.partial(text_part_body, rows, own_text, chips)
    work = 8 * column * chips * rows * width
    operands = [scalars, text, speech, other]
    parts = list(call(body, outs, operands, (), work, temporary, "text_part"))
    far = [parts[groups // 2 + i * sides :][:sides] for i in range(groups // 2)]

    text_far = []
    bit = 1
    while bit < groups // 2:
        for k in reversed(range(bit, groups // 2, 2 * bit)):
            came = [exchanged(v, "group", bit) for v in far[k]]
            sums = []
            for mine, v in zip(far[k - bit], came):
                if sums and square and not text_far:
                    text_far = far_halves(text_near, column // 2, tuple(sums))
                    gate = tuple(half for half, _ in text_far)
                else:
                    gate = ()
                sums.append(call(sum_body, side, [mine, v], gate, name="sum_near"))
            far[k - bit] = sums
        bit *= 2
    if square:
        text_far = [came for _, came in text_far]
    from_far = [exchanged(v, "group", groups // 2) for v in far[0]]
    from_near = [exchanged(parts[k], "group", k) for k in range(1, groups // 2)]

    def speech_part(speech, start, places, texts, after=(), pieces=1):
        body = functools.partial(
            speech_part_body, rows, own_text, bool(start), chips, places, pieces
        )
        work = 40 * rows * sum(v.shape[0] for v in texts) * width
        outs = [f32(rows // pieces, width)] * pieces
        operands = [scalars, speech, *start, *texts]
        return call(body, outs, operands, after, work, temporary, "speech_part")

    near = [[(k, 0) for k in (0, *masks)], [text, *text_near], tuple(far[0])]
    if square:
        away = speech_part(other, [], *near)
        home = speech_part(speech, [], *near)
        far_places = [(3, 0), (3, groups // 2)]
        away = speech_part(other, away, far_places[1:], text_far[1:])
        away = speech_part(other, away, far_places[:1], text_far[:1], pieces=2)
        home = speech_part(speech, home, far_places, text_far)
    else:
        away = speech_part(other, [], *near, pieces=2)
        home = speech_part(speech, [], *near)
    back = [exchanged(piece, "member", 1) for piece in away]
    text_back = call(
        add_sides_body,
        f32(own_text, width),
        [*from_far, *from_near, parts[0]],
        tuple(home),
        EARLY,
        name="text_sum",
    )
    results = [f32(rows, width), f32(own_text, width)]
    speech_grad, text_grad = pl.pallas_call(
        functools.partial(finish_body, len(back)),
        out_shape=results,
        in_specs=[pl.BlockSpec(memory_space=pltpu.VMEM)] * (4 + len(back)),
        out_specs=[pl.BlockSpec(memory_space=pltpu.HBM)] * 2,
        scratch_shapes=[
            *[pltpu.VMEM(v.shape, v.dtype) for v in results],
            pltpu.SemaphoreType.DMA((1 + len(back),)),
        ],
        compiler_params=pltpu.CompilerParams(vmem_limit_bytes=8 << 20),
        name="finish",
    )(audio, *home, *back, sentence, text_back)
    return (speech_grad, text_grad)


def solution(mesh):
    in_specs = (
        P(("group", "member"), None),
        P(("group", "member"), None),
        P(("group", "member")),
        P(),
        P(),
    )
    out_specs = (P(("group", "member"), None), P(("group", "member"), None))
    return jax.shard_map(shards, mesh=mesh, in_specs=in_specs, out_specs=out_specs, check_vma=False)
```

```python
import functools
import jax
import jax.numpy as jnp
from jax import lax
from jax.experimental import pallas as pl
from jax.experimental.pallas import tpu as pltpu
from jax.sharding import PartitionSpec as P

MARK_ROWS = 8
TILE_ROWS = 16
RADIX = 256
CHUNK = 512
EARLY = 1 << 33


def exchanged(value, axis, mask):
    size = lax.axis_size(axis)
    return lax.ppermute(value, axis, [(i, i ^ mask) for i in range(size)])


def total_bytes(values):
    return sum(v.size * v.dtype.itemsize for v in jax.tree.leaves(values))


def call(body, out_shape, operands, after=(), flops=0, temporary=0, name="kernel"):
    specs = [pl.BlockSpec(memory_space=pltpu.VMEM) for _ in operands]
    specs += [pl.BlockSpec(memory_space=pl.ANY) for _ in after]
    used = len(operands)

    def whole(*refs):
        body(*refs[:used], *refs[used + len(after) :])

    moved = total_bytes(operands) + total_bytes(out_shape)
    return pl.pallas_call(
        whole,
        out_shape=out_shape,
        in_specs=specs,
        out_specs=jax.tree.map(lambda _: pl.BlockSpec(memory_space=pltpu.VMEM), out_shape),
        compiler_params=pltpu.CompilerParams(vmem_limit_bytes=(4 << 20) + 2 * moved + temporary),
        cost_estimate=pl.CostEstimate(flops=flops, bytes_accessed=moved, transcendentals=0),
        name=name,
    )(*operands, *after)


def direction(values):
    floats = values.astype(jnp.float32)
    norms = jnp.sqrt(jnp.sum(floats * floats, axis=-1, keepdims=True) + 1e-06)
    return floats / norms, norms


def prepare_body(*refs):
    sources, (speech, text) = refs[:3], refs[3:5]
    held, done = refs[5:8], refs[8]
    copies = [pltpu.make_async_copy(sources[i], held[i], done.at[i]) for i in range(3)]
    for copy in copies:
        copy.start()
    for copy in copies:
        copy.wait()
    audio, sentence, label = held
    rows = audio.shape[0]
    speech[0:rows, :] = direction(audio[...])[0].astype(jnp.bfloat16)
    text[...] = direction(sentence[...])[0].astype(jnp.bfloat16)
    number = label[...]
    digits = jnp.concatenate([number % RADIX, number // RADIX], axis=1).astype(jnp.float32)
    wide = jnp.concatenate(
        [digits, jnp.zeros((1, speech.shape[1] - 2 * rows), jnp.float32)], axis=1
    )
    speech[rows : rows + MARK_ROWS, :] = jnp.broadcast_to(
        wide, (MARK_ROWS, speech.shape[1])
    ).astype(jnp.bfloat16)


def join_body(*refs):
    out = refs[-1]
    at = 0
    for ref in refs[:-1]:
        out[at : at + ref.shape[0], :] = ref[...]
        at += ref.shape[0]


def digits_of(rows, block):
    digits = block[rows : rows + MARK_ROWS, 0 : 2 * rows].astype(jnp.float32)
    return digits[0:1, 0:rows], digits[0:1, rows : 2 * rows]


def mark_rows_of(chips, rows):
    chunks = -(-chips // (CHUNK // rows))
    return -(-2 * chunks // TILE_ROWS) * TILE_ROWS


def join_both_body(count, *refs):
    text, speech = refs[-2:]
    join_body(*refs[:count], text)
    blocks = refs[count:-2]
    rows = blocks[0].shape[0] - MARK_ROWS
    width = speech.shape[1]
    for k, ref in enumerate(blocks):
        speech[k * rows : (k + 1) * rows, :] = ref[0:rows, :]
    per = CHUNK // rows
    height = mark_rows_of(len(blocks), rows)
    place = lax.broadcasted_iota(jnp.int32, (height, width), 0)
    table = jnp.zeros((height, width), jnp.float32)
    for chunk in range(0, len(blocks), per):
        both = [digits_of(rows, ref) for ref in blocks[chunk : chunk + per]]
        for i in range(2):
            parts = [digits[i] for digits in both]
            rest = width - rows * len(parts)
            line = jnp.concatenate([*parts, jnp.zeros((1, rest), jnp.float32)], axis=1)
            table = jnp.where(place == 2 * (chunk // per) + i, line, table)
    speech[len(blocks) * rows :, :] = table.astype(jnp.bfloat16)


def cut_body(first, source, out):
    out[...] = source[first : first + out.shape[0], :]


def marks_of(table, chunk, count):
    digits = table[2 * chunk : 2 * chunk + 2, 0:count]
    return digits[0:1, :] + RADIX * digits[1:2, :]


def coefficients(dots, match, sharp, shift):
    logits = sharp * dots + shift
    probs = 1.0 / (1.0 + jnp.exp(-logits))
    return (sharp * (probs - jnp.where(match, 1.0, 0.0))).astype(jnp.bfloat16)


def dot_rows(left, right):
    return lax.dot_general(left, right, (((1,), (1,)), ((), ())), preferred_element_type=jnp.float32)


def text_part_body(rows, own_text, chips, *refs):
    sharp, shift = refs[0][0:1, 0:1], refs[0][1:2, 0:1]
    text, speeches, outs = refs[1][...], refs[2:4], refs[4:]
    groups = lax.axis_size("group")
    members = lax.axis_size("member")
    group = lax.axis_index("group")
    member = lax.axis_index("member")
    total = None
    for speech in speeches:
        table = speech[chips * rows :, :].astype(jnp.float32)
        for first in range(0, chips * rows, CHUNK):
            chunk = speech[first : min(first + CHUNK, chips * rows), :]
            marks = marks_of(table, first // CHUNK, chunk.shape[0])
            iota = lax.broadcasted_iota(jnp.int32, (own_text, chunk.shape[0]), 0)
            ids = [((group ^ k) * members + member) * own_text + iota for k in range(groups)]
            match = jnp.concatenate(ids, axis=0).astype(jnp.float32) == marks
            coef = coefficients(dot_rows(text, chunk), match, sharp, shift)
            part = jnp.dot(coef, chunk, preferred_element_type=jnp.float32)
            total = part if total is None else total + part
    row, at = 0, 0
    for out in outs:
        out[...] = total[row : row + out.shape[0], at : at + out.shape[1]]
        at += out.shape[1]
        if at == total.shape[1]:
            row, at = row + out.shape[0], 0


def speech_part_body(rows, own_text, has_start, chips, places, outputs, *refs):
    sharp, shift, speech = refs[0][0:1, 0:1], refs[0][1:2, 0:1], refs[1]
    texts, outs = list(refs[4 if has_start else 2 : -outputs]), refs[-outputs:]
    members = lax.axis_size("member")
    group = lax.axis_index("group")
    member = lax.axis_index("member")
    if has_start:
        total = refs[2][...]
        marks = refs[3][:, 0:1]
    else:
        total = None
        table = speech[chips * rows :, :].astype(jnp.float32)
        spread = jnp.broadcast_to(marks_of(table, 0, rows), (rows, rows)).T
        outs, kept = outs[:-1], outs[-1]
        kept[...] = spread
        marks = spread[:, 0:1]
    block = speech[0:rows, :]
    for mask, first, count in places:
        text = jnp.concatenate([texts.pop(0)[...] for _ in range(count)], axis=0)
        lane = lax.broadcasted_iota(jnp.int32, (1, text.shape[0]), 1)
        owner = (group ^ (first + lane // own_text)) * members + (member ^ (2 * mask))
        ids = (owner * own_text + lane % own_text).astype(jnp.float32)
        coef = coefficients(dot_rows(block, text), marks == ids, sharp, shift)
        part = jnp.dot(coef, text, preferred_element_type=jnp.float32)
        total = part if total is None else total + part
    for k, out in enumerate(outs):
        out[...] = total[k * out.shape[0] : (k + 1) * out.shape[0], :]


def add_sides_body(*refs):
    out = refs[-1]
    sides = [ref for ref in refs[:-1] if ref.shape != out.shape]
    whole = [ref for ref in refs[:-1] if ref.shape == out.shape]
    at = 0
    for ref in sides:
        columns = slice(at, at + ref.shape[1])
        total = ref[...]
        for other in whole:
            total = total + other[:, columns]
        out[:, columns] = total
        at += ref.shape[1]


def sum_body(*refs):
    total = refs[0][...]
    for ref in refs[1:-1]:
        total = total + ref[...]
    refs[-1][...] = total


def project(values, back):
    floats = values.astype(jnp.float32)
    along = jnp.sum(floats * back, axis=-1, keepdims=True)
    square = jnp.sum(floats * floats, axis=-1, keepdims=True) + 1e-06
    return (back - floats * (along / square)) * (1.0 / jnp.sqrt(square))


def finish_body(pieces, audio, home, *refs):
    backs, (sentence, text_back) = refs[:pieces], refs[pieces : pieces + 2]
    speech_grad, text_grad, speech_held, text_held, done = refs[pieces + 2 :]
    text_held[...] = project(sentence[...], text_back[...])
    copies = [pltpu.make_async_copy(text_held, text_grad, done.at[0])]
    copies[0].start()
    for i, back in enumerate(backs):
        size = back.shape[0]
        some = slice(i * size, (i + 1) * size)
        speech_held[some, :] = project(audio[some, :], home[some, :] + back[...])
        copy = pltpu.make_async_copy(
            speech_held.at[some, :], speech_grad.at[some, :], done.at[i + 1]
        )
        copy.start()
        copies.append(copy)
    for copy in copies:
        copy.wait()


def shards(audio_vectors, sentence_vectors, matching_indices, sharpness_array, offset_term):
    members = lax.axis_size("member")
    groups = lax.axis_size("group")
    chips = members // 2
    rows, width = audio_vectors.shape
    own_text = sentence_vectors.shape[0]
    label = matching_indices.reshape(1, rows)
    scalars = jnp.concatenate(
        [v[:, None] for v in (sharpness_array, offset_term)], axis=0
    )

    def bf16(*shape):
        return jax.ShapeDtypeStruct(shape, jnp.bfloat16)

    def f32(*shape):
        return jax.ShapeDtypeStruct(shape, jnp.float32)

    arguments = [audio_vectors, sentence_vectors, label]
    speech_own, text_own, audio, sentence = pl.pallas_call(
        prepare_body,
        out_shape=[
            bf16(rows + MARK_ROWS, width),
            bf16(own_text, width),
            bf16(rows, width),
            bf16(own_text, width),
        ],
        in_specs=[pl.BlockSpec(memory_space=pltpu.HBM)] * 3,
        out_specs=[pl.BlockSpec(memory_space=pltpu.VMEM)] * 4,
        scratch_shapes=[pltpu.VMEM((1, rows), jnp.int32), pltpu.SemaphoreType.DMA((3,))],
        compiler_params=pltpu.CompilerParams(vmem_limit_bytes=8 << 20),
        name="unit_rows",
    )(*[pltpu.with_memory_space_constraint(v, pltpu.HBM) for v in arguments])

    def passed_on(block):
        return call(join_body, bf16(own_text, width), [block], (), 1 << 29, name="pass_on")

    text_blocks = [text_own] + [None] * (groups - 1)
    for k in [1 << i for i in reversed(range(groups.bit_length() - 1))]:
        for j in range(0, groups, 2 * k):
            came = exchanged(text_blocks[j], "group", k)
            text_blocks[j + k] = passed_on(came) if k > 1 else came
    square = chips == 4
    masks = [1, 2] if square else list(range(1, chips))

    def far_halves(near, middle, after=()):
        pairs = []
        for i, (source, k) in enumerate(zip(near[::-1], masks)):
            half = call(
                functools.partial(cut_body, i * middle), bf16(middle, width), [source], after, name="cut"
            )
            pairs.append((half, exchanged(half, "member", 2 * k)))
        return pairs

    speech_blocks = [exchanged(speech_own, "member", 2 * k) for k in reversed(range(1, chips))]
    column = groups * own_text
    text, speech = call(
        functools.partial(join_both_body, groups),
        [bf16(column, width), bf16(chips * rows + mark_rows_of(chips, rows), width)],
        [*text_blocks, speech_own, *speech_blocks],
        (scalars,),
        name="join_rows",
    )
    other = exchanged(speech, "member", 1)
    text_near = [exchanged(text, "member", 2 * k) for k in masks]

    temporary = 4 * column * (6 * CHUNK + 3 * width)

    sides = 2
    side = f32(own_text, width // sides)
    outs = [f32(own_text, width)] * (groups // 2) + [side] * (groups // 2 * sides)
    body = functools.partial(text_part_body, rows, own_text, chips)
    work = 8 * column * chips * rows * width
    operands = [scalars, text, speech, other]
    parts = list(call(body, outs, operands, (), work, temporary, "text_part"))
    far = [parts[groups // 2 + i * sides :][:sides] for i in range(groups // 2)]

    text_far = []
    bit = 1
    while bit < groups // 2:
        for k in reversed(range(bit, groups // 2, 2 * bit)):
            came = [exchanged(v, "group", bit) for v in far[k]]
            sums = []
            for mine, v in zip(far[k - bit], came):
                if sums and square and not text_far:
                    text_far = far_halves(text_near, column // 2, tuple(sums))
                    gate = tuple(half for half, _ in text_far)
                else:
                    gate = ()
                sums.append(call(sum_body, side, [mine, v], gate, name="sum_near"))
            far[k - bit] = sums
        bit *= 2
    if square:
        text_far = [came for _, came in text_far]
    from_far = [exchanged(v, "group", groups // 2) for v in far[0]]
    from_near = [exchanged(parts[k], "group", k) for k in range(1, groups // 2)]

    def speech_part(speech, start, places, texts, after=(), pieces=1):
        outs = [f32(rows // pieces, width)] * pieces
        if not start:
            outs.append(f32(rows, rows))
        body = functools.partial(
            speech_part_body, rows, own_text, bool(start), chips, places, len(outs)
        )
        work = 40 * rows * sum(v.shape[0] for v in texts) * width
        operands = [scalars, speech, *start, *texts]
        return list(call(body, outs, operands, after, work, temporary, "speech_part"))

    near = [[(k, 0, 1) for k in (0, *masks)], [text, *text_near], tuple(far[0])]
    if square:
        away, away_marks = speech_part(other, [], *near)
        home, home_marks = speech_part(speech, [], *near)
        last = [(3, groups // 2, 1)]
        away = speech_part(other, [away, away_marks], last, text_far[1:])
        away = speech_part(other, [*away, away_marks], [(3, 0, 1)], text_far[:1], pieces=2)
        home = speech_part(speech, [home, home_marks], [(3, 0, 2)], text_far)
    else:
        away = speech_part(other, [], *near, pieces=2)[:-1]
        home = speech_part(speech, [], *near)[:-1]
    back = [exchanged(piece, "member", 1) for piece in away]
    text_back = call(
        add_sides_body,
        f32(own_text, width),
        [*from_far, *from_near, parts[0]],
        tuple(home),
        EARLY,
        name="text_sum",
    )
    results = [f32(rows, width), f32(own_text, width)]
    speech_grad, text_grad = pl.pallas_call(
        functools.partial(finish_body, len(back)),
        out_shape=results,
        in_specs=[pl.BlockSpec(memory_space=pltpu.VMEM)] * (4 + len(back)),
        out_specs=[pl.BlockSpec(memory_space=pltpu.HBM)] * 2,
        scratch_shapes=[
            *[pltpu.VMEM(v.shape, v.dtype) for v in results],
            pltpu.SemaphoreType.DMA((1 + len(back),)),
        ],
        compiler_params=pltpu.CompilerParams(vmem_limit_bytes=8 << 20),
        name="finish",
    )(audio, *home, *back, sentence, text_back)
    return (speech_grad, text_grad)


def solution(mesh):
    in_specs = (
        P(("group", "member"), None),
        P(("group", "member"), None),
        P(("group", "member")),
        P(),
        P(),
    )
    out_specs = (P(("group", "member"), None), P(("group", "member"), None))
    return jax.shard_map(shards, mesh=mesh, in_specs=in_specs, out_specs=out_specs, check_vma=False)
```

```python
import functools
import jax
import jax.numpy as jnp
from jax import lax
from jax.experimental import pallas as pl
from jax.experimental.pallas import tpu as pltpu
from jax.sharding import PartitionSpec as P

MARK_ROWS = 8
TILE_ROWS = 16
RADIX = 256
CHUNK = 512
EARLY = 1 << 33


def exchanged(value, axis, mask):
    size = lax.axis_size(axis)
    return lax.ppermute(value, axis, [(i, i ^ mask) for i in range(size)])


def total_bytes(values):
    return sum(v.size * v.dtype.itemsize for v in jax.tree.leaves(values))


def call(body, out_shape, operands, after=(), flops=0, temporary=0, name="kernel"):
    specs = [pl.BlockSpec(memory_space=pltpu.VMEM) for _ in operands]
    specs += [pl.BlockSpec(memory_space=pl.ANY) for _ in after]
    used = len(operands)

    def whole(*refs):
        body(*refs[:used], *refs[used + len(after) :])

    moved = total_bytes(operands) + total_bytes(out_shape)
    return pl.pallas_call(
        whole,
        out_shape=out_shape,
        in_specs=specs,
        out_specs=jax.tree.map(lambda _: pl.BlockSpec(memory_space=pltpu.VMEM), out_shape),
        compiler_params=pltpu.CompilerParams(vmem_limit_bytes=(4 << 20) + 2 * moved + temporary),
        cost_estimate=pl.CostEstimate(flops=flops, bytes_accessed=moved, transcendentals=0),
        name=name,
    )(*operands, *after)


def direction(values):
    floats = values.astype(jnp.float32)
    norms = jnp.sqrt(jnp.sum(floats * floats, axis=-1, keepdims=True) + 1e-06)
    return floats / norms, norms


def prepare_body(*refs):
    sources, (speech, text) = refs[:3], refs[3:5]
    held, done = refs[5:8], refs[8]
    copies = [pltpu.make_async_copy(sources[i], held[i], done.at[i]) for i in range(3)]
    for copy in copies:
        copy.start()
    for copy in copies:
        copy.wait()
    audio, sentence, label = held
    rows = audio.shape[0]
    speech[0:rows, :] = direction(audio[...])[0].astype(jnp.bfloat16)
    text[...] = direction(sentence[...])[0].astype(jnp.bfloat16)
    number = label[...]
    digits = jnp.concatenate([number % RADIX, number // RADIX], axis=1).astype(jnp.float32)
    wide = jnp.concatenate(
        [digits, jnp.zeros((1, speech.shape[1] - 2 * rows), jnp.float32)], axis=1
    )
    speech[rows : rows + MARK_ROWS, :] = jnp.broadcast_to(
        wide, (MARK_ROWS, speech.shape[1])
    ).astype(jnp.bfloat16)


def unit_body(values, out):
    out[...] = direction(values[...])[0].astype(jnp.bfloat16)


def join_body(*refs):
    out = refs[-1]
    at = 0
    for ref in refs[:-1]:
        out[at : at + ref.shape[0], :] = ref[...]
        at += ref.shape[0]


def digits_of(rows, block):
    digits = block[rows : rows + MARK_ROWS, 0 : 2 * rows].astype(jnp.float32)
    return digits[0:1, 0:rows], digits[0:1, rows : 2 * rows]


def mark_rows_of(chips, rows):
    chunks = -(-chips // (CHUNK // rows))
    return -(-2 * chunks // TILE_ROWS) * TILE_ROWS


def join_both_body(count, *refs):
    text, speech = refs[-2:]
    join_body(*refs[:count], text)
    blocks = refs[count:-2]
    rows = blocks[0].shape[0] - MARK_ROWS
    width = speech.shape[1]
    for k, ref in enumerate(blocks):
        speech[k * rows : (k + 1) * rows, :] = ref[0:rows, :]
    per = CHUNK // rows
    height = mark_rows_of(len(blocks), rows)
    place = lax.broadcasted_iota(jnp.int32, (height, width), 0)
    table = jnp.zeros((height, width), jnp.float32)
    for chunk in range(0, len(blocks), per):
        both = [digits_of(rows, ref) for ref in blocks[chunk : chunk + per]]
        for i in range(2):
            parts = [digits[i] for digits in both]
            rest = width - rows * len(parts)
            line = jnp.concatenate([*parts, jnp.zeros((1, rest), jnp.float32)], axis=1)
            table = jnp.where(place == 2 * (chunk // per) + i, line, table)
    speech[len(blocks) * rows :, :] = table.astype(jnp.bfloat16)


def cut_body(first, source, out):
    out[...] = source[first : first + out.shape[0], :]


def marks_of(table, chunk, count):
    digits = table[2 * chunk : 2 * chunk + 2, 0:count]
    return digits[0:1, :] + RADIX * digits[1:2, :]


def coefficients(dots, match, sharp, shift):
    logits = sharp * dots + shift
    probs = 1.0 / (1.0 + jnp.exp(-logits))
    return (sharp * (probs - jnp.where(match, 1.0, 0.0))).astype(jnp.bfloat16)


def dot_rows(left, right):
    return lax.dot_general(left, right, (((1,), (1,)), ((), ())), preferred_element_type=jnp.float32)


def text_part_body(rows, own_text, chips, *refs):
    sharp, shift = refs[0][0:1, 0:1], refs[0][1:2, 0:1]
    text, speeches, outs = refs[1][...], refs[2:4], refs[4:]
    groups = lax.axis_size("group")
    members = lax.axis_size("member")
    group = lax.axis_index("group")
    member = lax.axis_index("member")
    total = None
    for speech in speeches:
        table = speech[chips * rows :, :].astype(jnp.float32)
        for first in range(0, chips * rows, CHUNK):
            chunk = speech[first : min(first + CHUNK, chips * rows), :]
            marks = marks_of(table, first // CHUNK, chunk.shape[0])
            iota = lax.broadcasted_iota(jnp.int32, (own_text, chunk.shape[0]), 0)
            ids = [((group ^ k) * members + member) * own_text + iota for k in range(groups)]
            match = jnp.concatenate(ids, axis=0).astype(jnp.float32) == marks
            coef = coefficients(dot_rows(text, chunk), match, sharp, shift)
            part = jnp.dot(coef, chunk, preferred_element_type=jnp.float32)
            total = part if total is None else total + part
    row, at = 0, 0
    for out in outs:
        out[...] = total[row : row + out.shape[0], at : at + out.shape[1]]
        at += out.shape[1]
        if at == total.shape[1]:
            row, at = row + out.shape[0], 0


def speech_part_body(rows, own_text, has_start, chips, places, outputs, *refs):
    sharp, shift, speech = refs[0][0:1, 0:1], refs[0][1:2, 0:1], refs[1]
    total = refs[2][...] if has_start else None
    texts, outs = refs[3 if has_start else 2 : -outputs], refs[-outputs:]
    members = lax.axis_size("member")
    group = lax.axis_index("group")
    member = lax.axis_index("member")
    table = speech[chips * rows :, :].astype(jnp.float32)
    marks = jnp.broadcast_to(marks_of(table, 0, rows), (rows, rows)).T[:, 0:1]
    block = speech[0:rows, :]
    for (mask, first), ref in zip(places, texts):
        text = ref[...]
        lane = lax.broadcasted_iota(jnp.int32, (1, text.shape[0]), 1)
        owner = (group ^ (first + lane // own_text)) * members + (member ^ (2 * mask))
        ids = (owner * own_text + lane % own_text).astype(jnp.float32)
        coef = coefficients(dot_rows(block, text), marks == ids, sharp, shift)
        part = jnp.dot(coef, text, preferred_element_type=jnp.float32)
        total = part if total is None else total + part
    for k, out in enumerate(outs):
        out[...] = total[k * out.shape[0] : (k + 1) * out.shape[0], :]


def add_sides_body(*refs):
    out = refs[-1]
    sides = [ref for ref in refs[:-1] if ref.shape != out.shape]
    whole = [ref for ref in refs[:-1] if ref.shape == out.shape]
    at = 0
    for ref in sides:
        columns = slice(at, at + ref.shape[1])
        total = ref[...]
        for other in whole:
            total = total + other[:, columns]
        out[:, columns] = total
        at += ref.shape[1]


def sum_body(*refs):
    total = refs[0][...]
    for ref in refs[1:-1]:
        total = total + ref[...]
    refs[-1][...] = total


def project(values, back):
    floats = values.astype(jnp.float32)
    along = jnp.sum(floats * back, axis=-1, keepdims=True)
    square = jnp.sum(floats * floats, axis=-1, keepdims=True) + 1e-06
    return (back - floats * (along / square)) * (1.0 / jnp.sqrt(square))


def finish_body(pieces, audio, home, *refs):
    backs, (sentence, text_back) = refs[:pieces], refs[pieces : pieces + 2]
    speech_grad, text_grad, speech_held, text_held, done = refs[pieces + 2 :]
    text_held[...] = project(sentence[...], text_back[...])
    copies = [pltpu.make_async_copy(text_held, text_grad, done.at[0])]
    copies[0].start()
    for i, back in enumerate(backs):
        size = back.shape[0]
        some = slice(i * size, (i + 1) * size)
        speech_held[some, :] = project(audio[some, :], home[some, :] + back[...])
        copy = pltpu.make_async_copy(
            speech_held.at[some, :], speech_grad.at[some, :], done.at[i + 1]
        )
        copy.start()
        copies.append(copy)
    for copy in copies:
        copy.wait()


def shards(audio_vectors, sentence_vectors, matching_indices, sharpness_array, offset_term):
    members = lax.axis_size("member")
    groups = lax.axis_size("group")
    chips = members // 2
    rows, width = audio_vectors.shape
    own_text = sentence_vectors.shape[0]
    label = matching_indices.reshape(1, rows)
    scalars = jnp.concatenate(
        [v[:, None] for v in (sharpness_array, offset_term)], axis=0
    )

    def bf16(*shape):
        return jax.ShapeDtypeStruct(shape, jnp.bfloat16)

    def f32(*shape):
        return jax.ShapeDtypeStruct(shape, jnp.float32)

    arguments = [audio_vectors, sentence_vectors, label]
    speech_own, text_own, audio, sentence = pl.pallas_call(
        prepare_body,
        out_shape=[
            bf16(rows + MARK_ROWS, width),
            bf16(own_text, width),
            bf16(rows, width),
            bf16(own_text, width),
        ],
        in_specs=[pl.BlockSpec(memory_space=pltpu.HBM)] * 3,
        out_specs=[pl.BlockSpec(memory_space=pltpu.VMEM)] * 4,
        scratch_shapes=[pltpu.VMEM((1, rows), jnp.int32), pltpu.SemaphoreType.DMA((3,))],
        compiler_params=pltpu.CompilerParams(vmem_limit_bytes=8 << 20),
        name="unit_rows",
    )(*[pltpu.with_memory_space_constraint(v, pltpu.HBM) for v in arguments])

    def unit_far(block):
        return call(unit_body, bf16(own_text, width), [block], (), 1 << 29, name="unit_far")

    text_blocks = [text_own] + [None] * (groups - 1)
    for k in [1 << i for i in reversed(range(groups.bit_length() - 1))]:
        for j in range(0, groups, 2 * k):
            if k == groups // 2 and k > 1:
                text_blocks[k] = unit_far(exchanged(sentence_vectors, "group", k))
            else:
                text_blocks[j + k] = exchanged(text_blocks[j], "group", k)
    square = chips == 4
    masks = [1, 2] if square else list(range(1, chips))

    def far_halves(near, middle, after=()):
        pairs = []
        for i, (source, k) in enumerate(zip(near[::-1], masks)):
            half = call(
                functools.partial(cut_body, i * middle), bf16(middle, width), [source], after, name="cut"
            )
            pairs.append((half, exchanged(half, "member", 2 * k)))
        return pairs

    speech_blocks = [exchanged(speech_own, "member", 2 * k) for k in reversed(range(1, chips))]
    column = groups * own_text
    text, speech = call(
        functools.partial(join_both_body, groups),
        [bf16(column, width), bf16(chips * rows + mark_rows_of(chips, rows), width)],
        [*text_blocks, speech_own, *speech_blocks],
        (scalars,),
        name="join_rows",
    )
    other = exchanged(speech, "member", 1)
    text_near = [exchanged(text, "member", 2 * k) for k in masks]

    temporary = 4 * column * (6 * CHUNK + 3 * width)

    sides = 2
    side = f32(own_text, width // sides)
    outs = [f32(own_text, width)] * (groups // 2) + [side] * (groups // 2 * sides)
    body = functools.partial(text_part_body, rows, own_text, chips)
    work = 8 * column * chips * rows * width
    operands = [scalars, text, speech, other]
    parts = list(call(body, outs, operands, (), work, temporary, "text_part"))
    far = [parts[groups // 2 + i * sides :][:sides] for i in range(groups // 2)]

    text_far = []
    bit = 1
    while bit < groups // 2:
        for k in reversed(range(bit, groups // 2, 2 * bit)):
            came = [exchanged(v, "group", bit) for v in far[k]]
            sums = []
            for mine, v in zip(far[k - bit], came):
                if sums and square and not text_far:
                    text_far = far_halves(text_near, column // 2, tuple(sums))
                    gate = tuple(half for half, _ in text_far)
                else:
                    gate = ()
                sums.append(call(sum_body, side, [mine, v], gate, name="sum_near"))
            far[k - bit] = sums
        bit *= 2
    if square:
        text_far = [came for _, came in text_far]
    from_far = [exchanged(v, "group", groups // 2) for v in far[0]]
    from_near = [exchanged(parts[k], "group", k) for k in range(1, groups // 2)]

    def speech_part(speech, start, places, texts, after=(), pieces=1):
        body = functools.partial(
            speech_part_body, rows, own_text, bool(start), chips, places, pieces
        )
        work = 40 * rows * sum(v.shape[0] for v in texts) * width
        outs = [f32(rows // pieces, width)] * pieces
        operands = [scalars, speech, *start, *texts]
        return call(body, outs, operands, after, work, temporary, "speech_part")

    near = [[(k, 0) for k in (0, *masks)], [text, *text_near], tuple(far[0])]
    if square:
        away = speech_part(other, [], *near)
        home = speech_part(speech, [], *near)
        far_places = [(3, 0), (3, groups // 2)]
        away = speech_part(other, away, far_places[1:], text_far[1:])
        away = speech_part(other, away, far_places[:1], text_far[:1], pieces=2)
        home = speech_part(speech, home, far_places, text_far)
    else:
        away = speech_part(other, [], *near, pieces=2)
        home = speech_part(speech, [], *near)
    back = [exchanged(piece, "member", 1) for piece in away]
    text_back = call(
        add_sides_body,
        f32(own_text, width),
        [*from_far, *from_near, parts[0]],
        tuple(home),
        EARLY,
        name="text_sum",
    )
    results = [f32(rows, width), f32(own_text, width)]
    speech_grad, text_grad = pl.pallas_call(
        functools.partial(finish_body, len(back)),
        out_shape=results,
        in_specs=[pl.BlockSpec(memory_space=pltpu.VMEM)] * (4 + len(back)),
        out_specs=[pl.BlockSpec(memory_space=pltpu.HBM)] * 2,
        scratch_shapes=[
            *[pltpu.VMEM(v.shape, v.dtype) for v in results],
            pltpu.SemaphoreType.DMA((1 + len(back),)),
        ],
        compiler_params=pltpu.CompilerParams(vmem_limit_bytes=8 << 20),
        name="finish",
    )(audio, *home, *back, sentence, text_back)
    return (speech_grad, text_grad)


def solution(mesh):
    in_specs = (
        P(("group", "member"), None),
        P(("group", "member"), None),
        P(("group", "member")),
        P(),
        P(),
    )
    out_specs = (P(("group", "member"), None), P(("group", "member"), None))
    return jax.shard_map(shards, mesh=mesh, in_specs=in_specs, out_specs=out_specs, check_vma=False)
```

```python
import functools
import jax
import jax.numpy as jnp
from jax import lax
from jax.experimental import pallas as pl
from jax.experimental.pallas import tpu as pltpu
from jax.sharding import PartitionSpec as P

MARK_ROWS = 8
TILE_ROWS = 16
RADIX = 256
CHUNK = 512
EARLY = 1 << 33


def exchanged(value, axis, mask):
    size = lax.axis_size(axis)
    return lax.ppermute(value, axis, [(i, i ^ mask) for i in range(size)])


def total_bytes(values):
    return sum(v.size * v.dtype.itemsize for v in jax.tree.leaves(values))


def call(body, out_shape, operands, after=(), flops=0, temporary=0, name="kernel"):
    specs = [pl.BlockSpec(memory_space=pltpu.VMEM) for _ in operands]
    specs += [pl.BlockSpec(memory_space=pl.ANY) for _ in after]
    used = len(operands)

    def whole(*refs):
        body(*refs[:used], *refs[used + len(after) :])

    moved = total_bytes(operands) + total_bytes(out_shape)
    return pl.pallas_call(
        whole,
        out_shape=out_shape,
        in_specs=specs,
        out_specs=jax.tree.map(lambda _: pl.BlockSpec(memory_space=pltpu.VMEM), out_shape),
        compiler_params=pltpu.CompilerParams(vmem_limit_bytes=(4 << 20) + 2 * moved + temporary),
        cost_estimate=pl.CostEstimate(flops=flops, bytes_accessed=moved, transcendentals=0),
        name=name,
    )(*operands, *after)


def direction(values):
    floats = values.astype(jnp.float32)
    norms = jnp.sqrt(jnp.sum(floats * floats, axis=-1, keepdims=True) + 1e-06)
    return floats / norms, norms


def prepare_body(*refs):
    sources, (speech, text) = refs[:3], refs[3:5]
    held, done = refs[5:8], refs[8]
    copies = [pltpu.make_async_copy(sources[i], held[i], done.at[i]) for i in range(3)]
    for copy in copies:
        copy.start()
    for copy in copies:
        copy.wait()
    audio, sentence, label = held
    rows = audio.shape[0]
    speech[0:rows, :] = direction(audio[...])[0].astype(jnp.bfloat16)
    text[...] = direction(sentence[...])[0].astype(jnp.bfloat16)
    number = label[...]
    digits = jnp.concatenate([number % RADIX, number // RADIX], axis=1).astype(jnp.float32)
    wide = jnp.concatenate(
        [digits, jnp.zeros((1, speech.shape[1] - 2 * rows), jnp.float32)], axis=1
    )
    speech[rows : rows + MARK_ROWS, :] = jnp.broadcast_to(
        wide, (MARK_ROWS, speech.shape[1])
    ).astype(jnp.bfloat16)


def unit_body(values, out):
    out[...] = direction(values[...])[0].astype(jnp.bfloat16)


def join_body(*refs):
    out = refs[-1]
    at = 0
    for ref in refs[:-1]:
        out[at : at + ref.shape[0], :] = ref[...]
        at += ref.shape[0]


def digits_of(rows, block):
    digits = block[rows : rows + MARK_ROWS, 0 : 2 * rows].astype(jnp.float32)
    return digits[0:1, 0:rows], digits[0:1, rows : 2 * rows]


def mark_rows_of(chips, rows):
    chunks = -(-chips // (CHUNK // rows))
    return -(-2 * chunks // TILE_ROWS) * TILE_ROWS


def join_both_body(count, *refs):
    text, speech = refs[-2:]
    join_body(*refs[:count], text)
    blocks = refs[count:-2]
    rows = blocks[0].shape[0] - MARK_ROWS
    width = speech.shape[1]
    for k, ref in enumerate(blocks):
        speech[k * rows : (k + 1) * rows, :] = ref[0:rows, :]
    per = CHUNK // rows
    height = mark_rows_of(len(blocks), rows)
    place = lax.broadcasted_iota(jnp.int32, (height, width), 0)
    table = jnp.zeros((height, width), jnp.float32)
    for chunk in range(0, len(blocks), per):
        both = [digits_of(rows, ref) for ref in blocks[chunk : chunk + per]]
        for i in range(2):
            parts = [digits[i] for digits in both]
            rest = width - rows * len(parts)
            line = jnp.concatenate([*parts, jnp.zeros((1, rest), jnp.float32)], axis=1)
            table = jnp.where(place == 2 * (chunk // per) + i, line, table)
    speech[len(blocks) * rows :, :] = table.astype(jnp.bfloat16)


def cut_body(first, source, out):
    out[...] = source[first : first + out.shape[0], :]


def marks_of(table, chunk, count):
    digits = table[2 * chunk : 2 * chunk + 2, 0:count]
    return digits[0:1, :] + RADIX * digits[1:2, :]


def coefficients(dots, match, sharp, shift):
    logits = sharp * dots + shift
    probs = 1.0 / (1.0 + jnp.exp(-logits))
    return (sharp * (probs - jnp.where(match, 1.0, 0.0))).astype(jnp.bfloat16)


def dot_rows(left, right):
    return lax.dot_general(left, right, (((1,), (1,)), ((), ())), preferred_element_type=jnp.float32)


def text_part_body(rows, own_text, chips, *refs):
    sharp, shift = refs[0][0:1, 0:1], refs[0][1:2, 0:1]
    text, speeches, outs = refs[1][...], refs[2:4], refs[4:]
    groups = lax.axis_size("group")
    members = lax.axis_size("member")
    group = lax.axis_index("group")
    member = lax.axis_index("member")
    total = None
    for speech in speeches:
        table = speech[chips * rows :, :].astype(jnp.float32)
        for first in range(0, chips * rows, CHUNK):
            chunk = speech[first : min(first + CHUNK, chips * rows), :]
            marks = marks_of(table, first // CHUNK, chunk.shape[0])
            iota = lax.broadcasted_iota(jnp.int32, (own_text, chunk.shape[0]), 0)
            ids = [((group ^ k) * members + member) * own_text + iota for k in range(groups)]
            match = jnp.concatenate(ids, axis=0).astype(jnp.float32) == marks
            coef = coefficients(dot_rows(text, chunk), match, sharp, shift)
            part = jnp.dot(coef, chunk, preferred_element_type=jnp.float32)
            total = part if total is None else total + part
    row, at = 0, 0
    for out in outs:
        out[...] = total[row : row + out.shape[0], at : at + out.shape[1]]
        at += out.shape[1]
        if at == total.shape[1]:
            row, at = row + out.shape[0], 0


def speech_part_body(rows, own_text, has_start, chips, places, outputs, *refs):
    sharp, shift, speech = refs[0][0:1, 0:1], refs[0][1:2, 0:1], refs[1]
    total = refs[2][...] if has_start else None
    texts, outs = refs[3 if has_start else 2 : -outputs], refs[-outputs:]
    members = lax.axis_size("member")
    group = lax.axis_index("group")
    member = lax.axis_index("member")
    table = speech[chips * rows :, :].astype(jnp.float32)
    marks = jnp.broadcast_to(marks_of(table, 0, rows), (rows, rows)).T[:, 0:1]
    block = speech[0:rows, :]
    for (mask, first), ref in zip(places, texts):
        text = ref[...]
        lane = lax.broadcasted_iota(jnp.int32, (1, text.shape[0]), 1)
        owner = (group ^ (first + lane // own_text)) * members + (member ^ (2 * mask))
        ids = (owner * own_text + lane % own_text).astype(jnp.float32)
        coef = coefficients(dot_rows(block, text), marks == ids, sharp, shift)
        part = jnp.dot(coef, text, preferred_element_type=jnp.float32)
        total = part if total is None else total + part
    for k, out in enumerate(outs):
        out[...] = total[k * out.shape[0] : (k + 1) * out.shape[0], :]


def add_sides_body(*refs):
    out = refs[-1]
    sides = [ref for ref in refs[:-1] if ref.shape != out.shape]
    whole = [ref for ref in refs[:-1] if ref.shape == out.shape]
    at = 0
    for ref in sides:
        columns = slice(at, at + ref.shape[1])
        total = ref[...]
        for other in whole:
            total = total + other[:, columns]
        out[:, columns] = total
        at += ref.shape[1]


def sum_body(*refs):
    total = refs[0][...]
    for ref in refs[1:-1]:
        total = total + ref[...]
    refs[-1][...] = total


def project(values, back):
    floats = values.astype(jnp.float32)
    along = jnp.sum(floats * back, axis=-1, keepdims=True)
    square = jnp.sum(floats * floats, axis=-1, keepdims=True) + 1e-06
    return (back - floats * (along / square)) * (1.0 / jnp.sqrt(square))


def finish_body(pieces, audio, home, *refs):
    backs, (sentence, text_back) = refs[:pieces], refs[pieces : pieces + 2]
    speech_grad, text_grad, speech_held, text_held, done = refs[pieces + 2 :]
    text_held[...] = project(sentence[...], text_back[...])
    copies = [pltpu.make_async_copy(text_held, text_grad, done.at[0])]
    copies[0].start()
    for i, back in enumerate(backs):
        size = back.shape[0]
        some = slice(i * size, (i + 1) * size)
        speech_held[some, :] = project(audio[some, :], home[some, :] + back[...])
        copy = pltpu.make_async_copy(
            speech_held.at[some, :], speech_grad.at[some, :], done.at[i + 1]
        )
        copy.start()
        copies.append(copy)
    for copy in copies:
        copy.wait()


def shards(audio_vectors, sentence_vectors, matching_indices, sharpness_array, offset_term):
    members = lax.axis_size("member")
    groups = lax.axis_size("group")
    chips = members // 2
    rows, width = audio_vectors.shape
    own_text = sentence_vectors.shape[0]
    label = matching_indices.reshape(1, rows)
    scalars = jnp.concatenate(
        [v[:, None] for v in (sharpness_array, offset_term)], axis=0
    )

    def bf16(*shape):
        return jax.ShapeDtypeStruct(shape, jnp.bfloat16)

    def f32(*shape):
        return jax.ShapeDtypeStruct(shape, jnp.float32)

    arguments = [audio_vectors, sentence_vectors, label]
    speech_own, text_own, audio, sentence = pl.pallas_call(
        prepare_body,
        out_shape=[
            bf16(rows + MARK_ROWS, width),
            bf16(own_text, width),
            bf16(rows, width),
            bf16(own_text, width),
        ],
        in_specs=[pl.BlockSpec(memory_space=pltpu.HBM)] * 3,
        out_specs=[pl.BlockSpec(memory_space=pltpu.VMEM)] * 4,
        scratch_shapes=[pltpu.VMEM((1, rows), jnp.int32), pltpu.SemaphoreType.DMA((3,))],
        compiler_params=pltpu.CompilerParams(vmem_limit_bytes=8 << 20),
        name="unit_rows",
    )(*[pltpu.with_memory_space_constraint(v, pltpu.HBM) for v in arguments])

    def unit_far(block):
        return call(unit_body, bf16(own_text, width), [block], (), 1 << 29, name="unit_far")

    text_blocks = [text_own] + [None] * (groups - 1)
    for k in [1 << i for i in reversed(range(groups.bit_length() - 1))]:
        for j in range(0, groups, 2 * k):
            if k == groups // 2 and k > 1:
                text_blocks[k] = unit_far(exchanged(sentence_vectors, "group", k))
            else:
                text_blocks[j + k] = exchanged(text_blocks[j], "group", k)
    square = chips == 4
    masks = [1, 2] if square else list(range(1, chips))

    def far_halves(near, middle, after=()):
        pairs = []
        for i, (source, k) in enumerate(zip(near[::-1], masks)):
            half = call(
                functools.partial(cut_body, i * middle), bf16(middle, width), [source], after, name="cut"
            )
            pairs.append((half, exchanged(half, "member", 2 * k)))
        return pairs

    speech_blocks = [exchanged(speech_own, "member", 2 * k) for k in reversed(range(1, chips))]
    column = groups * own_text
    text, speech = call(
        functools.partial(join_both_body, groups),
        [bf16(column, width), bf16(chips * rows + mark_rows_of(chips, rows), width)],
        [*text_blocks, speech_own, *speech_blocks],
        (scalars,),
        name="join_rows",
    )
    other = exchanged(speech, "member", 1)
    text_near = [exchanged(text, "member", 2 * k) for k in masks]

    temporary = 4 * column * (6 * CHUNK + 3 * width)

    sides = 2
    side = f32(own_text, width // sides)
    outs = [f32(own_text, width)] * (groups // 2) + [side] * (groups // 2 * sides)
    body = functools.partial(text_part_body, rows, own_text, chips)
    work = 8 * column * chips * rows * width
    operands = [scalars, text, speech, other]
    parts = list(call(body, outs, operands, (), work, temporary, "text_part"))
    far = [parts[groups // 2 + i * sides :][:sides] for i in range(groups // 2)]

    text_far = []
    bit = 1
    while bit < groups // 2:
        for k in reversed(range(bit, groups // 2, 2 * bit)):
            came = [exchanged(v, "group", bit) for v in far[k]]
            sums = []
            for mine, v in zip(far[k - bit], came):
                if sums and square and not text_far:
                    text_far = far_halves(text_near, column // 2, tuple(sums))
                    gate = tuple(half for half, _ in text_far)
                else:
                    gate = ()
                sums.append(call(sum_body, side, [mine, v], gate, name="sum_near"))
            far[k - bit] = sums
        bit *= 2
    if square:
        text_far = [came for _, came in text_far]
    from_far = [exchanged(v, "group", groups // 2) for v in far[0]]
    from_near = [exchanged(parts[k], "group", k) for k in range(1, groups // 2)]

    def speech_part(speech, start, places, texts, after=(), pieces=1):
        body = functools.partial(
            speech_part_body, rows, own_text, bool(start), chips, places, pieces
        )
        work = 40 * rows * sum(v.shape[0] for v in texts) * width
        outs = [f32(rows // pieces, width)] * pieces
        operands = [scalars, speech, *start, *texts]
        return call(body, outs, operands, after, work, temporary, "speech_part")

    near = [[(k, 0) for k in (0, *masks)], [text, *text_near], tuple(far[0])]
    if square:
        away = speech_part(other, [], *near)
        home = speech_part(speech, [], *near)
        far_places = [(3, 0), (3, groups // 2)]
        away = speech_part(other, away, far_places[1:], text_far[1:])
        away = speech_part(other, away, far_places[:1], text_far[:1])
        home = speech_part(speech, home, far_places, text_far)
    else:
        away = speech_part(other, [], *near, pieces=2)
        home = speech_part(speech, [], *near)
    back = [exchanged(piece, "member", 1) for piece in away]
    text_back = call(
        add_sides_body,
        f32(own_text, width),
        [*from_far, *from_near, parts[0]],
        tuple(home),
        EARLY,
        name="text_sum",
    )
    results = [f32(rows, width), f32(own_text, width)]
    speech_grad, text_grad = pl.pallas_call(
        functools.partial(finish_body, len(back)),
        out_shape=results,
        in_specs=[pl.BlockSpec(memory_space=pltpu.VMEM)] * (4 + len(back)),
        out_specs=[pl.BlockSpec(memory_space=pltpu.HBM)] * 2,
        scratch_shapes=[
            *[pltpu.VMEM(v.shape, v.dtype) for v in results],
            pltpu.SemaphoreType.DMA((1 + len(back),)),
        ],
        compiler_params=pltpu.CompilerParams(vmem_limit_bytes=8 << 20),
        name="finish",
    )(audio, *home, *back, sentence, text_back)
    return (speech_grad, text_grad)


def solution(mesh):
    in_specs = (
        P(("group", "member"), None),
        P(("group", "member"), None),
        P(("group", "member")),
        P(),
        P(),
    )
    out_specs = (P(("group", "member"), None), P(("group", "member"), None))
    return jax.shard_map(shards, mesh=mesh, in_specs=in_specs, out_specs=out_specs, check_vma=False)
```
